1024 devices in a mesh: dp: 32 (over x, z_hi, core), pipe: 8 (over y), tensor: 4 (over z_lo).
Axes of the slice: x: 4, y: 8, z: 16 (z_hi: 4, z_lo: 4; z = z_hi * 4 + z_lo), core: 2. Of those that a mesh axis runs over, the one named last changes fastest.
Arguments:
- down_in: bfloat16 [64, 32, 2048], P('dp'), may hold values from -6 to 6
- up_in: bfloat16 [64, 32, 2048], P('dp'), may hold values from -6 to 6
- w_qkv: bfloat16 [8, 2048, 1536], P(None, 'dp', 'tensor'), may hold values from -0.125 to 0.125
- w_out: bfloat16 [8, 1024, 2048], P(None, 'tensor', 'dp'), may hold values from -0.1875 to 0.1875
- norm_gain: bfloat16 [8, 2048], P(None, 'dp'), may hold values from 0.099609375 to 1.8984375
- down_docs: int32 [64, 32], P('dp'), may hold values from 0 to 3, never falling along the last dimension, each value on 1 to 16 neighbouring positions
- up_docs: int32 [64, 32], P('dp'), may hold values from 0 to 3, never falling along the last dimension, each value on 1 to 16 neighbouring positions
Outputs:
- down_acts: bfloat16 [8, 64, 32, 2048], P('pipe', 'dp', 'tensor')
- up_acts: bfloat16 [8, 64, 32, 2048], P('pipe', 'dp', 'tensor')
The draws below stay inside these ranges and needn't reach their ends.
Inputs may be any that keep to these rules, and one draw needn't show every extreme that they name: `down_docs`: in every micro-batch the document numbers never fall along the positions, every one of the 4 numbers occurs, and no document is longer than 16 positions. `up_docs`: in every micro-batch the document numbers never fall along the positions, every one of the 4 numbers occurs, and no document is longer than 16 positions.
All inputs are finite; a program needn't handle non-finite values.
Results may differ from the reference program's by a relative error of at most 0.034.
Values may be sent and summed in bfloat16 or wider, within the bound.
No kernel may reach another device: no remote copies, remote signals or barrier semaphores. Data moves between devices by JAX's collectives and lax.ppermute only.
A program may use at most 32 MiB of HBM per device.

```python
import math
import jax
import jax.numpy as jnp
import numpy as np
from jax import lax

D = 2048
HEADS = 16
KV_HEADS = 4
HEAD_DIM = 64
SEQ = 32
SECTIONS = 8
BATCH = 64
N_TENSOR = 4


def block_levels(rng, dims, cuts, least, top_value):
    def one(position, blocks):
        heights = jax.random.uniform(jax.random.fold_in(jax.random.fold_in(rng, 6), position), (blocks,), jnp.float32, least / len(cuts), top_value / len(cuts))
        return jnp.repeat(jnp.exp(heights), dims[position] // blocks).reshape((-1,) + (1,) * (len(dims) - position - 1))

    factor_of = one(*cuts[0])
    for cut in cuts[1:]:
        factor_of = factor_of * one(*cut)
    return factor_of


def profile(number_of, total, bound, slope):
    weights = [(1 << 20) // math.isqrt(standing ** slope) + 1 for standing in range(2, number_of + 1)]
    spare, holding = total - bound - (number_of - 1), [1] * (number_of - 1)
    while spare > 0:
        free = [i for i in range(number_of - 1) if holding[i] < bound]
        whole, remaining = sum([weights[i] for i in free]), spare
        for i in free:
            more = min(bound - holding[i], max(1, remaining * weights[i] // whole), spare)
            holding[i] = holding[i] + more
            spare = spare - more
    return np.array([bound] + holding)


def uneven(own_key, number_of, total, bound, skew):
    if number_of == 2:
        one = jax.random.randint(own_key, (), max(1, total - bound), min(bound, total - 1) + 1)
        return jnp.stack([one, total - one])
    tallies = jnp.asarray(profile(number_of, total, bound, skew), jnp.int32)
    twos = (number_of - 1) // 2
    donor, taker = tallies[1:1 + 2 * twos:2], tallies[2:2 + 2 * twos:2]
    room = jnp.minimum(donor - 1, bound - taker)
    moved = jax.random.randint(jax.random.fold_in(own_key, 1), (twos,), 0, 1 << 20) % (room + 1)
    tallies = tallies.at[1:1 + 2 * twos:2].set(donor - moved).at[2:2 + 2 * twos:2].set(taker + moved)
    return tallies[jax.random.permutation(jax.random.fold_in(own_key, 2), number_of)]


def bell_draw(key, shape, spread, limit, pieces=(), kind=jnp.bfloat16):
    entries = jax.random.normal(key, shape, jnp.float32) * spread
    if len(pieces) > 0:
        entries = block_levels(key, shape, pieces, -0.22, 0.18) * entries
    return jnp.clip(entries, min=-limit, max=limit).astype(kind)


def setup_inputs(seed: int = 0) -> dict:
    arg_keys = jax.random.split(jax.random.key(seed), 8)
    down_in = bell_draw(arg_keys[0], (BATCH, SEQ, D), 1.0, 6.0, ((0, 32),))
    up_in = bell_draw(arg_keys[1], (BATCH, SEQ, D), 1.0, 6.0, ((0, 32),))
    w_qkv = bell_draw(arg_keys[2], (SECTIONS, D, (HEADS + 2 * KV_HEADS) * HEAD_DIM), D ** -0.5, 0.125, ((1, 32), (2, 4)))
    w_out = bell_draw(arg_keys[3], (SECTIONS, HEADS * HEAD_DIM, D), (HEADS * HEAD_DIM) ** -0.5, 0.1875, ((1, 4), (2, 32)))
    norm_gain = jnp.clip(1.0 + 0.18 * jax.random.normal(arg_keys[4], (SECTIONS, D), jnp.float32), 0.099609375, 1.8984375).astype(jnp.bfloat16)
    down_docs = jax.vmap(lambda own: jnp.searchsorted(jnp.cumsum(uneven(own, 4, SEQ, SEQ // 2, 2)), jnp.arange(SEQ), side="right"))(jax.random.split(arg_keys[5], BATCH)).reshape((BATCH, SEQ)).astype(jnp.int32)
    up_docs = jax.vmap(lambda own: jnp.searchsorted(jnp.cumsum(uneven(own, 4, SEQ, SEQ // 2, 2)), jnp.arange(SEQ), side="right"))(jax.random.split(arg_keys[6], BATCH)).reshape((BATCH, SEQ)).astype(jnp.int32)
    return dict(down_in=down_in, up_in=up_in, w_qkv=w_qkv, w_out=w_out, norm_gain=norm_gain, down_docs=down_docs, up_docs=up_docs)


EPSILON = 1e-05
THETA = 500000.0

def rotary_tables(length, width):
    half_width = width // 2
    frequency = THETA ** (-(jnp.arange(half_width, dtype=jnp.float32) * 2.0 / width))
    angles = jnp.arange(length, dtype=jnp.float32)[:, None] * frequency[None, :]
    return (jnp.cos(angles), jnp.sin(angles))

def rotate(values, cosine, sine):
    half_width = values.shape[-1] // 2
    first = values[..., :half_width]
    second = values[..., half_width:]
    cosine = cosine[:, None, :]
    sine = sine[:, None, :]
    return jnp.concatenate([first * cosine - second * sine, second * cosine + first * sine], axis=-1)

def normalize(inputs, gain):
    values = inputs.astype(jnp.float32)
    scale = lax.rsqrt(lax.optimization_barrier(jnp.mean(values * values, axis=-1, keepdims=True)) + EPSILON)
    return (values * scale * gain.astype(jnp.float32)).astype(jnp.bfloat16)

def attend(normed, qkv_cols, out_rows, docs, cosine, sine, heads_here, kv_here):
    length = normed.shape[0]
    query_width = heads_here * HEAD_DIM
    key_width = kv_here * HEAD_DIM
    projected = jnp.dot(normed, qkv_cols, preferred_element_type=jnp.float32)
    query = rotate(projected[:, :query_width].reshape(length, heads_here, HEAD_DIM), cosine, sine).astype(jnp.bfloat16)
    keys = rotate(projected[:, query_width:query_width + key_width].reshape(length, kv_here, HEAD_DIM), cosine, sine).astype(jnp.bfloat16)
    values = projected[:, query_width + key_width:].reshape(length, kv_here, HEAD_DIM).astype(jnp.bfloat16)
    query = query.reshape(length, kv_here, heads_here // kv_here, HEAD_DIM)
    scores = jnp.einsum('qgrd,kgd->grqk', query.astype(jnp.float32), keys.astype(jnp.float32)) * HEAD_DIM ** (-0.5)
    positions = jnp.arange(length)
    allowed = (positions[:, None] >= positions[None, :]) & (docs[:, None] == docs[None, :])
    scores = jnp.where(allowed, scores, -1e+30)
    weights = jax.nn.softmax(scores, axis=-1).astype(jnp.bfloat16)
    context = jnp.einsum('grqk,kgd->qgrd', weights.astype(jnp.float32), values.astype(jnp.float32))
    context = context.reshape(length, query_width).astype(jnp.bfloat16)
    return jnp.dot(context, out_rows, preferred_element_type=jnp.float32)

def section(inputs, qkv_weight, out_weight, gain, docs):
    cosine, sine = rotary_tables(SEQ, HEAD_DIM)
    normed = normalize(inputs, gain)
    heads_here = HEADS // N_TENSOR
    kv_here = KV_HEADS // N_TENSOR
    group = qkv_weight.shape[1] // N_TENSOR
    rows_here = heads_here * HEAD_DIM
    total = jnp.zeros(inputs.shape, jnp.float32)
    for member in range(N_TENSOR):
        qkv_cols = qkv_weight[:, member * group:(member + 1) * group]
        out_rows = out_weight[member * rows_here:(member + 1) * rows_here, :]
        partial_sum = attend(normed, qkv_cols, out_rows, docs, cosine, sine, heads_here, kv_here)
        total = total + partial_sum.astype(jnp.bfloat16).astype(jnp.float32)
    return (inputs.astype(jnp.float32) + total).astype(jnp.bfloat16)

def run_sections(inputs, docs, w_qkv, w_out, norm_gain):
    outputs = []
    current = inputs
    for index in range(SECTIONS):
        current = jax.vmap(section, in_axes=(0, None, None, None, 0))(current, w_qkv[index], w_out[index], norm_gain[index], docs)
        outputs.append(current)
    return jnp.stack(outputs)

def reference(down_in, up_in, w_qkv, w_out, norm_gain, down_docs, up_docs):
    down_acts = run_sections(down_in, down_docs, w_qkv, w_out, norm_gain)
    up_acts = run_sections(up_in, up_docs, w_qkv, w_out, norm_gain)[::-1]
    return (down_acts, up_acts)
```

```python
import functools

import jax
import jax.numpy as jnp
import numpy as np
from jax import lax
from jax.experimental import pallas as pl
from jax.experimental.pallas import tpu as pltpu
from jax.sharding import Mesh, PartitionSpec as P

HEADS = 16
KV_HEADS = 4
HEAD_DIM = 64
SEQ = 32
D = 2048
EPSILON = 1e-05
THETA = 500000.0

GROUPS = 4
GROUP_HEADS = 4
QKV = 384
CTX = 256
X = 4
ZH = 4
ZL = 4
Z = ZH * ZL
STEPS = Z // 2
BLOCK = 512


def rotary_tables():
    half = HEAD_DIM // 2
    frequency = THETA ** (-(jnp.arange(half, dtype=jnp.float32) * 2.0 / HEAD_DIM))
    angles = jnp.arange(SEQ, dtype=jnp.float32)[:, None] * frequency[None, :]
    return jnp.cos(angles), jnp.sin(angles)


def block_class(kind, k):
    return k % ZL if kind == "ring" else (-k) % ZL


BLOCKS = [("ring", k) for k in range(STEPS + 1)] + [("swap", k) for k in range(1, STEPS)]


def section_kernel(step, info, x_ref, allowed_ref, rope_ref, held_ref, *refs):
    blocks, (out_ref, xs, total) = refs[:Z], refs[Z:]

    @pl.when(info[0] != step)
    def _():
        out_ref[...] = held_ref[...]

    @pl.when(info[0] == step)
    def _():
        f32, bf16 = jnp.float32, jnp.bfloat16
        squares = jnp.zeros((SEQ, 1), f32)
        for zh in range(ZH):
            for x in range(X):
                part = x_ref[:, pl.ds(x * 512 + zh * 128, 128)]
                xs[zh, :, pl.ds(x * 128, 128)] = part
                wide = part.astype(f32)
                total[zh, :, pl.ds(x * 128, 128)] = wide
                squares = squares + jnp.sum(wide * wide, axis=-1, keepdims=True)
        scale = lax.rsqrt(squares * (1.0 / D) + EPSILON)

        cos, sin = rope_ref[0], rope_ref[1]
        kcos, ksin_a, ksin_b = rope_ref[2], rope_ref[3], rope_ref[4]
        allowed = allowed_ref[...] > 0.5
        lane = lax.broadcasted_iota(jnp.int32, (SEQ, 128), 1)
        lane2 = lax.broadcasted_iota(jnp.int32, (SEQ, 256), 1)
        head_of = (lane2 % 128) // 32

        contexts = []
        for c in range(GROUPS):
            projected = jnp.zeros((SEQ, QKV), f32)
            for i, (kind, k) in enumerate(BLOCKS):
                if block_class(kind, k) == c:
                    projected = projected + jnp.dot(
                        xs[info[1 + i]], blocks[i][:, :QKV], preferred_element_type=f32
                    )
            projected = projected * scale
            first, second = projected[:, :128], projected[:, 128:256]
            query = jnp.concatenate(
                [first * cos - second * sin, second * cos + first * sin], axis=-1
            ).astype(bf16)
            kv = projected[:, 256:]
            kv = kv * kcos + pltpu.roll(kv, 96, 1) * ksin_a + pltpu.roll(kv, 32, 1) * ksin_b
            key_a = jnp.where(lane < 32, kv, 0.0)
            key_a = key_a + pltpu.roll(key_a, 32, 1)
            key_a = key_a + pltpu.roll(key_a, 64, 1)
            key_b = jnp.where((lane >= 32) & (lane < 64), kv, 0.0)
            key_b = key_b + pltpu.roll(key_b, 32, 1)
            key_b = key_b + pltpu.roll(key_b, 64, 1)
            keys = jnp.concatenate([key_a, key_b], axis=-1).astype(bf16)
            zero = jnp.zeros((), bf16)
            queries = jnp.concatenate(
                [jnp.where(head_of == h, query, zero) for h in range(GROUP_HEADS)], axis=0
            )
            scores = lax.dot_general(
                queries, keys, (((1,), (1,)), ((), ())), preferred_element_type=f32
            ) * HEAD_DIM ** (-0.5)
            scores = jnp.where(allowed, scores, -1e30)
            scores = jnp.exp(scores - jnp.max(scores, axis=-1, keepdims=True))
            weights = (scores / jnp.sum(scores, axis=-1, keepdims=True)).astype(bf16)
            mixed = jnp.dot(weights, kv.astype(bf16), preferred_element_type=f32)
            rows = [mixed[h * SEQ : (h + 1) * SEQ] for h in range(GROUP_HEADS)]
            context = jnp.concatenate(
                [
                    jnp.where(lane < 64, pltpu.roll(rows[0], 64, 1), rows[1]),
                    jnp.where(lane < 64, pltpu.roll(rows[2], 64, 1), rows[3]),
                ],
                axis=-1,
            )
            contexts.append(context.astype(bf16))

        for i, (kind, k) in enumerate(BLOCKS):
            zh = info[1 + i]
            total[zh] = total[zh] + lax.dot_general(
                contexts[block_class(kind, k)],
                blocks[i][:, QKV:],
                (((1,), (1,)), ((), ())),
                preferred_element_type=f32,
            )
        for zh in range(ZH):
            for x in range(X):
                out_ref[:, pl.ds(x * 512 + zh * 128, 128)] = total[
                    zh, :, pl.ds(x * 128, 128)
                ].astype(bf16)


def run_section(step, info, values, allowed, rope, held, blocks):
    vmem = pl.BlockSpec(memory_space=pltpu.VMEM)
    return pl.pallas_call(
        functools.partial(section_kernel, step),
        out_shape=jax.ShapeDtypeStruct((SEQ, D), jnp.bfloat16),
        in_specs=[pl.BlockSpec(memory_space=pltpu.SMEM)] + [vmem] * (4 + Z),
        out_specs=vmem,
        scratch_shapes=[
            pltpu.VMEM((ZH, SEQ, BLOCK), jnp.bfloat16),
            pltpu.VMEM((ZH, SEQ, BLOCK), jnp.float32),
        ],
        input_output_aliases={4: 0},
        compiler_params=pltpu.CompilerParams(vmem_limit_bytes=20 * 1024 * 1024),
        name="section",
    )(info, values, allowed, rope, held, *blocks)


def gather_section(shard):
    block = lax.all_to_all(
        jnp.broadcast_to(shard[None], (2 * X, *shard.shape)), ("x", "core"), 0, 0
    ).reshape(BLOCK, QKV + CTX)

    def index(z, core):
        return ((z // ZL) * 2 + core) * ZL + z % ZL

    around = [
        (index(z, core), index((z + (1 if core == 0 else -1)) % Z, core))
        for z in range(Z)
        for core in range(2)
    ]
    ring, swap = [block], []
    for k in range(1, STEPS + 1):
        ring.append(lax.ppermute(ring[-1], ("z_hi", "core", "tensor"), around))
        if k < STEPS:
            swap.append(lax.ppermute(ring[-1], "core", [(0, 1), (1, 0)]))
    return ring + swap


def on_device(down_in, up_in, w_qkv, w_out, norm_gain, down_docs, up_docs):
    position = lax.axis_index("pipe")
    member = lax.axis_index("tensor")
    core = lax.axis_index("core")
    z = lax.axis_index("z_hi") * ZL + member
    sections = lax.axis_size("pipe")

    def pick(array, index):
        return lax.dynamic_index_in_dim(array, index, 0, keepdims=False)

    qkv = pick(w_qkv, position).astype(jnp.float32)
    qkv = qkv * pick(norm_gain, position).astype(jnp.float32)[:, None]
    qkv = qkv.astype(jnp.bfloat16)
    rows = qkv.shape[0]
    query = qkv[:, :256].reshape(rows, GROUP_HEADS, 2, 32).transpose(0, 2, 1, 3).reshape(rows, 256)
    shard = jnp.concatenate([query, qkv[:, 256:], pick(w_out, position).T], axis=1)
    blocks = gather_section(shard)

    offsets = np.array([0] + [-k if kind == "ring" else k for kind, k in BLOCKS], np.int32)
    places = ((z + (1 - 2 * core) * offsets) & (Z - 1)) >> 2
    info = jnp.where(np.arange(1 + Z) == 0, position, places).astype(jnp.int32)

    cos, sin = rotary_tables()
    one, zero = jnp.ones((SEQ, 64), jnp.float32), jnp.zeros((SEQ, 32), jnp.float32)
    rope = jnp.stack(
        [
            jnp.tile(cos, (1, 4)),
            jnp.tile(sin, (1, 4)),
            jnp.concatenate([cos, cos, one], axis=1),
            jnp.concatenate([-sin, zero, zero, zero], axis=1),
            jnp.concatenate([zero, sin, zero, zero], axis=1),
        ]
    )
    docs = pick(jnp.concatenate([down_docs, up_docs]), member)
    spots = jnp.arange(SEQ)
    allowed = (spots[:, None] >= spots[None, :]) & (docs[:, None] == docs[None, :])
    allowed = jnp.tile(allowed.astype(jnp.float32), (GROUP_HEADS, 1))

    values = pick(jnp.concatenate([down_in, up_in]), member)
    held = jnp.zeros((SEQ, D), jnp.bfloat16)
    for step in range(sections):
        held = run_section(step, info, values, allowed, rope, held, blocks)
        if step + 1 < sections:
            values = lax.ppermute(held, "pipe", [(step, step + 1)])

    parts = lax.all_to_all(held.reshape(4, SEQ // 4, D), "tensor", 0, 0)
    down = parts[:2]
    up = lax.ppermute(parts[2:], "pipe", [(i, sections - 1 - i) for i in range(sections)])
    return down[None], up[None]


def solution(mesh):
    fine = Mesh(
        mesh.devices.reshape(X, ZH, 2, *mesh.devices.shape[1:]),
        ("x", "z_hi", "core", "pipe", "tensor"),
    )
    dp = ("x", "z_hi", "core")
    placed = (
        P(dp, None, None),
        P(dp, None, None),
        P(None, dp, "tensor"),
        P(None, "tensor", dp),
        P(None, dp),
        P(dp, None),
        P(dp, None),
    )
    return jax.shard_map(
        on_device,
        mesh=fine,
        in_specs=placed,
        out_specs=(P("pipe", dp, "tensor", None), P("pipe", dp, "tensor", None)),
        check_vma=False,
    )
```

```python
import functools

import jax
import jax.numpy as jnp
import numpy as np
from jax import lax
from jax.experimental import pallas as pl
from jax.experimental.pallas import tpu as pltpu
from jax.sharding import Mesh, PartitionSpec as P

HEAD_DIM = 64
SEQ = 32
D = 2048
EPSILON = 1e-05
THETA = 500000.0

GROUPS = 4
GROUP_HEADS = 4
QKV = 384
CTX = 256
X = 4
ZH = 4
ZL = 4
Z = ZH * ZL
STEPS = Z // 2
ROWS = 256

OFFSETS = [-k for k in range(STEPS + 1)] + list(range(1, STEPS))

F32, BF16 = jnp.float32, jnp.bfloat16


def rotary_tables():
    half = HEAD_DIM // 2
    frequency = THETA ** (-(jnp.arange(half, dtype=jnp.float32) * 2.0 / HEAD_DIM))
    angles = jnp.arange(SEQ, dtype=jnp.float32)[:, None] * frequency[None, :]
    return jnp.cos(angles), jnp.sin(angles)


def attention(projected, rope, allowed):
    lane = lax.broadcasted_iota(jnp.int32, (SEQ, 128), 1)
    lane2 = lax.broadcasted_iota(jnp.int32, (SEQ, 256), 1)
    head_of = (lane2 % 128) // 32
    zero = jnp.zeros((), BF16)
    cos, sin, kcos, ksin_a, ksin_b = rope
    queries, keys, values = [], [], []
    for part in projected:
        first, second = part[:, :128], part[:, 128:256]
        query = jnp.concatenate(
            [first * cos - second * sin, second * cos + first * sin], axis=-1
        ).astype(BF16)
        queries.append(
            jnp.concatenate([jnp.where(head_of == h, query, zero) for h in range(GROUP_HEADS)], axis=0)
        )
    for part in projected:
        kv = part[:, 256:]
        kv = kv * kcos + pltpu.roll(kv, 96, 1) * ksin_a + pltpu.roll(kv, 32, 1) * ksin_b
        key_a = jnp.where(lane < 32, kv, 0.0)
        key_a = key_a + pltpu.roll(key_a, 32, 1)
        key_a = key_a + pltpu.roll(key_a, 64, 1)
        key_b = jnp.where((lane >= 32) & (lane < 64), kv, 0.0)
        key_b = key_b + pltpu.roll(key_b, 32, 1)
        key_b = key_b + pltpu.roll(key_b, 64, 1)
        keys.append(jnp.concatenate([key_a, key_b], axis=-1).astype(BF16))
        values.append(kv.astype(BF16))
    scores = [
        lax.dot_general(q, k, (((1,), (1,)), ((), ())), preferred_element_type=F32)
        for q, k in zip(queries, keys)
    ]
    scores = [jnp.where(allowed, s * HEAD_DIM ** (-0.5), -1e30) for s in scores]
    scores = [jnp.exp(s - jnp.max(s, axis=-1, keepdims=True)) for s in scores]
    weights = [(s * (1.0 / jnp.sum(s, axis=-1, keepdims=True))).astype(BF16) for s in scores]
    contexts = []
    for weight, value in zip(weights, values):
        mixed = jnp.dot(weight, value, preferred_element_type=F32)
        rows = [mixed[h * SEQ : (h + 1) * SEQ] for h in range(GROUP_HEADS)]
        context = jnp.concatenate(
            [
                jnp.where(lane < 64, pltpu.roll(rows[0], 64, 1), rows[1]),
                jnp.where(lane < 64, pltpu.roll(rows[2], 64, 1), rows[3]),
            ],
            axis=-1,
        )
        contexts.append(context.astype(BF16))
    return contexts


def section_kernel(step, last, info, x_ref, allowed_ref, rope_ref, held_ref, *refs):
    blocks, refs = refs[: 2 * Z], refs[2 * Z :]
    out_ref, xs, total = refs[0], refs[-2], refs[-1]

    @pl.when(info[0] != step)
    def _():
        out_ref[...] = held_ref[...]

    @pl.when(info[0] == step)
    def _():
        squares = jnp.zeros((SEQ, 1), F32)
        for j in range(2 * ZH):
            part = x_ref[:, pl.ds(j * ROWS, ROWS)]
            xs[j] = part
            wide = part.astype(F32)
            total[j] = wide
            squares = squares + jnp.sum(wide * wide, axis=-1, keepdims=True)
        scale = lax.rsqrt(squares * (1.0 / D) + EPSILON)

        projected = []
        for c in range(GROUPS):
            terms = [
                jnp.dot(xs[info[1 + i]], blocks[i][:, :QKV], preferred_element_type=F32)
                for i in range(2 * Z)
                if OFFSETS[i % Z] % ZL == c
            ]
            projected.append(functools.reduce(jnp.add, terms) * scale)
        contexts = attention(projected, [rope_ref[i] for i in range(5)], allowed_ref[...] > 0.5)
        for i in range(2 * Z):
            j = info[1 + i]
            total[j] = total[j] + jnp.dot(
                contexts[OFFSETS[i % Z] % ZL], blocks[i][:, QKV:], preferred_element_type=F32
            )

        if not last:
            for j in range(2 * ZH):
                refs[1][:, pl.ds(j * ROWS, ROWS)] = total[j].astype(BF16)
        lane = lax.broadcasted_iota(jnp.int32, (SEQ, 128), 1)
        for zh in range(ZH):
            for pair in range(2):
                one = total[zh, :, pl.ds(pair * 128, 128)]
                two = total[ZH + zh, :, pl.ds(pair * 128, 128)]
                even = jnp.where(lane < 64, one, pltpu.roll(two, 64, 1))
                odd = jnp.where(lane < 64, pltpu.roll(one, 64, 1), two)
                out_ref[:, pl.ds(2 * pair * 512 + zh * 128, 128)] = even.astype(BF16)
                out_ref[:, pl.ds((2 * pair + 1) * 512 + zh * 128, 128)] = odd.astype(BF16)


def run_section(step, last, info, values, allowed, rope, held, blocks):
    vmem = pl.BlockSpec(memory_space=pltpu.VMEM)
    shape = jax.ShapeDtypeStruct((SEQ, D), BF16)
    return pl.pallas_call(
        functools.partial(section_kernel, step, last),
        out_shape=[shape] if last else [shape, shape],
        in_specs=[pl.BlockSpec(memory_space=pltpu.SMEM)] + [vmem] * (4 + 2 * Z),
        out_specs=[vmem] if last else [vmem, vmem],
        scratch_shapes=[
            pltpu.VMEM((2 * ZH, SEQ, ROWS), BF16),
            pltpu.VMEM((2 * ZH, SEQ, ROWS), F32),
        ],
        input_output_aliases={4: 0},
        compiler_params=pltpu.CompilerParams(vmem_limit_bytes=20 * 1024 * 1024),
        name="section",
    )(info, values, allowed, rope, held, *blocks)


def shard_kernel(where, qkv_ref, out_ref, gain_ref, shard_ref):
    rows = qkv_ref.shape[1]
    section = lax.broadcasted_iota(jnp.int32, gain_ref.shape, 0)
    gain = jnp.where(section == where[0], gain_ref[...].astype(F32), 0.0)
    gain = jnp.sum(gain, axis=0, keepdims=True)
    row = lax.broadcasted_iota(jnp.int32, (rows, rows), 0)
    column = lax.broadcasted_iota(jnp.int32, (rows, rows), 1)
    gain = jnp.sum(jnp.where(row == column, gain, 0.0), axis=1, keepdims=True)
    qkv = qkv_ref[0].astype(F32) * gain
    one, two = qkv[:, :128], qkv[:, 128:256]
    lane = lax.broadcasted_iota(jnp.int32, (rows, 128), 1)

    def lanes(parts):
        result = parts[3]
        for i in (2, 1, 0):
            result = jnp.where(lane < 32 * (i + 1), parts[i], result)
        return result

    first = lanes([one, pltpu.roll(one, 96, 1), pltpu.roll(two, 64, 1), pltpu.roll(two, 32, 1)])
    second = lanes([pltpu.roll(one, 96, 1), pltpu.roll(one, 64, 1), pltpu.roll(two, 32, 1), two])
    shard = jnp.concatenate([first, second, qkv[:, 256:]], axis=1).astype(BF16)
    for x in range(X):
        shard_ref[x, :, pl.ds(0, QKV)] = shard
        shard_ref[x, :, pl.ds(QKV, CTX)] = out_ref[0]


def block_kernel(parts_ref, block_ref):
    rows = parts_ref.shape[1]
    for x in range(X):
        block_ref[pl.ds(x * rows, rows), pl.ds(0, QKV)] = parts_ref[x, :, pl.ds(0, QKV)]
    columns = jnp.concatenate([parts_ref[x, :, pl.ds(QKV, CTX)] for x in range(X)], axis=0)
    block_ref[:, pl.ds(QKV, CTX)] = columns.astype(F32).T.astype(BF16)


def gather_section(position, w_qkv, w_out, norm_gain):
    rows = w_qkv.shape[1]
    vmem = pl.BlockSpec(memory_space=pltpu.VMEM)
    shard = pl.pallas_call(
        shard_kernel,
        out_shape=jax.ShapeDtypeStruct((X, rows, QKV + CTX), BF16),
        grid_spec=pltpu.PrefetchScalarGridSpec(
            num_scalar_prefetch=1,
            grid=(1,),
            in_specs=[
                pl.BlockSpec((1, rows, QKV), lambda i, where: (where[0], 0, 0)),
                pl.BlockSpec((1, rows, CTX), lambda i, where: (where[0], 0, 0)),
                pl.BlockSpec(norm_gain.shape, lambda i, where: (0, 0)),
            ],
            out_specs=pl.BlockSpec((X, rows, QKV + CTX), lambda i, where: (0, 0, 0)),
        ),
        name="shard",
    )(position.reshape(1), w_qkv, w_out.transpose(0, 2, 1), norm_gain)
    block = pl.pallas_call(
        block_kernel,
        out_shape=jax.ShapeDtypeStruct((ROWS, QKV + CTX), BF16),
        in_specs=[vmem],
        out_specs=vmem,
        name="block",
    )(lax.all_to_all(shard, "x", 0, 0))

    axes = ("z_hi", "tensor")
    forward = [(z, (z + 1) % Z) for z in range(Z)]
    backward = [(z, (z - 1) % Z) for z in range(Z)]

    def swapped(value):
        return lax.ppermute(value, "core", [(0, 1), (1, 0)])

    own = {0: block}
    other = {}
    for k in range(1, STEPS + 1):
        ahead, behind = own[1 - k], own[k - 1]
        if k >= 2:
            other[2 - k], ahead = lax.optimization_barrier((other[2 - k], ahead))
        if k >= 3:
            other[k - 2], behind = lax.optimization_barrier((other[k - 2], behind))
        own[-k] = lax.ppermute(ahead, axes, forward)
        if k < STEPS:
            own[k] = lax.ppermute(behind, axes, backward)
        for i in sorted({1 - k, k - 1}):
            other[i] = swapped(own[i])
    other[-STEPS] = swapped(own[-STEPS])
    return [own[i] for i in OFFSETS] + [other[i] for i in OFFSETS]


def order_kernel(member, *refs):
    *received, down_ref, up_ref = refs
    for k, part in enumerate(received):
        source = (member[0] + len(received) - k) % len(received)

        @pl.when(source < 2)
        def _():
            down_ref[0, source] = part[...]

        @pl.when(source >= 2)
        def _():
            up_ref[0, source - 2] = part[...]


def exchange(held, member):
    planes, members = lax.axis_size("pipe"), lax.axis_size("tensor")
    rows = SEQ // members
    received = []
    for k in range(members):
        chunk = lax.dynamic_slice_in_dim(held, ((member + k) % members) * rows, rows, 0)
        pairs = [
            (y * members + t, (y if t < 2 else planes - 1 - y) * members + (t + k) % members)
            for y in range(planes)
            for t in range(members)
        ]
        received.append(lax.ppermute(chunk, ("pipe", "tensor"), pairs))
    vmem = pl.BlockSpec(memory_space=pltpu.VMEM)
    shape = jax.ShapeDtypeStruct((1, members // 2, rows, D), BF16)
    return pl.pallas_call(
        order_kernel,
        out_shape=[shape, shape],
        in_specs=[pl.BlockSpec(memory_space=pltpu.SMEM)] + [vmem] * members,
        out_specs=[vmem, vmem],
        name="order",
    )(member.reshape(1), *received)


def on_device(down_in, up_in, w_qkv, w_out, norm_gain, down_docs, up_docs):
    position = lax.axis_index("pipe")
    member = lax.axis_index("tensor")
    core = lax.axis_index("core")
    z = lax.axis_index("z_hi") * ZL + member
    sections = lax.axis_size("pipe")

    def pick(array, index):
        return lax.dynamic_index_in_dim(array, index, 0, keepdims=False)

    blocks = gather_section(position, w_qkv, w_out, norm_gain)

    offsets = np.array([0] + OFFSETS + OFFSETS, np.int32)
    mine = np.arange(1 + 2 * Z) <= Z
    parts = jnp.where(mine, core, 1 - core) * ZH + (((z + offsets) & (Z - 1)) >> 2)
    info = jnp.where(np.arange(1 + 2 * Z) == 0, position, parts).astype(jnp.int32)

    cos, sin = rotary_tables()
    one, zero = jnp.ones((SEQ, 64), F32), jnp.zeros((SEQ, 32), F32)
    rope = jnp.stack(
        [
            jnp.tile(cos, (1, 4)),
            jnp.tile(sin, (1, 4)),
            jnp.concatenate([cos, cos, one], axis=1),
            jnp.concatenate([-sin, zero, zero, zero], axis=1),
            jnp.concatenate([zero, sin, zero, zero], axis=1),
        ]
    )
    docs = pick(jnp.concatenate([down_docs, up_docs]), member)
    spots = jnp.arange(SEQ)
    allowed = (spots[:, None] >= spots[None, :]) & (docs[:, None] == docs[None, :])
    allowed = jnp.tile(allowed.astype(F32), (GROUP_HEADS, 1))

    values = pick(jnp.concatenate([down_in, up_in]), member)
    values = values.reshape(SEQ, X, ZH, 2, 64).transpose(0, 3, 2, 1, 4).reshape(SEQ, D)
    held = jnp.zeros((SEQ, D), BF16)
    for step in range(sections):
        last = step + 1 == sections
        held, *following = run_section(step, last, info, values, allowed, rope, held, blocks)
        if not last:
            values = lax.ppermute(following[0], "pipe", [(step, step + 1)])
    return exchange(held, member)


def solution(mesh):
    fine = Mesh(
        mesh.devices.reshape(X, ZH, 2, *mesh.devices.shape[1:]),
        ("x", "z_hi", "core", "pipe", "tensor"),
    )
    dp = ("x", "z_hi", "core")
    placed = (
        P(dp, None, None),
        P(dp, None, None),
        P(None, dp, "tensor"),
        P(None, "tensor", dp),
        P(None, dp),
        P(dp, None),
        P(dp, None),
    )
    return jax.shard_map(
        on_device,
        mesh=fine,
        in_specs=placed,
        out_specs=(P("pipe", dp, "tensor", None), P("pipe", dp, "tensor", None)),
        check_vma=False,
    )
```

```python
import functools

import jax
import jax.numpy as jnp
import numpy as np
from jax import lax
from jax.experimental import pallas as pl
from jax.experimental.pallas import tpu as pltpu
from jax.sharding import Mesh, PartitionSpec as P

HEAD_DIM = 64
SEQ = 32
D = 2048
EPSILON = 1e-05
THETA = 500000.0

GROUPS = 4
GROUP_HEADS = 4
QKV = 384
CTX = 256
X = 4
ZH = 4
ZL = 4
Z = ZH * ZL
ROWS = 256

F32, BF16 = jnp.float32, jnp.bfloat16

SMALL = pltpu.CompilerParams(vmem_limit_bytes=4 * 1024 * 1024)
MEDIUM = pltpu.CompilerParams(vmem_limit_bytes=20 * 1024 * 1024)


def rotary_tables():
    half = HEAD_DIM // 2
    lane = jnp.arange(4 * half)[None, :]
    frequency = THETA ** (-((lane % half).astype(F32) * 2.0 / HEAD_DIM))
    angles = jnp.arange(SEQ, dtype=F32)[:, None] * frequency
    cos, sin = jnp.cos(angles), jnp.sin(angles)
    return [
        cos,
        sin,
        jnp.where(lane < 2 * half, cos, 1.0),
        jnp.where(lane < half, -sin, 0.0),
        jnp.where((lane >= half) & (lane < 2 * half), sin, 0.0),
    ]


def attention(projected, rope, allowed):
    lane = lax.broadcasted_iota(jnp.int32, (SEQ, 128), 1)
    lane2 = lax.broadcasted_iota(jnp.int32, (SEQ, 256), 1)
    head_of = (lane2 % 128) // 32
    zero = jnp.zeros((), BF16)
    cos, sin, kcos, ksin_a, ksin_b = rope
    queries, keys, values = [], [], []
    for part in projected:
        first, second = part[:, :128], part[:, 128:256]
        query = jnp.concatenate(
            [first * cos - second * sin, second * cos + first * sin], axis=-1
        ).astype(BF16)
        queries.append(
            jnp.concatenate([jnp.where(head_of == h, query, zero) for h in range(GROUP_HEADS)], axis=0)
        )
    for part in projected:
        kv = part[:, 256:]
        kv = kv * kcos + pltpu.roll(kv, 96, 1) * ksin_a + pltpu.roll(kv, 32, 1) * ksin_b
        key_a = jnp.where(lane < 32, kv, 0.0)
        key_a = key_a + pltpu.roll(key_a, 32, 1)
        key_a = key_a + pltpu.roll(key_a, 64, 1)
        key_b = jnp.where((lane >= 32) & (lane < 64), kv, 0.0)
        key_b = key_b + pltpu.roll(key_b, 32, 1)
        key_b = key_b + pltpu.roll(key_b, 64, 1)
        keys.append(jnp.concatenate([key_a, key_b], axis=-1).astype(BF16))
        values.append(kv.astype(BF16))
    scores = [
        lax.dot_general(q, k, (((1,), (1,)), ((), ())), preferred_element_type=F32)
        for q, k in zip(queries, keys)
    ]
    scores = [jnp.where(allowed, s * HEAD_DIM ** (-0.5), -1e30) for s in scores]
    scores = [jnp.exp(s - jnp.max(s, axis=-1, keepdims=True)) for s in scores]
    weights = [(s * (1.0 / jnp.sum(s, axis=-1, keepdims=True))).astype(BF16) for s in scores]
    contexts = []
    for weight, value in zip(weights, values):
        mixed = jnp.dot(weight, value, preferred_element_type=F32)
        rows = [mixed[h * SEQ : (h + 1) * SEQ] for h in range(GROUP_HEADS)]
        context = jnp.concatenate(
            [
                jnp.where(lane < 64, pltpu.roll(rows[0], 64, 1), rows[1]),
                jnp.where(lane < 64, pltpu.roll(rows[2], 64, 1), rows[3]),
            ],
            axis=-1,
        )
        contexts.append(context.astype(BF16))
    return contexts


def section_kernel(step, last, where, x_ref, allowed_ref, held_ref, *refs):
    rope, weights, outputs = refs[:5], (refs[5:8], refs[8:11]), refs[11:]
    out_ref = outputs[-1]

    def rows_of(i, zh, t, columns):
        part, first = ((0, 0), (1, ZH), (2, 0), (1, 0))[t]
        return jnp.concatenate(
            [weights[i][part][x, first + zh, :, columns] for x in range(X)], axis=0
        )

    @pl.when(where[0] != step)
    def _():
        out_ref[...] = held_ref[...].astype(out_ref.dtype)

    @pl.when(where[0] == step)
    def _():
        places = [(i, zh) for i in range(2) for zh in range(ZH)]
        parts = [x_ref[:, pl.ds(j * ROWS, ROWS)] for j in range(2 * ZH)]
        squares = [jnp.sum(jnp.square(part.astype(F32)), axis=-1, keepdims=True) for part in parts]
        scale = lax.rsqrt(functools.reduce(jnp.add, squares) * (1.0 / D) + EPSILON)
        projected = []
        for t in range(GROUPS):
            terms = [
                jnp.dot(part, rows_of(i, zh, t, pl.ds(0, QKV)), preferred_element_type=F32)
                for part, (i, zh) in zip(parts, places)
            ]
            projected.append(functools.reduce(jnp.add, terms) * scale)
        contexts = attention(projected, [part[...] for part in rope], allowed_ref[...] > 0.5)
        for j, (i, zh) in enumerate(places):
            terms = [
                lax.dot_general(
                    contexts[t],
                    rows_of(i, zh, t, pl.ds(QKV, CTX)),
                    (((1,), (1,)), ((), ())),
                    preferred_element_type=F32,
                )
                for t in range(GROUPS)
            ]
            total = x_ref[:, pl.ds(j * ROWS, ROWS)].astype(F32) + functools.reduce(jnp.add, terms)
            out_ref[:, pl.ds(j * ROWS, ROWS)] = total.astype(out_ref.dtype)

    if last:
        rows = outputs[0].shape[0]
        for k, chunk_ref in enumerate(outputs[:-1]):
            place = (where[3] + k) % (SEQ // rows)
            chunk_ref[...] = out_ref[pl.ds(pl.multiple_of(place * rows, rows), rows), :].astype(BF16)


def run_section(step, last, where, values, allowed, held, rope, weights):
    vmem = pl.BlockSpec(memory_space=pltpu.VMEM)
    whole, chunk = (jax.ShapeDtypeStruct((rows, D), BF16) for rows in (SEQ, SEQ // 4))
    return pl.pallas_call(
        functools.partial(section_kernel, step, last),
        out_shape=[chunk] * 4 if last else whole,
        in_specs=[pl.BlockSpec(memory_space=pltpu.SMEM)] + [vmem] * 14,
        out_specs=[vmem] * 4 if last else vmem,
        scratch_shapes=[pltpu.VMEM((SEQ, D), F32)] if last else [],
        input_output_aliases={} if last else {3: 0},
        compiler_params=MEDIUM,
        name="section",
    )(where, values, allowed, held, *rope, *weights)


def shard_kernel(where, qkv_ref, out_ref, gain_ref, shard_ref):
    rows = qkv_ref.shape[1]
    section = lax.broadcasted_iota(jnp.int32, gain_ref.shape, 0)
    gain = jnp.where(section == where[0], gain_ref[...].astype(F32), 0.0)
    gain = jnp.sum(gain, axis=0, keepdims=True)
    row = lax.broadcasted_iota(jnp.int32, (rows, rows), 0)
    column = lax.broadcasted_iota(jnp.int32, (rows, rows), 1)
    gain = jnp.sum(jnp.where(row == column, gain, 0.0), axis=1, keepdims=True)
    qkv = qkv_ref[0].astype(F32) * gain
    one, two = qkv[:, :128], qkv[:, 128:256]
    lane = lax.broadcasted_iota(jnp.int32, (rows, 128), 1)

    def lanes(parts):
        result = parts[3]
        for i in (2, 1, 0):
            result = jnp.where(lane < 32 * (i + 1), parts[i], result)
        return result

    first = lanes([one, pltpu.roll(one, 96, 1), pltpu.roll(two, 64, 1), pltpu.roll(two, 32, 1)])
    second = lanes([pltpu.roll(one, 96, 1), pltpu.roll(one, 64, 1), pltpu.roll(two, 32, 1), two])
    shard = jnp.concatenate([first, second, qkv[:, 256:]], axis=1).astype(BF16)
    for z in range(shard_ref.shape[0]):
        shard_ref[z, :, pl.ds(0, QKV)] = shard
        shard_ref[z, :, pl.ds(QKV, CTX)] = out_ref[0]


def join_kernel(here_ref, after_ref, before_ref, half_ref, rest_ref, out_ref):
    half = half_ref.shape[0]
    out_ref[0] = here_ref[...]
    out_ref[1] = after_ref[...]
    out_ref[2, pl.ds(0, half)] = half_ref[...]
    out_ref[2, pl.ds(half, half)] = rest_ref[...]
    out_ref[3] = before_ref[...]


def gather_section(where, w_qkv, w_out, norm_gain):
    rows = w_qkv.shape[1]
    shape = (ZH, rows, QKV + CTX)
    vmem = pl.BlockSpec(memory_space=pltpu.VMEM)
    shards = pl.pallas_call(
        shard_kernel,
        out_shape=jax.ShapeDtypeStruct(shape, BF16),
        grid_spec=pltpu.PrefetchScalarGridSpec(
            num_scalar_prefetch=1,
            grid=(1,),
            in_specs=[
                pl.BlockSpec((1, rows, QKV), lambda i, where: (where[0], 0, 0)),
                pl.BlockSpec((1, rows, CTX), lambda i, where: (where[0], 0, 0)),
                pl.BlockSpec(norm_gain.shape, lambda i, where: (0, 0)),
            ],
            out_specs=pl.BlockSpec(shape, lambda i, where: (0, 0, 0)),
        ),
        compiler_params=SMALL,
        name="shard",
    )(where, w_qkv, w_out.transpose(0, 2, 1), norm_gain)

    one, other = [(x, (x + 1) % X) for x in range(X)], [(x, (x - 1) % X) for x in range(X)]

    def first_along_x(parts):
        return lax.ppermute(parts, "x", one), lax.ppermute(parts, "x", other)

    def rest_along_x(parts, before, after):
        half = parts.shape[0] // 2
        return pl.pallas_call(
            join_kernel,
            out_shape=jax.ShapeDtypeStruct((X, *parts.shape), BF16),
            in_specs=[vmem] * 5,
            out_specs=vmem,
            compiler_params=MEDIUM,
            name="join",
        )(
            parts,
            after,
            before,
            lax.ppermute(before[:half], "x", one),
            lax.ppermute(after[half:], "x", other),
        )

    def along_z(parts, by):
        return lax.ppermute(parts, ("z_hi", "tensor"), [(z, (z + by) % Z) for z in range(Z)])

    here = lax.all_to_all(shards, "z_hi", 0, 0)
    half = ZH // 2
    ahead, behind = along_z(here, 1), along_z(here, -1)
    here_x = first_along_x(here)
    near, *here_x = lax.optimization_barrier((jnp.concatenate([ahead, behind]), *here_x))
    near_x = first_along_x(near)
    across = jnp.concatenate([along_z(ahead[:half], 1), along_z(behind[half:], -1)])
    across, *here_x = lax.optimization_barrier((across, *here_x))
    across_x = first_along_x(across)
    _, *near_x = lax.optimization_barrier((across, *near_x))
    own = [
        rest_along_x(here, *here_x),
        rest_along_x(near, *near_x),
        rest_along_x(across, *across_x),
    ]
    return own + [lax.ppermute(part, "core", [(0, 1), (1, 0)]) for part in own]


def turned(values, by):
    result = values
    for count in range(1, X):
        result = jnp.where(by == count, pltpu.roll(values, 64 * count, 1), result)
    return result


def enter_kernel(where, down_ref, up_ref, down_docs_ref, up_docs_ref, out_ref, allowed_ref):
    member = where[3]
    x_ref = jnp.where(member < 2, down_ref[member % 2], up_ref[member % 2]).astype(F32)
    docs = [docs_ref[...] for docs_ref in (down_docs_ref, up_docs_ref)]
    docs = jnp.where(member < 2, docs[0], docs[1])
    docs = jnp.where(member % 2 == 0, docs[:1], docs[1:])
    row = lax.broadcasted_iota(jnp.int32, (SEQ, SEQ), 0)
    column = lax.broadcasted_iota(jnp.int32, (SEQ, SEQ), 1)
    own_docs = jnp.sum(jnp.where(row == column, docs, 0), axis=1, keepdims=True)
    allowed = jnp.where((row >= column) & (own_docs == docs), 1.0, 0.0)
    for h in range(GROUP_HEADS):
        allowed_ref[pl.ds(h * SEQ, SEQ), :] = allowed
    lane = lax.broadcasted_iota(jnp.int32, (SEQ, 128), 1)
    for zh in range(ZH):
        tiles = [x_ref[:, x * 512 + zh * 128 : x * 512 + zh * 128 + 128] for x in range(X)]
        cores = []
        for core in range(2):
            pairs = [
                jnp.where(lane < 64, a, pltpu.roll(b, 64, 1))
                if core == 0
                else jnp.where(lane < 64, pltpu.roll(a, 64, 1), b)
                for a, b in (tiles[:2], tiles[2:])
            ]
            cores.append(turned(jnp.concatenate(pairs, axis=1), (X - where[1]) % X))
        for i in range(2):
            part = jnp.where(where[2] == i, cores[0], cores[1])
            out_ref[:, pl.ds((i * ZH + zh) * ROWS, ROWS)] = part.astype(BF16)


def order_kernel(where, *refs):
    *received, down_ref, up_ref = refs
    rows = received[0].shape[0]
    values = jnp.concatenate([part[...] for part in received], axis=0).astype(F32)
    lane = lax.broadcasted_iota(jnp.int32, (values.shape[0], 128), 1)
    tiles = {}
    for zh in range(ZH):
        mine, other = (
            turned(values[:, (i * ZH + zh) * ROWS : (i * ZH + zh + 1) * ROWS], where[1])
            for i in range(2)
        )
        zero, one = jnp.where(where[2] == 0, mine, other), jnp.where(where[2] == 0, other, mine)
        for pair in range(2):
            a, b = (part[:, pair * 128 : (pair + 1) * 128] for part in (zero, one))
            tiles[2 * pair, zh] = jnp.where(lane < 64, a, pltpu.roll(b, 64, 1))
            tiles[2 * pair + 1, zh] = jnp.where(lane < 64, pltpu.roll(a, 64, 1), b)
    natural = jnp.concatenate(
        [tiles[x, zh] for x in range(X) for zh in range(ZH)], axis=1
    ).astype(BF16)
    for k in range(len(received)):
        source = (where[3] + len(received) - k) % len(received)
        part = natural[k * rows : (k + 1) * rows]

        @pl.when(source < 2)
        def _():
            down_ref[0, source] = part

        @pl.when(source >= 2)
        def _():
            up_ref[0, source - 2] = part


def exchange(chunks, where):
    planes, members = lax.axis_size("pipe"), lax.axis_size("tensor")
    rows = SEQ // members
    received = []
    for k, chunk in enumerate(chunks):
        pairs = [
            (y * members + t, (y if t < 2 else planes - 1 - y) * members + (t + k) % members)
            for y in range(planes)
            for t in range(members)
        ]
        received.append(lax.ppermute(chunk, ("pipe", "tensor"), pairs))
    vmem = pl.BlockSpec(memory_space=pltpu.VMEM)
    shape = jax.ShapeDtypeStruct((1, members // 2, rows, D), BF16)
    return pl.pallas_call(
        order_kernel,
        out_shape=[shape, shape],
        in_specs=[pl.BlockSpec(memory_space=pltpu.SMEM)] + [vmem] * members,
        out_specs=[vmem, vmem],
        compiler_params=SMALL,
        name="order",
    )(where, *received)


def on_device(down_in, up_in, w_qkv, w_out, norm_gain, down_docs, up_docs):
    where = jnp.stack([lax.axis_index(name) for name in ("pipe", "x", "core", "tensor")])
    sections = lax.axis_size("pipe")
    weights = gather_section(where, w_qkv, w_out, norm_gain)
    rope = rotary_tables()
    vmem = pl.BlockSpec(memory_space=pltpu.VMEM)
    values, allowed = pl.pallas_call(
        enter_kernel,
        out_shape=[
            jax.ShapeDtypeStruct((SEQ, D), BF16),
            jax.ShapeDtypeStruct((GROUP_HEADS * SEQ, SEQ), F32),
        ],
        in_specs=[pl.BlockSpec(memory_space=pltpu.SMEM)] + [vmem] * 4,
        out_specs=[vmem, vmem],
        compiler_params=SMALL,
        name="enter",
    )(where, down_in, up_in, down_docs, up_docs)
    held = jnp.zeros((SEQ, D), BF16)
    for step in range(sections - 1):
        held = run_section(step, False, where, values, allowed, held, rope, weights)
        values = lax.ppermute(held, "pipe", [(step, step + 1)])
    chunks = run_section(sections - 1, True, where, values, allowed, held, rope, weights)
    return exchange(chunks, where)


def solution(mesh):
    fine = Mesh(
        mesh.devices.reshape(X, ZH, 2, *mesh.devices.shape[1:]),
        ("x", "z_hi", "core", "pipe", "tensor"),
    )
    dp = ("x", "z_hi", "core")
    placed = (
        P(dp, None, None),
        P(dp, None, None),
        P(None, dp, "tensor"),
        P(None, "tensor", dp),
        P(None, dp),
        P(dp, None),
        P(dp, None),
    )
    return jax.shard_map(
        on_device,
        mesh=fine,
        in_specs=placed,
        out_specs=(P("pipe", dp, "tensor", None), P("pipe", dp, "tensor", None)),
        check_vma=False,
    )
```

```python
import functools

import jax
import jax.numpy as jnp
import numpy as np
from jax import lax
from jax.experimental import pallas as pl
from jax.experimental.pallas import tpu as pltpu
from jax.sharding import Mesh, PartitionSpec as P

HEAD_DIM = 64
SEQ = 32
D = 2048
EPSILON = 1e-05
THETA = 500000.0

GROUPS = 4
GROUP_HEADS = 4
QKV = 384
CTX = 256
X = 4
ZH = 4
ZL = 4
Z = ZH * ZL
ROWS = 256

F32, BF16 = jnp.float32, jnp.bfloat16

SMALL = pltpu.CompilerParams(vmem_limit_bytes=4 * 1024 * 1024)
MEDIUM = pltpu.CompilerParams(vmem_limit_bytes=20 * 1024 * 1024)


def rotary_tables():
    half = HEAD_DIM // 2
    lane = jnp.arange(4 * half)[None, :]
    frequency = THETA ** (-((lane % half).astype(F32) * 2.0 / HEAD_DIM))
    angles = jnp.arange(SEQ, dtype=F32)[:, None] * frequency
    cos, sin = jnp.cos(angles), jnp.sin(angles)
    return [
        cos,
        sin,
        jnp.where(lane < 2 * half, cos, 1.0),
        jnp.where(lane < half, -sin, 0.0),
        jnp.where((lane >= half) & (lane < 2 * half), sin, 0.0),
    ]


def attention(projected, rope, allowed):
    lane = lax.broadcasted_iota(jnp.int32, (SEQ, 128), 1)
    lane2 = lax.broadcasted_iota(jnp.int32, (SEQ, 256), 1)
    head_of = (lane2 % 128) // 32
    zero = jnp.zeros((), BF16)
    cos, sin, kcos, ksin_a, ksin_b = rope
    queries, keys, values = [], [], []
    for part in projected:
        first, second = part[:, :128], part[:, 128:256]
        query = jnp.concatenate(
            [first * cos - second * sin, second * cos + first * sin], axis=-1
        ).astype(BF16)
        queries.append(
            jnp.concatenate([jnp.where(head_of == h, query, zero) for h in range(GROUP_HEADS)], axis=0)
        )
    for part in projected:
        kv = part[:, 256:]
        kv = kv * kcos + pltpu.roll(kv, 96, 1) * ksin_a + pltpu.roll(kv, 32, 1) * ksin_b
        key_a = jnp.where(lane < 32, kv, 0.0)
        key_a = key_a + pltpu.roll(key_a, 32, 1)
        key_a = key_a + pltpu.roll(key_a, 64, 1)
        key_b = jnp.where((lane >= 32) & (lane < 64), kv, 0.0)
        key_b = key_b + pltpu.roll(key_b, 32, 1)
        key_b = key_b + pltpu.roll(key_b, 64, 1)
        keys.append(jnp.concatenate([key_a, key_b], axis=-1).astype(BF16))
        values.append(kv.astype(BF16))
    scores = [
        lax.dot_general(q, k, (((1,), (1,)), ((), ())), preferred_element_type=F32)
        for q, k in zip(queries, keys)
    ]
    scores = [jnp.where(allowed, s * HEAD_DIM ** (-0.5), -1e30) for s in scores]
    scores = [jnp.exp(s - jnp.max(s, axis=-1, keepdims=True)) for s in scores]
    weights = [(s * (1.0 / jnp.sum(s, axis=-1, keepdims=True))).astype(BF16) for s in scores]
    contexts = []
    for weight, value in zip(weights, values):
        mixed = jnp.dot(weight, value, preferred_element_type=F32)
        rows = [mixed[h * SEQ : (h + 1) * SEQ] for h in range(GROUP_HEADS)]
        context = jnp.concatenate(
            [
                jnp.where(lane < 64, pltpu.roll(rows[0], 64, 1), rows[1]),
                jnp.where(lane < 64, pltpu.roll(rows[2], 64, 1), rows[3]),
            ],
            axis=-1,
        )
        contexts.append(context.astype(BF16))
    return contexts


def section_kernel(step, last, where, x_ref, allowed_ref, held_ref, *refs):
    rope, weights, outputs = refs[:5], (refs[5:8], refs[8:11]), refs[11:]
    out_ref = outputs[-1]

    def rows_of(i, zh, t, columns):
        part, first = ((0, 0), (1, ZH), (2, 0), (1, 0))[t]
        return jnp.concatenate(
            [weights[i][part][x, first + zh, :, columns] for x in range(X)], axis=0
        )

    @pl.when(where[0] != step)
    def _():
        out_ref[...] = held_ref[...].astype(out_ref.dtype)

    @pl.when(where[0] == step)
    def _():
        places = [(i, zh) for i in range(2) for zh in range(ZH)]
        parts = [x_ref[:, pl.ds(j * ROWS, ROWS)] for j in range(2 * ZH)]
        squares = [jnp.sum(jnp.square(part.astype(F32)), axis=-1, keepdims=True) for part in parts]
        scale = lax.rsqrt(functools.reduce(jnp.add, squares) * (1.0 / D) + EPSILON)
        projected = []
        for t in range(GROUPS):
            terms = [
                jnp.dot(part, rows_of(i, zh, t, pl.ds(0, QKV)), preferred_element_type=F32)
                for part, (i, zh) in zip(parts, places)
            ]
            projected.append(functools.reduce(jnp.add, terms) * scale)
        contexts = attention(projected, [part[...] for part in rope], allowed_ref[...] > 0.5)
        for j, (i, zh) in enumerate(places):
            terms = [
                lax.dot_general(
                    contexts[t],
                    rows_of(i, zh, t, pl.ds(QKV, CTX)),
                    (((1,), (1,)), ((), ())),
                    preferred_element_type=F32,
                )
                for t in range(GROUPS)
            ]
            total = x_ref[:, pl.ds(j * ROWS, ROWS)].astype(F32) + functools.reduce(jnp.add, terms)
            out_ref[:, pl.ds(j * ROWS, ROWS)] = total.astype(out_ref.dtype)

    if last:
        rows = outputs[0].shape[0]
        for k, chunk_ref in enumerate(outputs[:-1]):
            place = (where[2] + k) % (SEQ // rows)
            chunk_ref[...] = out_ref[pl.ds(pl.multiple_of(place * rows, rows), rows), :].astype(BF16)


def run_section(step, last, where, values, allowed, held, rope, weights):
    vmem = pl.BlockSpec(memory_space=pltpu.VMEM)
    whole, chunk = (jax.ShapeDtypeStruct((rows, D), BF16) for rows in (SEQ, SEQ // 4))
    return pl.pallas_call(
        functools.partial(section_kernel, step, last),
        out_shape=[chunk] * 4 if last else whole,
        in_specs=[pl.BlockSpec(memory_space=pltpu.SMEM)] + [vmem] * 14,
        out_specs=[vmem] * 4 if last else vmem,
        scratch_shapes=[pltpu.VMEM((SEQ, D), F32)] if last else [],
        input_output_aliases={} if last else {3: 0},
        compiler_params=MEDIUM,
        name="section",
    )(where, values, allowed, held, *rope, *weights)


def shard_kernel(where, qkv_ref, out_ref, gain_ref, shard_ref):
    rows = qkv_ref.shape[1]
    section = lax.broadcasted_iota(jnp.int32, gain_ref.shape, 0)
    gain = jnp.where(section == where[0], gain_ref[...].astype(F32), 0.0)
    gain = jnp.sum(gain, axis=0, keepdims=True)
    row = lax.broadcasted_iota(jnp.int32, (rows, rows), 0)
    column = lax.broadcasted_iota(jnp.int32, (rows, rows), 1)
    gain = jnp.sum(jnp.where(row == column, gain, 0.0), axis=1, keepdims=True)
    qkv = qkv_ref[0].astype(F32) * gain
    one, two = qkv[:, :128], qkv[:, 128:256]
    lane = lax.broadcasted_iota(jnp.int32, (rows, 128), 1)

    def lanes(parts):
        result = parts[3]
        for i in (2, 1, 0):
            result = jnp.where(lane < 32 * (i + 1), parts[i], result)
        return result

    first = lanes([one, pltpu.roll(one, 96, 1), pltpu.roll(two, 64, 1), pltpu.roll(two, 32, 1)])
    second = lanes([pltpu.roll(one, 96, 1), pltpu.roll(one, 64, 1), pltpu.roll(two, 32, 1), two])
    shard = jnp.concatenate([first, second, qkv[:, 256:]], axis=1).astype(BF16)
    for z in range(shard_ref.shape[0]):
        shard_ref[z, :, pl.ds(0, QKV)] = shard
        shard_ref[z, :, pl.ds(QKV, CTX)] = out_ref[0]


def spread_kernel(*refs):
    *parts, out_ref, done = refs
    copies = []
    for x in range(X):
        first = 0
        for part_ref in parts:
            place = out_ref.at[x, pl.ds(first, part_ref.shape[0])]
            copies.append(pltpu.make_async_copy(part_ref, place, done.at[len(copies)]))
            first += part_ref.shape[0]
    for copy in copies:
        copy.start()
    for copy in copies:
        copy.wait()


def settle_kernel(*refs):
    count = len(refs) // 2
    copies = [
        pltpu.make_async_copy(refs[i], refs[count + i], refs[-1].at[i]) for i in range(count)
    ]
    for copy in copies:
        copy.start()
    for copy in copies:
        copy.wait()


def gather_section(where, w_qkv, w_out, norm_gain):
    rows = w_qkv.shape[1]
    shape = (ZH, rows, QKV + CTX)
    anywhere = pl.BlockSpec(memory_space=pl.ANY)
    shards = pl.pallas_call(
        shard_kernel,
        out_shape=jax.ShapeDtypeStruct(shape, BF16),
        grid_spec=pltpu.PrefetchScalarGridSpec(
            num_scalar_prefetch=1,
            grid=(1,),
            in_specs=[
                pl.BlockSpec((1, rows, QKV), lambda i, where: (where[0], 0, 0)),
                pl.BlockSpec((1, rows, CTX), lambda i, where: (where[0], 0, 0)),
                pl.BlockSpec(norm_gain.shape, lambda i, where: (0, 0)),
            ],
            out_specs=pl.BlockSpec(shape, lambda i, where: (0, 0, 0)),
        ),
        compiler_params=pltpu.CompilerParams(vmem_limit_bytes=48 * 1024 * 1024),
        name="shard",
    )(where, w_qkv, w_out.transpose(0, 2, 1), norm_gain)


    def along_x(*parts):
        count = sum(part.shape[0] for part in parts)
        copies = pl.pallas_call(
            spread_kernel,
            out_shape=jax.ShapeDtypeStruct((X, count, rows, QKV + CTX), BF16),
            in_specs=[anywhere] * len(parts),
            out_specs=anywhere,
            scratch_shapes=[pltpu.SemaphoreType.DMA((X * len(parts),))],
            compiler_params=SMALL,
            name="spread",
        )(*parts)
        return lax.all_to_all(copies, "x", 0, 0)

    def along_z(parts, by):
        return lax.ppermute(parts, ("z_hi", "tensor"), [(z, (z + by) % Z) for z in range(Z)])

    def swapped(parts):
        return lax.ppermute(parts, "core", [(0, 1), (1, 0)])

    here = lax.all_to_all(shards, "z_hi", 0, 0)
    half = ZH // 2
    ahead, behind = along_z(here, 1), along_z(here, -1)
    here_x = along_x(here)
    across = along_z(ahead[:half], 1), along_z(behind[half:], -1)
    *near, here_x = lax.optimization_barrier((ahead, behind, here_x))
    near_x = along_x(*near)
    *across, near_x = lax.optimization_barrier((*across, near_x))
    own = [here_x, near_x, along_x(*across)]
    weights = own + [swapped(part) for part in own]
    return pl.pallas_call(
        settle_kernel,
        out_shape=[jax.ShapeDtypeStruct(part.shape, part.dtype) for part in weights],
        in_specs=[anywhere] * len(weights),
        out_specs=[pl.BlockSpec(memory_space=pltpu.VMEM)] * len(weights),
        scratch_shapes=[pltpu.SemaphoreType.DMA((len(weights),))],
        compiler_params=MEDIUM,
        name="settle",
    )(*weights)


def enter_kernel(where, down_ref, up_ref, down_docs_ref, up_docs_ref, out_ref, allowed_ref):
    member = where[2]
    x_ref = jnp.where(member < 2, down_ref[member % 2], up_ref[member % 2]).astype(F32)
    docs = [docs_ref[...] for docs_ref in (down_docs_ref, up_docs_ref)]
    docs = jnp.where(member < 2, docs[0], docs[1])
    docs = jnp.where(member % 2 == 0, docs[:1], docs[1:])
    row = lax.broadcasted_iota(jnp.int32, (SEQ, SEQ), 0)
    column = lax.broadcasted_iota(jnp.int32, (SEQ, SEQ), 1)
    own_docs = jnp.sum(jnp.where(row == column, docs, 0), axis=1, keepdims=True)
    allowed = jnp.where((row >= column) & (own_docs == docs), 1.0, 0.0)
    for h in range(GROUP_HEADS):
        allowed_ref[pl.ds(h * SEQ, SEQ), :] = allowed
    lane = lax.broadcasted_iota(jnp.int32, (SEQ, 128), 1)
    for zh in range(ZH):
        tiles = [x_ref[:, x * 512 + zh * 128 : x * 512 + zh * 128 + 128] for x in range(X)]
        cores = []
        for core in range(2):
            pairs = [
                jnp.where(lane < 64, a, pltpu.roll(b, 64, 1))
                if core == 0
                else jnp.where(lane < 64, pltpu.roll(a, 64, 1), b)
                for a, b in (tiles[:2], tiles[2:])
            ]
            cores.append(jnp.concatenate(pairs, axis=1))
        for i in range(2):
            part = jnp.where(where[1] == i, cores[0], cores[1])
            out_ref[:, pl.ds((i * ZH + zh) * ROWS, ROWS)] = part.astype(BF16)


def order_kernel(where, *refs):
    *received, down_ref, up_ref = refs
    rows = received[0].shape[0]
    values = jnp.concatenate([part[...] for part in received], axis=0).astype(F32)
    lane = lax.broadcasted_iota(jnp.int32, (values.shape[0], 128), 1)
    tiles = {}
    for zh in range(ZH):
        mine, other = (
            values[:, (i * ZH + zh) * ROWS : (i * ZH + zh + 1) * ROWS] for i in range(2)
        )
        zero, one = jnp.where(where[1] == 0, mine, other), jnp.where(where[1] == 0, other, mine)
        for pair in range(2):
            a, b = (part[:, pair * 128 : (pair + 1) * 128] for part in (zero, one))
            tiles[2 * pair, zh] = jnp.where(lane < 64, a, pltpu.roll(b, 64, 1))
            tiles[2 * pair + 1, zh] = jnp.where(lane < 64, pltpu.roll(a, 64, 1), b)
    natural = jnp.concatenate(
        [tiles[x, zh] for x in range(X) for zh in range(ZH)], axis=1
    ).astype(BF16)
    for k in range(len(received)):
        source = (where[2] + len(received) - k) % len(received)
        part = natural[k * rows : (k + 1) * rows]

        @pl.when(source < 2)
        def _():
            down_ref[0, source] = part

        @pl.when(source >= 2)
        def _():
            up_ref[0, source - 2] = part


def exchange(chunks, where):
    planes, members = lax.axis_size("pipe"), lax.axis_size("tensor")
    rows = SEQ // members
    received = []
    for k, chunk in enumerate(chunks):
        pairs = [
            (y * members + t, (y if t < 2 else planes - 1 - y) * members + (t + k) % members)
            for y in range(planes)
            for t in range(members)
        ]
        received.append(lax.ppermute(chunk, ("pipe", "tensor"), pairs))
    vmem = pl.BlockSpec(memory_space=pltpu.VMEM)
    shape = jax.ShapeDtypeStruct((1, members // 2, rows, D), BF16)
    return pl.pallas_call(
        order_kernel,
        out_shape=[shape, shape],
        in_specs=[pl.BlockSpec(memory_space=pltpu.SMEM)] + [vmem] * members,
        out_specs=[vmem, vmem],
        compiler_params=SMALL,
        name="order",
    )(where, *received)


def on_device(down_in, up_in, w_qkv, w_out, norm_gain, down_docs, up_docs):
    where = jnp.stack([lax.axis_index(name) for name in ("pipe", "core", "tensor")])
    sections = lax.axis_size("pipe")
    weights = gather_section(where, w_qkv, w_out, norm_gain)
    rope = rotary_tables()
    vmem = pl.BlockSpec(memory_space=pltpu.VMEM)
    values, allowed = pl.pallas_call(
        enter_kernel,
        out_shape=[
            jax.ShapeDtypeStruct((SEQ, D), BF16),
            jax.ShapeDtypeStruct((GROUP_HEADS * SEQ, SEQ), F32),
        ],
        in_specs=[pl.BlockSpec(memory_space=pltpu.SMEM)] + [vmem] * 4,
        out_specs=[vmem, vmem],
        compiler_params=SMALL,
        name="enter",
    )(where, down_in, up_in, down_docs, up_docs)
    held = jnp.zeros((SEQ, D), BF16)
    for step in range(sections - 1):
        held = run_section(step, False, where, values, allowed, held, rope, weights)
        values = lax.ppermute(held, "pipe", [(step, step + 1)])
    chunks = run_section(sections - 1, True, where, values, allowed, held, rope, weights)
    return exchange(chunks, where)


def solution(mesh):
    fine = Mesh(
        mesh.devices.reshape(X, ZH, 2, *mesh.devices.shape[1:]),
        ("x", "z_hi", "core", "pipe", "tensor"),
    )
    dp = ("x", "z_hi", "core")
    placed = (
        P(dp, None, None),
        P(dp, None, None),
        P(None, dp, "tensor"),
        P(None, "tensor", dp),
        P(None, dp),
        P(dp, None),
        P(dp, None),
    )
    return jax.shard_map(
        on_device,
        mesh=fine,
        in_specs=placed,
        out_specs=(P("pipe", dp, "tensor", None), P("pipe", dp, "tensor", None)),
        check_vma=False,
    )
```

```python
import functools

import jax
import jax.numpy as jnp
import numpy as np
from jax import lax
from jax.experimental import pallas as pl
from jax.experimental.pallas import tpu as pltpu
from jax.sharding import Mesh, PartitionSpec as P

HEAD_DIM = 64
SEQ = 32
D = 2048
EPSILON = 1e-05
THETA = 500000.0

GROUPS = 4
GROUP_HEADS = 4
QKV = 384
CTX = 256
X = 4
ZH = 4
ZL = 4
Z = ZH * ZL
ROWS = 256

F32, BF16 = jnp.float32, jnp.bfloat16

SMALL = pltpu.CompilerParams(vmem_limit_bytes=4 * 1024 * 1024)
MEDIUM = pltpu.CompilerParams(vmem_limit_bytes=20 * 1024 * 1024)


def rotary_tables():
    half = HEAD_DIM // 2
    lane = jnp.arange(4 * half)[None, :]
    frequency = THETA ** (-((lane % half).astype(F32) * 2.0 / HEAD_DIM))
    angles = jnp.arange(SEQ, dtype=F32)[:, None] * frequency
    cos, sin = jnp.cos(angles), jnp.sin(angles)
    return [
        cos,
        sin,
        jnp.where(lane < 2 * half, cos, 1.0),
        jnp.where(lane < half, -sin, 0.0),
        jnp.where((lane >= half) & (lane < 2 * half), sin, 0.0),
    ]


def attention(projected, rope, allowed):
    lane = lax.broadcasted_iota(jnp.int32, (SEQ, 128), 1)
    lane2 = lax.broadcasted_iota(jnp.int32, (SEQ, 256), 1)
    head_of = (lane2 % 128) // 32
    zero = jnp.zeros((), BF16)
    cos, sin, kcos, ksin_a, ksin_b = rope
    queries, keys, values = [], [], []
    for part in projected:
        first, second = part[:, :128], part[:, 128:256]
        query = jnp.concatenate(
            [first * cos - second * sin, second * cos + first * sin], axis=-1
        ).astype(BF16)
        queries.append(
            jnp.concatenate([jnp.where(head_of == h, query, zero) for h in range(GROUP_HEADS)], axis=0)
        )
    for part in projected:
        kv = part[:, 256:]
        kv = kv * kcos + pltpu.roll(kv, 96, 1) * ksin_a + pltpu.roll(kv, 32, 1) * ksin_b
        key_a = jnp.where(lane < 32, kv, 0.0)
        key_a = key_a + pltpu.roll(key_a, 32, 1)
        key_a = key_a + pltpu.roll(key_a, 64, 1)
        key_b = jnp.where((lane >= 32) & (lane < 64), kv, 0.0)
        key_b = key_b + pltpu.roll(key_b, 32, 1)
        key_b = key_b + pltpu.roll(key_b, 64, 1)
        keys.append(jnp.concatenate([key_a, key_b], axis=-1).astype(BF16))
        values.append(kv.astype(BF16))
    scores = [
        lax.dot_general(q, k, (((1,), (1,)), ((), ())), preferred_element_type=F32)
        for q, k in zip(queries, keys)
    ]
    scores = [jnp.where(allowed, s * HEAD_DIM ** (-0.5), -1e30) for s in scores]
    scores = [jnp.exp(s - jnp.max(s, axis=-1, keepdims=True)) for s in scores]
    weights = [(s * (1.0 / jnp.sum(s, axis=-1, keepdims=True))).astype(BF16) for s in scores]
    contexts = []
    for weight, value in zip(weights, values):
        mixed = jnp.dot(weight, value, preferred_element_type=F32)
        rows = [mixed[h * SEQ : (h + 1) * SEQ] for h in range(GROUP_HEADS)]
        context = jnp.concatenate(
            [
                jnp.where(lane < 64, pltpu.roll(rows[0], 64, 1), rows[1]),
                jnp.where(lane < 64, pltpu.roll(rows[2], 64, 1), rows[3]),
            ],
            axis=-1,
        )
        contexts.append(context.astype(BF16))
    return contexts


def section_kernel(step, last, where, x_ref, allowed_ref, held_ref, *refs):
    rope, weights, outputs = refs[:5], (refs[5:8], refs[8:11]), refs[11:]
    out_ref = outputs[-1]

    def rows_of(i, zh, t, columns):
        part, first = ((0, 0), (1, ZH), (2, 0), (1, 0))[t]
        return jnp.concatenate(
            [weights[i][part][x, first + zh, :, columns] for x in range(X)], axis=0
        )

    @pl.when(where[0] != step)
    def _():
        out_ref[...] = held_ref[...].astype(out_ref.dtype)

    @pl.when(where[0] == step)
    def _():
        places = [(i, zh) for i in range(2) for zh in range(ZH)]
        parts = [x_ref[:, pl.ds(j * ROWS, ROWS)] for j in range(2 * ZH)]
        squares = [jnp.sum(jnp.square(part.astype(F32)), axis=-1, keepdims=True) for part in parts]
        scale = lax.rsqrt(functools.reduce(jnp.add, squares) * (1.0 / D) + EPSILON)
        projected = []
        for t in range(GROUPS):
            terms = [
                jnp.dot(part, rows_of(i, zh, t, pl.ds(0, QKV)), preferred_element_type=F32)
                for part, (i, zh) in zip(parts, places)
            ]
            projected.append(functools.reduce(jnp.add, terms) * scale)
        contexts = attention(projected, [part[...] for part in rope], allowed_ref[...] > 0.5)
        for j, (i, zh) in enumerate(places):
            terms = [
                lax.dot_general(
                    contexts[t],
                    rows_of(i, zh, t, pl.ds(QKV, CTX)),
                    (((1,), (1,)), ((), ())),
                    preferred_element_type=F32,
                )
                for t in range(GROUPS)
            ]
            total = x_ref[:, pl.ds(j * ROWS, ROWS)].astype(F32) + functools.reduce(jnp.add, terms)
            out_ref[:, pl.ds(j * ROWS, ROWS)] = total.astype(out_ref.dtype)

    if last:
        rows = outputs[0].shape[0]
        for k, chunk_ref in enumerate(outputs[:-1]):
            place = (where[3] + k) % (SEQ // rows)
            chunk_ref[...] = out_ref[pl.ds(pl.multiple_of(place * rows, rows), rows), :].astype(BF16)


def run_section(step, last, where, values, allowed, held, rope, weights):
    vmem = pl.BlockSpec(memory_space=pltpu.VMEM)
    whole, chunk = (jax.ShapeDtypeStruct((rows, D), BF16) for rows in (SEQ, SEQ // 4))
    return pl.pallas_call(
        functools.partial(section_kernel, step, last),
        out_shape=[chunk] * 4 if last else whole,
        in_specs=[pl.BlockSpec(memory_space=pltpu.SMEM)] + [vmem] * 14,
        out_specs=[vmem] * 4 if last else vmem,
        scratch_shapes=[pltpu.VMEM((SEQ, D), F32)] if last else [],
        input_output_aliases={} if last else {3: 0},
        compiler_params=MEDIUM,
        name="section",
    )(where, values, allowed, held, *rope, *weights)


def shard_kernel(where, qkv_any, out_any, gain_any, shard_ref, qkv_ref, out_ref, gain_ref, done):
    copies = [
        pltpu.make_async_copy(qkv_any.at[where[0]], qkv_ref, done.at[0]),
        pltpu.make_async_copy(out_any.at[where[0]], out_ref, done.at[1]),
        pltpu.make_async_copy(gain_any, gain_ref, done.at[2]),
    ]
    for copy in copies:
        copy.start()
    for copy in copies:
        copy.wait()
    rows = qkv_ref.shape[0]
    section = lax.broadcasted_iota(jnp.int32, gain_ref.shape, 0)
    gain = jnp.where(section == where[0], gain_ref[...].astype(F32), 0.0)
    gain = jnp.sum(gain, axis=0, keepdims=True)
    row = lax.broadcasted_iota(jnp.int32, (rows, rows), 0)
    column = lax.broadcasted_iota(jnp.int32, (rows, rows), 1)
    gain = jnp.sum(jnp.where(row == column, gain, 0.0), axis=1, keepdims=True)
    qkv = qkv_ref[...].astype(F32) * gain
    one, two = qkv[:, :128], qkv[:, 128:256]
    lane = lax.broadcasted_iota(jnp.int32, (rows, 128), 1)

    def lanes(parts):
        result = parts[3]
        for i in (2, 1, 0):
            result = jnp.where(lane < 32 * (i + 1), parts[i], result)
        return result

    first = lanes([one, pltpu.roll(one, 96, 1), pltpu.roll(two, 64, 1), pltpu.roll(two, 32, 1)])
    second = lanes([pltpu.roll(one, 96, 1), pltpu.roll(one, 64, 1), pltpu.roll(two, 32, 1), two])
    shard_ref[:, pl.ds(0, 128)] = first.astype(BF16)
    shard_ref[:, pl.ds(128, 128)] = second.astype(BF16)
    shard_ref[:, pl.ds(256, 128)] = qkv[:, 256:].astype(BF16)
    shard_ref[:, pl.ds(QKV, CTX)] = out_ref[...]


def column_kernel(where, own_ref, below_ref, above_ref, half_ref, rest_ref, out_ref):
    own, half = where[4], half_ref.shape[0]
    out_ref[own] = own_ref[...]
    out_ref[(own + ZH - 1) % ZH] = below_ref[...]
    out_ref[(own + 1) % ZH] = above_ref[...]
    out_ref[(own + 2) % ZH, pl.ds(0, half)] = half_ref[...]
    out_ref[(own + 2) % ZH, pl.ds(half, half)] = rest_ref[...]


def join_kernel(here_ref, after_ref, before_ref, half_ref, rest_ref, out_ref):
    half = half_ref.shape[0]
    out_ref[0] = here_ref[...]
    out_ref[1] = after_ref[...]
    out_ref[2, pl.ds(0, half)] = half_ref[...]
    out_ref[2, pl.ds(half, half)] = rest_ref[...]
    out_ref[3] = before_ref[...]


def gather_section(where, w_qkv, w_out, norm_gain):
    rows = w_qkv.shape[1]
    vmem = pl.BlockSpec(memory_space=pltpu.VMEM)
    smem = pl.BlockSpec(memory_space=pltpu.SMEM)
    shard = pl.pallas_call(
        shard_kernel,
        out_shape=jax.ShapeDtypeStruct((rows, QKV + CTX), BF16),
        in_specs=[smem] + [pl.BlockSpec(memory_space=pl.ANY)] * 3,
        out_specs=vmem,
        scratch_shapes=[
            pltpu.VMEM((rows, QKV), BF16),
            pltpu.VMEM((rows, CTX), BF16),
            pltpu.VMEM(norm_gain.shape, BF16),
            pltpu.SemaphoreType.DMA((3,)),
        ],
        name="shard",
    )(where, w_qkv, w_out.transpose(0, 2, 1), norm_gain)

    one, other = [(x, (x + 1) % X) for x in range(X)], [(x, (x - 1) % X) for x in range(X)]

    def first_along_x(parts):
        return lax.ppermute(parts, "x", one), lax.ppermute(parts, "x", other)

    def rest_along_x(before, after):
        half = before.shape[0] // 2
        return lax.ppermute(before[:half], "x", one), lax.ppermute(after[half:], "x", other)

    def join(here, before, after, half, rest):
        return pl.pallas_call(
            join_kernel,
            out_shape=jax.ShapeDtypeStruct((X, *here.shape), BF16),
            in_specs=[vmem] * 5,
            out_specs=vmem,
            compiler_params=MEDIUM,
            name="join",
        )(here, after, before, half, rest)

    def along_z(parts, by):
        return lax.ppermute(parts, ("z_hi", "tensor"), [(z, (z + by) % Z) for z in range(Z)])

    here = pl.pallas_call(
        column_kernel,
        out_shape=jax.ShapeDtypeStruct((ZH, *shard.shape), BF16),
        in_specs=[smem] + [vmem] * 5,
        out_specs=vmem,
        compiler_params=SMALL,
        name="column",
    )(
        where,
        shard,
        along_z(shard, ZL),
        along_z(shard, -ZL),
        along_z(shard[: rows // 2], 2 * ZL),
        along_z(shard[rows // 2 :], -2 * ZL),
    )
    half = ZH // 2
    ahead, behind = along_z(here, 1), along_z(here, -1)
    here_x = first_along_x(here)
    near, *here_x = lax.optimization_barrier((jnp.concatenate([ahead, behind]), *here_x))
    near_x = first_along_x(near)
    across = jnp.concatenate([along_z(ahead[:half], 1), along_z(behind[half:], -1)])
    here_rest = rest_along_x(*here_x)
    across, *here_rest = lax.optimization_barrier((across, *here_rest))
    across_x = first_along_x(across)
    near_rest = rest_along_x(*near_x)
    *across_x, near_0, near_1 = lax.optimization_barrier((*across_x, *near_rest))
    across_rest = rest_along_x(*across_x)
    own = [
        join(here, *here_x, *here_rest),
        join(near, *near_x, near_0, near_1),
        join(across, *across_x, *across_rest),
    ]
    return own + [lax.ppermute(part, "core", [(0, 1), (1, 0)]) for part in own]


def turned(values, by):
    result = values
    for count in range(1, X):
        result = jnp.where(by == count, pltpu.roll(values, 64 * count, 1), result)
    return result


def enter_kernel(where, down_ref, up_ref, down_docs_ref, up_docs_ref, out_ref, allowed_ref):
    member = where[3]
    x_ref = jnp.where(member < 2, down_ref[member % 2], up_ref[member % 2]).astype(F32)
    docs = [docs_ref[...] for docs_ref in (down_docs_ref, up_docs_ref)]
    docs = jnp.where(member < 2, docs[0], docs[1])
    docs = jnp.where(member % 2 == 0, docs[:1], docs[1:])
    row = lax.broadcasted_iota(jnp.int32, (SEQ, SEQ), 0)
    column = lax.broadcasted_iota(jnp.int32, (SEQ, SEQ), 1)
    own_docs = jnp.sum(jnp.where(row == column, docs, 0), axis=1, keepdims=True)
    allowed = jnp.where((row >= column) & (own_docs == docs), 1.0, 0.0)
    for h in range(GROUP_HEADS):
        allowed_ref[pl.ds(h * SEQ, SEQ), :] = allowed
    lane = lax.broadcasted_iota(jnp.int32, (SEQ, 128), 1)
    for zh in range(ZH):
        tiles = [x_ref[:, x * 512 + zh * 128 : x * 512 + zh * 128 + 128] for x in range(X)]
        cores = []
        for core in range(2):
            pairs = [
                jnp.where(lane < 64, a, pltpu.roll(b, 64, 1))
                if core == 0
                else jnp.where(lane < 64, pltpu.roll(a, 64, 1), b)
                for a, b in (tiles[:2], tiles[2:])
            ]
            cores.append(turned(jnp.concatenate(pairs, axis=1), (X - where[1]) % X))
        for i in range(2):
            part = jnp.where(where[2] == i, cores[0], cores[1])
            out_ref[:, pl.ds((i * ZH + zh) * ROWS, ROWS)] = part.astype(BF16)


def order_kernel(where, *refs):
    *received, down_ref, up_ref = refs
    rows = received[0].shape[0]
    values = jnp.concatenate([part[...] for part in received], axis=0).astype(F32)
    lane = lax.broadcasted_iota(jnp.int32, (values.shape[0], 128), 1)
    tiles = {}
    for zh in range(ZH):
        mine, other = (
            turned(values[:, (i * ZH + zh) * ROWS : (i * ZH + zh + 1) * ROWS], where[1])
            for i in range(2)
        )
        zero, one = jnp.where(where[2] == 0, mine, other), jnp.where(where[2] == 0, other, mine)
        for pair in range(2):
            a, b = (part[:, pair * 128 : (pair + 1) * 128] for part in (zero, one))
            tiles[2 * pair, zh] = jnp.where(lane < 64, a, pltpu.roll(b, 64, 1))
            tiles[2 * pair + 1, zh] = jnp.where(lane < 64, pltpu.roll(a, 64, 1), b)
    natural = jnp.concatenate(
        [tiles[x, zh] for x in range(X) for zh in range(ZH)], axis=1
    ).astype(BF16)
    for k in range(len(received)):
        source = (where[3] + len(received) - k) % len(received)
        part = natural[k * rows : (k + 1) * rows]

        @pl.when(source < 2)
        def _():
            down_ref[0, source] = part

        @pl.when(source >= 2)
        def _():
            up_ref[0, source - 2] = part


def exchange(chunks, where):
    planes, members = lax.axis_size("pipe"), lax.axis_size("tensor")
    rows = SEQ // members
    received = []
    for k, chunk in enumerate(chunks):
        pairs = [
            (y * members + t, (y if t < 2 else planes - 1 - y) * members + (t + k) % members)
            for y in range(planes)
            for t in range(members)
        ]
        received.append(lax.ppermute(chunk, ("pipe", "tensor"), pairs))
    vmem = pl.BlockSpec(memory_space=pltpu.VMEM)
    shape = jax.ShapeDtypeStruct((1, members // 2, rows, D), BF16)
    return pl.pallas_call(
        order_kernel,
        out_shape=[shape, shape],
        in_specs=[pl.BlockSpec(memory_space=pltpu.SMEM)] + [vmem] * members,
        out_specs=[vmem, vmem],
        compiler_params=SMALL,
        name="order",
    )(where, *received)


def on_device(down_in, up_in, w_qkv, w_out, norm_gain, down_docs, up_docs):
    where = jnp.stack([lax.axis_index(name) for name in ("pipe", "x", "core", "tensor", "z_hi")])
    sections = lax.axis_size("pipe")
    weights = gather_section(where, w_qkv, w_out, norm_gain)
    rope = rotary_tables()
    vmem = pl.BlockSpec(memory_space=pltpu.VMEM)
    values, allowed = pl.pallas_call(
        enter_kernel,
        out_shape=[
            jax.ShapeDtypeStruct((SEQ, D), BF16),
            jax.ShapeDtypeStruct((GROUP_HEADS * SEQ, SEQ), F32),
        ],
        in_specs=[pl.BlockSpec(memory_space=pltpu.SMEM)] + [vmem] * 4,
        out_specs=[vmem, vmem],
        compiler_params=SMALL,
        name="enter",
    )(where, down_in, up_in, down_docs, up_docs)
    held = jnp.zeros((SEQ, D), BF16)
    for step in range(sections - 1):
        held = run_section(step, False, where, values, allowed, held, rope, weights)
        values = lax.ppermute(held, "pipe", [(step, step + 1)])
    chunks = run_section(sections - 1, True, where, values, allowed, held, rope, weights)
    return exchange(chunks, where)


def solution(mesh):
    fine = Mesh(
        mesh.devices.reshape(X, ZH, 2, *mesh.devices.shape[1:]),
        ("x", "z_hi", "core", "pipe", "tensor"),
    )
    dp = ("x", "z_hi", "core")
    placed = (
        P(dp, None, None),
        P(dp, None, None),
        P(None, dp, "tensor"),
        P(None, "tensor", dp),
        P(None, dp),
        P(dp, None),
        P(dp, None),
    )
    return jax.shard_map(
        on_device,
        mesh=fine,
        in_specs=placed,
        out_specs=(P("pipe", dp, "tensor", None), P("pipe", dp, "tensor", None)),
        check_vma=False,
    )
```

```python
import functools

import jax
import jax.numpy as jnp
import numpy as np
from jax import lax
from jax.experimental import pallas as pl
from jax.experimental.pallas import tpu as pltpu
from jax.sharding import Mesh, PartitionSpec as P

HEAD_DIM = 64
SEQ = 32
D = 2048
EPSILON = 1e-05
THETA = 500000.0

GROUPS = 4
GROUP_HEADS = 4
QKV = 384
CTX = 256
X = 4
ZH = 4
ZL = 4
Z = ZH * ZL
ROWS = 256

F32, BF16 = jnp.float32, jnp.bfloat16

SMALL = pltpu.CompilerParams(vmem_limit_bytes=4 * 1024 * 1024)
MEDIUM = pltpu.CompilerParams(vmem_limit_bytes=20 * 1024 * 1024)


def rotary_tables():
    half = HEAD_DIM // 2
    lane = jnp.arange(4 * half)[None, :]
    frequency = THETA ** (-((lane % half).astype(F32) * 2.0 / HEAD_DIM))
    angles = jnp.arange(SEQ, dtype=F32)[:, None] * frequency
    cos, sin = jnp.cos(angles), jnp.sin(angles)
    return [
        cos,
        sin,
        jnp.where(lane < 2 * half, cos, 1.0),
        jnp.where(lane < half, -sin, 0.0),
        jnp.where((lane >= half) & (lane < 2 * half), sin, 0.0),
    ]


def attention(projected, rope, allowed):
    lane = lax.broadcasted_iota(jnp.int32, (SEQ, 128), 1)
    lane2 = lax.broadcasted_iota(jnp.int32, (SEQ, 256), 1)
    head_of = (lane2 % 128) // 32
    zero = jnp.zeros((), BF16)
    cos, sin, kcos, ksin_a, ksin_b = rope
    queries, keys, values = [], [], []
    for part in projected:
        first, second = part[:, :128], part[:, 128:256]
        query = jnp.concatenate(
            [first * cos - second * sin, second * cos + first * sin], axis=-1
        ).astype(BF16)
        queries.append(
            jnp.concatenate([jnp.where(head_of == h, query, zero) for h in range(GROUP_HEADS)], axis=0)
        )
    for part in projected:
        kv = part[:, 256:]
        kv = kv * kcos + pltpu.roll(kv, 96, 1) * ksin_a + pltpu.roll(kv, 32, 1) * ksin_b
        key_a = jnp.where(lane < 32, kv, 0.0)
        key_a = key_a + pltpu.roll(key_a, 32, 1)
        key_a = key_a + pltpu.roll(key_a, 64, 1)
        key_b = jnp.where((lane >= 32) & (lane < 64), kv, 0.0)
        key_b = key_b + pltpu.roll(key_b, 32, 1)
        key_b = key_b + pltpu.roll(key_b, 64, 1)
        keys.append(jnp.concatenate([key_a, key_b], axis=-1).astype(BF16))
        values.append(kv.astype(BF16))
    scores = [
        lax.dot_general(q, k, (((1,), (1,)), ((), ())), preferred_element_type=F32)
        for q, k in zip(queries, keys)
    ]
    scores = [jnp.where(allowed, s * HEAD_DIM ** (-0.5), -1e30) for s in scores]
    scores = [jnp.exp(s - jnp.max(s, axis=-1, keepdims=True)) for s in scores]
    weights = [(s * (1.0 / jnp.sum(s, axis=-1, keepdims=True))).astype(BF16) for s in scores]
    contexts = []
    for weight, value in zip(weights, values):
        mixed = jnp.dot(weight, value, preferred_element_type=F32)
        rows = [mixed[h * SEQ : (h + 1) * SEQ] for h in range(GROUP_HEADS)]
        context = jnp.concatenate(
            [
                jnp.where(lane < 64, pltpu.roll(rows[0], 64, 1), rows[1]),
                jnp.where(lane < 64, pltpu.roll(rows[2], 64, 1), rows[3]),
            ],
            axis=-1,
        )
        contexts.append(context.astype(BF16))
    return contexts


def section_kernel(step, last, where, x_ref, allowed_ref, held_ref, *refs):
    rope, group, weights, outputs = refs[:5], refs[5], (refs[6:8], refs[8:10]), refs[10:]
    out_ref = outputs[-1]

    def rows_of(i, zh, t, columns):
        if t == 0:
            core = where[2] if i == 0 else 1 - where[2]
            places = [(((where[1] + x) % X) * ZH + zh) * 2 + core for x in range(X)]
            return jnp.concatenate([group[place, :, columns] for place in places], axis=0)
        part, first = ((0, ZH), (1, 0), (0, 0))[t - 1]
        return jnp.concatenate(
            [weights[i][part][x, first + zh, :, columns] for x in range(X)], axis=0
        )

    @pl.when(where[0] != step)
    def _():
        out_ref[...] = held_ref[...].astype(out_ref.dtype)

    @pl.when(where[0] == step)
    def _():
        places = [(i, zh) for i in range(2) for zh in range(ZH)]
        parts = [x_ref[:, pl.ds(j * ROWS, ROWS)] for j in range(2 * ZH)]
        squares = [jnp.sum(jnp.square(part.astype(F32)), axis=-1, keepdims=True) for part in parts]
        scale = lax.rsqrt(functools.reduce(jnp.add, squares) * (1.0 / D) + EPSILON)
        projected = []
        for t in range(GROUPS):
            terms = [
                jnp.dot(part, rows_of(i, zh, t, pl.ds(0, QKV)), preferred_element_type=F32)
                for part, (i, zh) in zip(parts, places)
            ]
            projected.append(functools.reduce(jnp.add, terms) * scale)
        contexts = attention(projected, [part[...] for part in rope], allowed_ref[...] > 0.5)
        for j, (i, zh) in enumerate(places):
            terms = [
                lax.dot_general(
                    contexts[t],
                    rows_of(i, zh, t, pl.ds(QKV, CTX)),
                    (((1,), (1,)), ((), ())),
                    preferred_element_type=F32,
                )
                for t in range(GROUPS)
            ]
            total = x_ref[:, pl.ds(j * ROWS, ROWS)].astype(F32) + functools.reduce(jnp.add, terms)
            out_ref[:, pl.ds(j * ROWS, ROWS)] = total.astype(out_ref.dtype)

    if last:
        rows = outputs[0].shape[0]
        for k, chunk_ref in enumerate(outputs[:-1]):
            place = (where[3] + k) % (SEQ // rows)
            chunk_ref[...] = out_ref[pl.ds(pl.multiple_of(place * rows, rows), rows), :].astype(BF16)


def run_section(step, last, where, values, allowed, held, rope, weights):
    vmem = pl.BlockSpec(memory_space=pltpu.VMEM)
    whole, chunk = (jax.ShapeDtypeStruct((rows, D), BF16) for rows in (SEQ, SEQ // 4))
    return pl.pallas_call(
        functools.partial(section_kernel, step, last),
        out_shape=[chunk] * 4 if last else whole,
        in_specs=[pl.BlockSpec(memory_space=pltpu.SMEM)] + [vmem] * 13,
        out_specs=[vmem] * 4 if last else vmem,
        scratch_shapes=[pltpu.VMEM((SEQ, D), F32)] if last else [],
        input_output_aliases={} if last else {3: 0},
        compiler_params=MEDIUM,
        name="section",
    )(where, values, allowed, held, *rope, *weights)


def shard_kernel(
    where, qkv_any, out_any, gain_any, shard_ref, copies_ref, qkv_ref, out_ref, gain_ref, done
):
    copies = [
        pltpu.make_async_copy(qkv_any.at[where[0]], qkv_ref, done.at[0]),
        pltpu.make_async_copy(out_any.at[where[0]], out_ref, done.at[1]),
        pltpu.make_async_copy(gain_any, gain_ref, done.at[2]),
    ]
    for copy in copies:
        copy.start()
    for copy in copies:
        copy.wait()
    rows = qkv_ref.shape[0]
    section = lax.broadcasted_iota(jnp.int32, gain_ref.shape, 0)
    gain = jnp.where(section == where[0], gain_ref[...].astype(F32), 0.0)
    gain = jnp.sum(gain, axis=0, keepdims=True)
    row = lax.broadcasted_iota(jnp.int32, (rows, rows), 0)
    column = lax.broadcasted_iota(jnp.int32, (rows, rows), 1)
    gain = jnp.sum(jnp.where(row == column, gain, 0.0), axis=1, keepdims=True)
    qkv = qkv_ref[...].astype(F32) * gain
    one, two = qkv[:, :128], qkv[:, 128:256]
    lane = lax.broadcasted_iota(jnp.int32, (rows, 128), 1)

    def lanes(parts):
        result = parts[3]
        for i in (2, 1, 0):
            result = jnp.where(lane < 32 * (i + 1), parts[i], result)
        return result

    first = lanes([one, pltpu.roll(one, 96, 1), pltpu.roll(two, 64, 1), pltpu.roll(two, 32, 1)])
    second = lanes([pltpu.roll(one, 96, 1), pltpu.roll(one, 64, 1), pltpu.roll(two, 32, 1), two])
    shard_ref[:, pl.ds(0, 128)] = first.astype(BF16)
    shard_ref[:, pl.ds(128, 128)] = second.astype(BF16)
    shard_ref[:, pl.ds(256, 128)] = qkv[:, 256:].astype(BF16)
    shard_ref[:, pl.ds(QKV, CTX)] = out_ref[...]
    for zh in range(copies_ref.shape[0]):
        copies_ref[zh] = shard_ref[...]


def settle_kernel(*refs):
    count = len(refs) // 2
    copies = [
        pltpu.make_async_copy(refs[i], refs[count + i], refs[-1].at[i]) for i in range(count)
    ]
    for copy in copies:
        copy.start()
    for copy in copies:
        copy.wait()


def join_kernel(here_ref, after_ref, before_ref, half_ref, rest_ref, out_ref):
    half = half_ref.shape[0]
    out_ref[0] = here_ref[...]
    out_ref[1] = after_ref[...]
    out_ref[2, pl.ds(0, half)] = half_ref[...]
    out_ref[2, pl.ds(half, half)] = rest_ref[...]
    out_ref[3] = before_ref[...]


def gather_section(where, w_qkv, w_out, norm_gain):
    rows = w_qkv.shape[1]
    vmem = pl.BlockSpec(memory_space=pltpu.VMEM)
    smem = pl.BlockSpec(memory_space=pltpu.SMEM)
    anywhere = pl.BlockSpec(memory_space=pl.ANY)
    shard, shards = pl.pallas_call(
        shard_kernel,
        out_shape=[
            jax.ShapeDtypeStruct((rows, QKV + CTX), BF16),
            jax.ShapeDtypeStruct((ZH, rows, QKV + CTX), BF16),
        ],
        in_specs=[smem] + [anywhere] * 3,
        out_specs=[vmem, vmem],
        scratch_shapes=[
            pltpu.VMEM((rows, QKV), BF16),
            pltpu.VMEM((rows, CTX), BF16),
            pltpu.VMEM(norm_gain.shape, BF16),
            pltpu.SemaphoreType.DMA((3,)),
        ],
        name="shard",
    )(where, w_qkv, w_out.transpose(0, 2, 1), norm_gain)
    group = lax.all_gather(shard, ("x", "z_hi", "core"))

    one, other = [(x, (x + 1) % X) for x in range(X)], [(x, (x - 1) % X) for x in range(X)]

    def first_along_x(parts):
        return lax.ppermute(parts, "x", one), lax.ppermute(parts, "x", other)

    def rest_along_x(before, after):
        half = before.shape[0] // 2
        return lax.ppermute(before[:half], "x", one), lax.ppermute(after[half:], "x", other)

    def join(here, before, after, half, rest):
        return pl.pallas_call(
            join_kernel,
            out_shape=jax.ShapeDtypeStruct((X, *here.shape), BF16),
            in_specs=[vmem] * 5,
            out_specs=vmem,
            compiler_params=MEDIUM,
            name="join",
        )(here, after, before, half, rest)

    def along_z(parts, by):
        return lax.ppermute(parts, ("z_hi", "tensor"), [(z, (z + by) % Z) for z in range(Z)])

    here = lax.all_to_all(shards, "z_hi", 0, 0)
    half = ZH // 2
    ahead, behind = along_z(here, 1), along_z(here, -1)
    near = jnp.concatenate([ahead, behind])
    near_x = first_along_x(near)
    across = jnp.concatenate([along_z(ahead[:half], 1), along_z(behind[half:], -1)])
    across_x = first_along_x(across)
    near_rest = rest_along_x(*near_x)
    *across_x, near_0, near_1 = lax.optimization_barrier((*across_x, *near_rest))
    across_rest = rest_along_x(*across_x)
    own = [join(near, *near_x, near_0, near_1), join(across, *across_x, *across_rest)]
    other_core = [lax.ppermute(part, "core", [(0, 1), (1, 0)]) for part in own]
    weights = [group] + own + other_core
    return pl.pallas_call(
        settle_kernel,
        out_shape=[jax.ShapeDtypeStruct(part.shape, BF16) for part in weights],
        in_specs=[anywhere] * len(weights),
        out_specs=[vmem] * len(weights),
        scratch_shapes=[pltpu.SemaphoreType.DMA((len(weights),))],
        compiler_params=MEDIUM,
        name="settle",
    )(*weights)


def turned(values, by):
    result = values
    for count in range(1, X):
        result = jnp.where(by == count, pltpu.roll(values, 64 * count, 1), result)
    return result


def enter_kernel(where, down_ref, up_ref, down_docs_ref, up_docs_ref, out_ref, allowed_ref):
    member = where[3]
    x_ref = jnp.where(member < 2, down_ref[member % 2], up_ref[member % 2]).astype(F32)
    docs = [docs_ref[...] for docs_ref in (down_docs_ref, up_docs_ref)]
    docs = jnp.where(member < 2, docs[0], docs[1])
    docs = jnp.where(member % 2 == 0, docs[:1], docs[1:])
    row = lax.broadcasted_iota(jnp.int32, (SEQ, SEQ), 0)
    column = lax.broadcasted_iota(jnp.int32, (SEQ, SEQ), 1)
    own_docs = jnp.sum(jnp.where(row == column, docs, 0), axis=1, keepdims=True)
    allowed = jnp.where((row >= column) & (own_docs == docs), 1.0, 0.0)
    for h in range(GROUP_HEADS):
        allowed_ref[pl.ds(h * SEQ, SEQ), :] = allowed
    lane = lax.broadcasted_iota(jnp.int32, (SEQ, 128), 1)
    for zh in range(ZH):
        tiles = [x_ref[:, x * 512 + zh * 128 : x * 512 + zh * 128 + 128] for x in range(X)]
        cores = []
        for core in range(2):
            pairs = [
                jnp.where(lane < 64, a, pltpu.roll(b, 64, 1))
                if core == 0
                else jnp.where(lane < 64, pltpu.roll(a, 64, 1), b)
                for a, b in (tiles[:2], tiles[2:])
            ]
            cores.append(turned(jnp.concatenate(pairs, axis=1), (X - where[1]) % X))
        for i in range(2):
            part = jnp.where(where[2] == i, cores[0], cores[1])
            out_ref[:, pl.ds((i * ZH + zh) * ROWS, ROWS)] = part.astype(BF16)


def order_kernel(where, *refs):
    *received, down_ref, up_ref = refs
    rows = received[0].shape[0]
    values = jnp.concatenate([part[...] for part in received], axis=0).astype(F32)
    lane = lax.broadcasted_iota(jnp.int32, (values.shape[0], 128), 1)
    tiles = {}
    for zh in range(ZH):
        mine, other = (
            turned(values[:, (i * ZH + zh) * ROWS : (i * ZH + zh + 1) * ROWS], where[1])
            for i in range(2)
        )
        zero, one = jnp.where(where[2] == 0, mine, other), jnp.where(where[2] == 0, other, mine)
        for pair in range(2):
            a, b = (part[:, pair * 128 : (pair + 1) * 128] for part in (zero, one))
            tiles[2 * pair, zh] = jnp.where(lane < 64, a, pltpu.roll(b, 64, 1))
            tiles[2 * pair + 1, zh] = jnp.where(lane < 64, pltpu.roll(a, 64, 1), b)
    natural = jnp.concatenate(
        [tiles[x, zh] for x in range(X) for zh in range(ZH)], axis=1
    ).astype(BF16)
    for k in range(len(received)):
        source = (where[3] + len(received) - k) % len(received)
        part = natural[k * rows : (k + 1) * rows]

        @pl.when(source < 2)
        def _():
            down_ref[0, source] = part

        @pl.when(source >= 2)
        def _():
            up_ref[0, source - 2] = part


def exchange(chunks, where):
    planes, members = lax.axis_size("pipe"), lax.axis_size("tensor")
    rows = SEQ // members
    received = []
    for k, chunk in enumerate(chunks):
        pairs = [
            (y * members + t, (y if t < 2 else planes - 1 - y) * members + (t + k) % members)
            for y in range(planes)
            for t in range(members)
        ]
        received.append(lax.ppermute(chunk, ("pipe", "tensor"), pairs))
    vmem = pl.BlockSpec(memory_space=pltpu.VMEM)
    shape = jax.ShapeDtypeStruct((1, members // 2, rows, D), BF16)
    return pl.pallas_call(
        order_kernel,
        out_shape=[shape, shape],
        in_specs=[pl.BlockSpec(memory_space=pltpu.SMEM)] + [vmem] * members,
        out_specs=[vmem, vmem],
        compiler_params=SMALL,
        name="order",
    )(where, *received)


def on_device(down_in, up_in, w_qkv, w_out, norm_gain, down_docs, up_docs):
    where = jnp.stack([lax.axis_index(name) for name in ("pipe", "x", "core", "tensor")])
    sections = lax.axis_size("pipe")
    weights = gather_section(where, w_qkv, w_out, norm_gain)
    rope = rotary_tables()
    vmem = pl.BlockSpec(memory_space=pltpu.VMEM)
    values, allowed = pl.pallas_call(
        enter_kernel,
        out_shape=[
            jax.ShapeDtypeStruct((SEQ, D), BF16),
            jax.ShapeDtypeStruct((GROUP_HEADS * SEQ, SEQ), F32),
        ],
        in_specs=[pl.BlockSpec(memory_space=pltpu.SMEM)] + [vmem] * 4,
        out_specs=[vmem, vmem],
        compiler_params=SMALL,
        name="enter",
    )(where, down_in, up_in, down_docs, up_docs)
    held = jnp.zeros((SEQ, D), BF16)
    for step in range(sections - 1):
        held = run_section(step, False, where, values, allowed, held, rope, weights)
        values = lax.ppermute(held, "pipe", [(step, step + 1)])
    chunks = run_section(sections - 1, True, where, values, allowed, held, rope, weights)
    return exchange(chunks, where)


def solution(mesh):
    fine = Mesh(
        mesh.devices.reshape(X, ZH, 2, *mesh.devices.shape[1:]),
        ("x", "z_hi", "core", "pipe", "tensor"),
    )
    dp = ("x", "z_hi", "core")
    placed = (
        P(dp, None, None),
        P(dp, None, None),
        P(None, dp, "tensor"),
        P(None, "tensor", dp),
        P(None, dp),
        P(dp, None),
        P(dp, None),
    )
    return jax.shard_map(
        on_device,
        mesh=fine,
        in_specs=placed,
        out_specs=(P("pipe", dp, "tensor", None), P("pipe", dp, "tensor", None)),
        check_vma=False,
    )
```

```python
import functools

import jax
import jax.numpy as jnp
import numpy as np
from jax import lax
from jax.experimental import pallas as pl
from jax.experimental.pallas import tpu as pltpu
from jax.sharding import Mesh, PartitionSpec as P

HEAD_DIM = 64
SEQ = 32
D = 2048
EPSILON = 1e-05
THETA = 500000.0

GROUPS = 4
GROUP_HEADS = 4
QKV = 384
CTX = 256
X = 4
ZH = 4
ZL = 4
Z = ZH * ZL
HALF = SEQ // 2
ROWS = 256

F32, BF16 = jnp.float32, jnp.bfloat16

SMALL = pltpu.CompilerParams(vmem_limit_bytes=4 * 1024 * 1024)
MEDIUM = pltpu.CompilerParams(vmem_limit_bytes=20 * 1024 * 1024)


def rotary_tables():
    half = HEAD_DIM // 2
    lane = jnp.arange(4 * half)[None, :]
    frequency = THETA ** (-((lane % half).astype(F32) * 2.0 / HEAD_DIM))
    angles = jnp.arange(SEQ, dtype=F32)[:, None] * frequency
    cos, sin = jnp.cos(angles), jnp.sin(angles)
    return [
        cos,
        sin,
        jnp.where(lane < 2 * half, cos, 1.0),
        jnp.where(lane < half, -sin, 0.0),
        jnp.where((lane >= half) & (lane < 2 * half), sin, 0.0),
    ]


def attention(projected, rope, allowed, earlier):
    rows = projected[0].shape[0]
    lane = lax.broadcasted_iota(jnp.int32, (rows, 128), 1)
    lane2 = lax.broadcasted_iota(jnp.int32, (rows, 256), 1)
    head_of = (lane2 % 128) // 32
    zero = jnp.zeros((), BF16)
    cos, sin, kcos, ksin_a, ksin_b = rope
    queries, keys, values = [], [], []
    for part in projected:
        first, second = part[:, :128], part[:, 128:256]
        query = jnp.concatenate(
            [first * cos - second * sin, second * cos + first * sin], axis=-1
        ).astype(BF16)
        queries.append(
            jnp.concatenate([jnp.where(head_of == h, query, zero) for h in range(GROUP_HEADS)], axis=0)
        )
    for part in projected:
        kv = part[:, 256:]
        kv = kv * kcos + pltpu.roll(kv, 96, 1) * ksin_a + pltpu.roll(kv, 32, 1) * ksin_b
        key_a = jnp.where(lane < 32, kv, 0.0)
        key_a = key_a + pltpu.roll(key_a, 32, 1)
        key_a = key_a + pltpu.roll(key_a, 64, 1)
        key_b = jnp.where((lane >= 32) & (lane < 64), kv, 0.0)
        key_b = key_b + pltpu.roll(key_b, 32, 1)
        key_b = key_b + pltpu.roll(key_b, 64, 1)
        keys.append(jnp.concatenate([key_a, key_b], axis=-1).astype(BF16))
        values.append(kv.astype(BF16))
    all_keys, all_values = keys, values
    if earlier is not None:
        all_keys = [jnp.concatenate(pair, axis=0) for pair in zip(earlier[0], keys)]
        all_values = [jnp.concatenate(pair, axis=0) for pair in zip(earlier[1], values)]
    scores = [
        lax.dot_general(q, k, (((1,), (1,)), ((), ())), preferred_element_type=F32)
        for q, k in zip(queries, all_keys)
    ]
    scores = [jnp.where(allowed, s * HEAD_DIM ** (-0.5), -1e30) for s in scores]
    scores = [jnp.exp(s - jnp.max(s, axis=-1, keepdims=True)) for s in scores]
    weights = [(s * (1.0 / jnp.sum(s, axis=-1, keepdims=True))).astype(BF16) for s in scores]
    contexts = []
    for weight, value in zip(weights, all_values):
        mixed = jnp.dot(weight, value, preferred_element_type=F32)
        heads = [mixed[h * rows : (h + 1) * rows] for h in range(GROUP_HEADS)]
        context = jnp.concatenate(
            [
                jnp.where(lane < 64, pltpu.roll(heads[0], 64, 1), heads[1]),
                jnp.where(lane < 64, pltpu.roll(heads[2], 64, 1), heads[3]),
            ],
            axis=-1,
        )
        contexts.append(context.astype(BF16))
    return contexts, keys, values


def section_kernel(step, half, last, where, x_ref, allowed_ref, held_ref, *refs):
    rope, weights, refs = refs[:5], (refs[5:8], refs[8:11]), refs[11:]
    first = half * HALF
    if half == 0:
        out_ref, keys_ref, values_ref = refs
    elif last:
        keys_ref, values_ref, before_ref, *chunks, out_ref = refs
    else:
        keys_ref, values_ref, out_ref = refs
    out_rows = pl.ds(first if last and half else 0, HALF)

    def rows_of(i, zh, t, columns):
        part, start = ((0, 0), (1, ZH), (2, 0), (1, 0))[t]
        return jnp.concatenate(
            [weights[i][part][x, start + zh, :, columns] for x in range(X)], axis=0
        )

    @pl.when(where[0] != step)
    def _():
        out_ref[out_rows, :] = held_ref[...].astype(out_ref.dtype)

    @pl.when(where[0] == step)
    def _():
        places = [(i, zh) for i in range(2) for zh in range(ZH)]
        parts = [x_ref[:, pl.ds(j * ROWS, ROWS)] for j in range(2 * ZH)]
        squares = [jnp.sum(jnp.square(part.astype(F32)), axis=-1, keepdims=True) for part in parts]
        scale = lax.rsqrt(functools.reduce(jnp.add, squares) * (1.0 / D) + EPSILON)
        projected = []
        for t in range(GROUPS):
            terms = [
                jnp.dot(part, rows_of(i, zh, t, pl.ds(0, QKV)), preferred_element_type=F32)
                for part, (i, zh) in zip(parts, places)
            ]
            projected.append(functools.reduce(jnp.add, terms) * scale)
        allowed = allowed_ref[pl.ds(first, HALF), pl.ds(0, first + HALF)] > 0.5
        allowed = jnp.concatenate([allowed] * GROUP_HEADS, axis=0)
        earlier = None
        if half:
            earlier = [[ref[t] for t in range(GROUPS)] for ref in (keys_ref, values_ref)]
        contexts, keys, values = attention(
            projected, [part[pl.ds(first, HALF), :] for part in rope], allowed, earlier
        )
        if not half:
            for t in range(GROUPS):
                keys_ref[t] = keys[t]
                values_ref[t] = values[t]
        for j, (i, zh) in enumerate(places):
            terms = [
                jnp.dot(
                    contexts[t], rows_of(i, zh, t, pl.ds(QKV, CTX)), preferred_element_type=F32
                )
                for t in range(GROUPS)
            ]
            total = x_ref[:, pl.ds(j * ROWS, ROWS)].astype(F32) + functools.reduce(jnp.add, terms)
            out_ref[out_rows, pl.ds(j * ROWS, ROWS)] = total.astype(out_ref.dtype)

    if last and half:
        out_ref[pl.ds(0, HALF), :] = before_ref[...].astype(F32)
        rows = chunks[0].shape[0]
        for k, chunk_ref in enumerate(chunks):
            place = (where[3] + k) % (SEQ // rows)
            chunk_ref[...] = out_ref[pl.ds(pl.multiple_of(place * rows, rows), rows), :].astype(BF16)


def run_section(step, half, last, where, values, allowed, held, rope, weights, *more):
    vmem = pl.BlockSpec(memory_space=pltpu.VMEM)
    part = jax.ShapeDtypeStruct((HALF, D), BF16)
    split = bool(last and half)
    if half == 0:
        shapes = [
            part,
            jax.ShapeDtypeStruct((GROUPS, HALF, 256), BF16),
            jax.ShapeDtypeStruct((GROUPS, HALF, 128), BF16),
        ]
    else:
        shapes = [jax.ShapeDtypeStruct((SEQ // 4, D), BF16)] * 4 if split else [part]
    return pl.pallas_call(
        functools.partial(section_kernel, step, half, last),
        out_shape=shapes,
        in_specs=[pl.BlockSpec(memory_space=pltpu.SMEM)] + [vmem] * (14 + len(more)),
        out_specs=[vmem] * len(shapes),
        scratch_shapes=[pltpu.VMEM((SEQ, D), F32)] if split else [],
        input_output_aliases={} if split else {3: 0},
        compiler_params=MEDIUM,
        name="section",
    )(where, values, allowed, held, *rope, *weights, *more)


def shard_kernel(where, qkv_any, out_any, gain_any, shard_ref, qkv_ref, out_ref, gain_ref, done):
    copies = [
        pltpu.make_async_copy(qkv_any.at[where[0]], qkv_ref, done.at[0]),
        pltpu.make_async_copy(out_any.at[where[0]], out_ref, done.at[1]),
        pltpu.make_async_copy(gain_any, gain_ref, done.at[2]),
    ]
    for copy in copies:
        copy.start()
    for copy in copies:
        copy.wait()
    rows = qkv_ref.shape[0]
    section = lax.broadcasted_iota(jnp.int32, gain_ref.shape, 0)
    gain = jnp.where(section == where[0], gain_ref[...].astype(F32), 0.0)
    gain = jnp.sum(gain, axis=0, keepdims=True)
    row = lax.broadcasted_iota(jnp.int32, (rows, rows), 0)
    column = lax.broadcasted_iota(jnp.int32, (rows, rows), 1)
    gain = jnp.sum(jnp.where(row == column, gain, 0.0), axis=1, keepdims=True)
    qkv = qkv_ref[...].astype(F32) * gain
    one, two = qkv[:, :128], qkv[:, 128:256]
    lane = lax.broadcasted_iota(jnp.int32, (rows, 128), 1)

    def lanes(parts):
        result = parts[3]
        for i in (2, 1, 0):
            result = jnp.where(lane < 32 * (i + 1), parts[i], result)
        return result

    first = lanes([one, pltpu.roll(one, 96, 1), pltpu.roll(two, 64, 1), pltpu.roll(two, 32, 1)])
    second = lanes([pltpu.roll(one, 96, 1), pltpu.roll(one, 64, 1), pltpu.roll(two, 32, 1), two])
    for zh in range(shard_ref.shape[0]):
        shard_ref[zh, :, pl.ds(0, 128)] = first.astype(BF16)
        shard_ref[zh, :, pl.ds(128, 128)] = second.astype(BF16)
        shard_ref[zh, :, pl.ds(256, 128)] = qkv[:, 256:].astype(BF16)
        shard_ref[zh, :, pl.ds(QKV, CTX)] = out_ref[...]


def join_kernel(here_ref, after_ref, before_ref, half_ref, rest_ref, out_ref):
    half = half_ref.shape[0]
    for i in range(out_ref.shape[1]):
        middle = half_ref.at[i] if i < half else rest_ref.at[i - half]
        parts = [here_ref.at[i], after_ref.at[i], middle, before_ref.at[i]]
        for x, part in enumerate(parts):
            out_ref[x, i, :, pl.ds(0, QKV)] = part[:, pl.ds(0, QKV)]
        columns = jnp.concatenate([part[:, pl.ds(QKV, CTX)] for part in parts], axis=0)
        turned_columns = columns.astype(F32).T.astype(BF16)
        for x in range(X):
            out_ref[x, i, :, pl.ds(QKV, CTX)] = turned_columns[x * 64 : (x + 1) * 64]


def gather_section(where, w_qkv, w_out, norm_gain):
    rows = w_qkv.shape[1]
    vmem = pl.BlockSpec(memory_space=pltpu.VMEM)
    smem = pl.BlockSpec(memory_space=pltpu.SMEM)
    shards = pl.pallas_call(
        shard_kernel,
        out_shape=jax.ShapeDtypeStruct((ZH, rows, QKV + CTX), BF16),
        in_specs=[smem] + [pl.BlockSpec(memory_space=pl.ANY)] * 3,
        out_specs=vmem,
        scratch_shapes=[
            pltpu.VMEM((rows, QKV), BF16),
            pltpu.VMEM((rows, CTX), BF16),
            pltpu.VMEM(norm_gain.shape, BF16),
            pltpu.SemaphoreType.DMA((3,)),
        ],
        name="shard",
    )(where, w_qkv, w_out.transpose(0, 2, 1), norm_gain)

    one, other = [(x, (x + 1) % X) for x in range(X)], [(x, (x - 1) % X) for x in range(X)]

    def first_along_x(parts):
        return lax.ppermute(parts, "x", one), lax.ppermute(parts, "x", other)

    def rest_along_x(before, after):
        half = before.shape[0] // 2
        return lax.ppermute(before[:half], "x", one), lax.ppermute(after[half:], "x", other)

    def join(here, before, after, half, rest):
        return pl.pallas_call(
            join_kernel,
            out_shape=jax.ShapeDtypeStruct((X, *here.shape), BF16),
            in_specs=[vmem] * 5,
            out_specs=vmem,
            compiler_params=MEDIUM,
            name="join",
        )(here, after, before, half, rest)

    def along_z(parts, by):
        return lax.ppermute(parts, ("z_hi", "tensor"), [(z, (z + by) % Z) for z in range(Z)])

    here = lax.all_to_all(shards, "z_hi", 0, 0)
    half = ZH // 2
    ahead, behind = along_z(here, 1), along_z(here, -1)
    here_x = first_along_x(here)
    near, *here_x = lax.optimization_barrier((jnp.concatenate([ahead, behind]), *here_x))
    near_x = first_along_x(near)
    across = jnp.concatenate([along_z(ahead[:half], 1), along_z(behind[half:], -1)])
    here_rest = rest_along_x(*here_x)
    across, *here_rest = lax.optimization_barrier((across, *here_rest))
    across_x = first_along_x(across)
    near_rest = rest_along_x(*near_x)
    *across_x, near_0, near_1 = lax.optimization_barrier((*across_x, *near_rest))
    across_rest = rest_along_x(*across_x)
    own = [
        join(here, *here_x, *here_rest),
        join(near, *near_x, near_0, near_1),
        join(across, *across_x, *across_rest),
    ]
    return own + [lax.ppermute(part, "core", [(0, 1), (1, 0)]) for part in own]


def turned(values, by):
    result = values
    for count in range(1, X):
        result = jnp.where(by == count, pltpu.roll(values, 64 * count, 1), result)
    return result


def enter_kernel(
    where, down_ref, up_ref, down_docs_ref, up_docs_ref, first_ref, second_ref, allowed_ref
):
    member = where[3]
    x_ref = jnp.where(member < 2, down_ref[member % 2], up_ref[member % 2]).astype(F32)
    docs = [docs_ref[...] for docs_ref in (down_docs_ref, up_docs_ref)]
    docs = jnp.where(member < 2, docs[0], docs[1])
    docs = jnp.where(member % 2 == 0, docs[:1], docs[1:])
    row = lax.broadcasted_iota(jnp.int32, (SEQ, SEQ), 0)
    column = lax.broadcasted_iota(jnp.int32, (SEQ, SEQ), 1)
    own_docs = jnp.sum(jnp.where(row == column, docs, 0), axis=1, keepdims=True)
    allowed = jnp.where((row >= column) & (own_docs == docs), 1.0, 0.0)
    allowed_ref[...] = allowed
    lane = lax.broadcasted_iota(jnp.int32, (SEQ, 128), 1)
    for zh in range(ZH):
        tiles = [x_ref[:, x * 512 + zh * 128 : x * 512 + zh * 128 + 128] for x in range(X)]
        cores = []
        for core in range(2):
            pairs = [
                jnp.where(lane < 64, a, pltpu.roll(b, 64, 1))
                if core == 0
                else jnp.where(lane < 64, pltpu.roll(a, 64, 1), b)
                for a, b in (tiles[:2], tiles[2:])
            ]
            cores.append(turned(jnp.concatenate(pairs, axis=1), (X - where[1]) % X))
        for i in range(2):
            part = jnp.where(where[2] == i, cores[0], cores[1])
            columns = pl.ds((i * ZH + zh) * ROWS, ROWS)
            first_ref[:, columns] = part[:HALF].astype(BF16)
            second_ref[:, columns] = part[HALF:].astype(BF16)


def order_kernel(where, *refs):
    *received, down_ref, up_ref = refs
    rows = received[0].shape[0]
    values = jnp.concatenate([part[...] for part in received], axis=0).astype(F32)
    lane = lax.broadcasted_iota(jnp.int32, (values.shape[0], 128), 1)
    tiles = {}
    for zh in range(ZH):
        mine, other = (
            turned(values[:, (i * ZH + zh) * ROWS : (i * ZH + zh + 1) * ROWS], where[1])
            for i in range(2)
        )
        zero, one = jnp.where(where[2] == 0, mine, other), jnp.where(where[2] == 0, other, mine)
        for pair in range(2):
            a, b = (part[:, pair * 128 : (pair + 1) * 128] for part in (zero, one))
            tiles[2 * pair, zh] = jnp.where(lane < 64, a, pltpu.roll(b, 64, 1))
            tiles[2 * pair + 1, zh] = jnp.where(lane < 64, pltpu.roll(a, 64, 1), b)
    natural = jnp.concatenate(
        [tiles[x, zh] for x in range(X) for zh in range(ZH)], axis=1
    ).astype(BF16)
    for k in range(len(received)):
        source = (where[3] + len(received) - k) % len(received)
        part = natural[k * rows : (k + 1) * rows]

        @pl.when(source < 2)
        def _():
            down_ref[0, source] = part

        @pl.when(source >= 2)
        def _():
            up_ref[0, source - 2] = part


def exchange(chunks, where):
    planes, members = lax.axis_size("pipe"), lax.axis_size("tensor")
    rows = SEQ // members
    received = []
    for k, chunk in enumerate(chunks):
        pairs = [
            (y * members + t, (y if t < 2 else planes - 1 - y) * members + (t + k) % members)
            for y in range(planes)
            for t in range(members)
        ]
        received.append(lax.ppermute(chunk, ("pipe", "tensor"), pairs))
    vmem = pl.BlockSpec(memory_space=pltpu.VMEM)
    shape = jax.ShapeDtypeStruct((1, members // 2, rows, D), BF16)
    return pl.pallas_call(
        order_kernel,
        out_shape=[shape, shape],
        in_specs=[pl.BlockSpec(memory_space=pltpu.SMEM)] + [vmem] * members,
        out_specs=[vmem, vmem],
        compiler_params=SMALL,
        name="order",
    )(where, *received)


def on_device(down_in, up_in, w_qkv, w_out, norm_gain, down_docs, up_docs):
    where = jnp.stack([lax.axis_index(name) for name in ("pipe", "x", "core", "tensor")])
    sections = lax.axis_size("pipe")
    weights = gather_section(where, w_qkv, w_out, norm_gain)
    rope = rotary_tables()
    vmem = pl.BlockSpec(memory_space=pltpu.VMEM)
    part = jax.ShapeDtypeStruct((HALF, D), BF16)
    *values, allowed = pl.pallas_call(
        enter_kernel,
        out_shape=[part, part, jax.ShapeDtypeStruct((SEQ, SEQ), F32)],
        in_specs=[pl.BlockSpec(memory_space=pltpu.SMEM)] + [vmem] * 4,
        out_specs=[vmem] * 3,
        compiler_params=SMALL,
        name="enter",
    )(where, down_in, up_in, down_docs, up_docs)
    held = [jnp.zeros((HALF, D), BF16)] * 2
    for step in range(sections):
        last = step + 1 == sections

        def run(half, *more):
            return run_section(
                step, half, last, where, values[half], allowed, held[half], rope, weights, *more
            )

        def next_plane(part):
            return lax.ppermute(part, "pipe", [(step, step + 1)])

        one, *state = run(0)
        if last:
            return exchange(run(1, *state, one), where)
        (two,) = run(1, *state)
        held = [one, two]
        values = [next_plane(one), next_plane(two)]


def solution(mesh):
    fine = Mesh(
        mesh.devices.reshape(X, ZH, 2, *mesh.devices.shape[1:]),
        ("x", "z_hi", "core", "pipe", "tensor"),
    )
    dp = ("x", "z_hi", "core")
    placed = (
        P(dp, None, None),
        P(dp, None, None),
        P(None, dp, "tensor"),
        P(None, "tensor", dp),
        P(None, dp),
        P(dp, None),
        P(dp, None),
    )
    return jax.shard_map(
        on_device,
        mesh=fine,
        in_specs=placed,
        out_specs=(P("pipe", dp, "tensor", None), P("pipe", dp, "tensor", None)),
        check_vma=False,
    )
```

```python
import functools

import jax
import jax.numpy as jnp
import numpy as np
from jax import lax
from jax.experimental import pallas as pl
from jax.experimental.pallas import tpu as pltpu
from jax.sharding import Mesh, PartitionSpec as P

HEAD_DIM = 64
SEQ = 32
D = 2048
EPSILON = 1e-05
THETA = 500000.0

GROUPS = 4
GROUP_HEADS = 4
QKV = 384
CTX = 256
X = 4
ZH = 4
ZL = 4
Z = ZH * ZL
HALF = SEQ // 2
ROWS = 256

F32, BF16 = jnp.float32, jnp.bfloat16

SMALL = pltpu.CompilerParams(vmem_limit_bytes=4 * 1024 * 1024)
MEDIUM = pltpu.CompilerParams(vmem_limit_bytes=20 * 1024 * 1024)


def rotary_tables():
    half = HEAD_DIM // 2
    lane = jnp.arange(4 * half)[None, :]
    frequency = THETA ** (-((lane % half).astype(F32) * 2.0 / HEAD_DIM))
    angles = jnp.arange(SEQ, dtype=F32)[:, None] * frequency
    cos, sin = jnp.cos(angles), jnp.sin(angles)
    return [
        cos,
        sin,
        jnp.where(lane < 2 * half, cos, 1.0),
        jnp.where(lane < half, -sin, 0.0),
        jnp.where((lane >= half) & (lane < 2 * half), sin, 0.0),
    ]


def attention(projected, rope, allowed, earlier):
    rows = projected[0].shape[0]
    lane = lax.broadcasted_iota(jnp.int32, (rows, 128), 1)
    lane2 = lax.broadcasted_iota(jnp.int32, (rows, 256), 1)
    head_of = (lane2 % 128) // 32
    zero = jnp.zeros((), BF16)
    cos, sin, kcos, ksin_a, ksin_b = rope
    queries, keys, values = [], [], []
    for part in projected:
        first, second = part[:, :128], part[:, 128:256]
        query = jnp.concatenate(
            [first * cos - second * sin, second * cos + first * sin], axis=-1
        ).astype(BF16)
        queries.append(
            jnp.concatenate([jnp.where(head_of == h, query, zero) for h in range(GROUP_HEADS)], axis=0)
        )
    for part in projected:
        kv = part[:, 256:]
        kv = kv * kcos + pltpu.roll(kv, 96, 1) * ksin_a + pltpu.roll(kv, 32, 1) * ksin_b
        key_a = jnp.where(lane < 32, kv, 0.0)
        key_a = key_a + pltpu.roll(key_a, 32, 1)
        key_a = key_a + pltpu.roll(key_a, 64, 1)
        key_b = jnp.where((lane >= 32) & (lane < 64), kv, 0.0)
        key_b = key_b + pltpu.roll(key_b, 32, 1)
        key_b = key_b + pltpu.roll(key_b, 64, 1)
        keys.append(jnp.concatenate([key_a, key_b], axis=-1).astype(BF16))
        values.append(kv.astype(BF16))
    all_keys, all_values = keys, values
    if earlier is not None:
        all_keys = [jnp.concatenate(pair, axis=0) for pair in zip(earlier[0], keys)]
        all_values = [jnp.concatenate(pair, axis=0) for pair in zip(earlier[1], values)]
    scores = [
        lax.dot_general(q, k, (((1,), (1,)), ((), ())), preferred_element_type=F32)
        for q, k in zip(queries, all_keys)
    ]
    scores = [jnp.where(allowed, s * HEAD_DIM ** (-0.5), -1e30) for s in scores]
    scores = [jnp.exp(s - jnp.max(s, axis=-1, keepdims=True)) for s in scores]
    weights = [(s * (1.0 / jnp.sum(s, axis=-1, keepdims=True))).astype(BF16) for s in scores]
    contexts = []
    for weight, value in zip(weights, all_values):
        mixed = jnp.dot(weight, value, preferred_element_type=F32)
        heads = [mixed[h * rows : (h + 1) * rows] for h in range(GROUP_HEADS)]
        context = jnp.concatenate(
            [
                jnp.where(lane < 64, pltpu.roll(heads[0], 64, 1), heads[1]),
                jnp.where(lane < 64, pltpu.roll(heads[2], 64, 1), heads[3]),
            ],
            axis=-1,
        )
        contexts.append(context.astype(BF16))
    return contexts, keys, values


def section_kernel(step, half, last, where, x_ref, allowed_ref, held_ref, *refs):
    rope, weights, refs = refs[:5], (refs[5:8], refs[8:11]), refs[11:]
    first = half * HALF
    if half == 0:
        out_ref, keys_ref, values_ref = refs
    elif last:
        keys_ref, values_ref, before_ref, chunks_ref, out_ref = refs
    else:
        keys_ref, values_ref, out_ref = refs
    out_rows = pl.ds(first if last and half else 0, HALF)

    def rows_of(i, zh, t, columns):
        part, start = ((0, 0), (1, ZH), (2, 0), (1, 0))[t]
        return jnp.concatenate(
            [weights[i][part][x, start + zh, :, columns] for x in range(X)], axis=0
        )

    @pl.when(where[0] != step)
    def _():
        out_ref[out_rows, :] = held_ref[...].astype(out_ref.dtype)

    @pl.when(where[0] == step)
    def _():
        places = [(i, zh) for i in range(2) for zh in range(ZH)]
        parts = [x_ref[:, pl.ds(j * ROWS, ROWS)] for j in range(2 * ZH)]
        squares = [jnp.sum(jnp.square(part.astype(F32)), axis=-1, keepdims=True) for part in parts]
        scale = lax.rsqrt(functools.reduce(jnp.add, squares) * (1.0 / D) + EPSILON)
        projected = []
        for t in range(GROUPS):
            terms = [
                jnp.dot(part, rows_of(i, zh, t, pl.ds(0, QKV)), preferred_element_type=F32)
                for part, (i, zh) in zip(parts, places)
            ]
            projected.append(functools.reduce(jnp.add, terms) * scale)
        allowed = allowed_ref[pl.ds(first, HALF), pl.ds(0, first + HALF)] > 0.5
        allowed = jnp.concatenate([allowed] * GROUP_HEADS, axis=0)
        earlier = None
        if half:
            earlier = [[ref[t] for t in range(GROUPS)] for ref in (keys_ref, values_ref)]
        contexts, keys, values = attention(
            projected, [part[pl.ds(first, HALF), :] for part in rope], allowed, earlier
        )
        if not half:
            for t in range(GROUPS):
                keys_ref[t] = keys[t]
                values_ref[t] = values[t]
        for j, (i, zh) in enumerate(places):
            terms = [
                jnp.dot(
                    contexts[t], rows_of(i, zh, t, pl.ds(QKV, CTX)), preferred_element_type=F32
                )
                for t in range(GROUPS)
            ]
            total = x_ref[:, pl.ds(j * ROWS, ROWS)].astype(F32) + functools.reduce(jnp.add, terms)
            out_ref[out_rows, pl.ds(j * ROWS, ROWS)] = total.astype(out_ref.dtype)

    if last and half:
        out_ref[pl.ds(0, HALF), :] = before_ref[...].astype(F32)
        for k in range(chunks_ref.shape[0]):
            place = k % GROUPS * (SEQ // GROUPS)
            chunks_ref[k] = out_ref[pl.ds(place, SEQ // GROUPS), :].astype(BF16)


def run_section(step, half, last, where, values, allowed, held, rope, weights, *more):
    vmem = pl.BlockSpec(memory_space=pltpu.VMEM)
    part = jax.ShapeDtypeStruct((HALF, D), BF16)
    split = bool(last and half)
    if half == 0:
        shapes = [
            part,
            jax.ShapeDtypeStruct((GROUPS, HALF, 256), BF16),
            jax.ShapeDtypeStruct((GROUPS, HALF, 128), BF16),
        ]
    else:
        shapes = [jax.ShapeDtypeStruct((8, SEQ // 4, D), BF16) if split else part]
    return pl.pallas_call(
        functools.partial(section_kernel, step, half, last),
        out_shape=shapes,
        in_specs=[pl.BlockSpec(memory_space=pltpu.SMEM)] + [vmem] * (14 + len(more)),
        out_specs=[vmem] * len(shapes),
        scratch_shapes=[pltpu.VMEM((SEQ, D), F32)] if split else [],
        input_output_aliases={} if split else {3: 0},
        compiler_params=MEDIUM,
        name="section",
    )(where, values, allowed, held, *rope, *weights, *more)


def shard_kernel(where, qkv_any, out_any, gain_any, shard_ref, qkv_ref, out_ref, gain_ref, done):
    copies = [
        pltpu.make_async_copy(qkv_any.at[where[0]], qkv_ref, done.at[0]),
        pltpu.make_async_copy(out_any.at[where[0]], out_ref, done.at[1]),
        pltpu.make_async_copy(gain_any, gain_ref, done.at[2]),
    ]
    for copy in copies:
        copy.start()
    for copy in copies:
        copy.wait()
    rows = qkv_ref.shape[0]
    section = lax.broadcasted_iota(jnp.int32, gain_ref.shape, 0)
    gain = jnp.where(section == where[0], gain_ref[...].astype(F32), 0.0)
    gain = jnp.sum(gain, axis=0, keepdims=True)
    row = lax.broadcasted_iota(jnp.int32, (rows, rows), 0)
    column = lax.broadcasted_iota(jnp.int32, (rows, rows), 1)
    gain = jnp.sum(jnp.where(row == column, gain, 0.0), axis=1, keepdims=True)
    qkv = qkv_ref[...].astype(F32) * gain
    one, two = qkv[:, :128], qkv[:, 128:256]
    lane = lax.broadcasted_iota(jnp.int32, (rows, 128), 1)

    def lanes(parts):
        result = parts[3]
        for i in (2, 1, 0):
            result = jnp.where(lane < 32 * (i + 1), parts[i], result)
        return result

    first = lanes([one, pltpu.roll(one, 96, 1), pltpu.roll(two, 64, 1), pltpu.roll(two, 32, 1)])
    second = lanes([pltpu.roll(one, 96, 1), pltpu.roll(one, 64, 1), pltpu.roll(two, 32, 1), two])
    for zh in range(shard_ref.shape[0]):
        shard_ref[zh, :, pl.ds(0, 128)] = first.astype(BF16)
        shard_ref[zh, :, pl.ds(128, 128)] = second.astype(BF16)
        shard_ref[zh, :, pl.ds(256, 128)] = qkv[:, 256:].astype(BF16)
        shard_ref[zh, :, pl.ds(QKV, CTX)] = out_ref[...]


def join_kernel(here_ref, after_ref, before_ref, half_ref, rest_ref, out_ref):
    half = half_ref.shape[0]
    for i in range(out_ref.shape[1]):
        middle = half_ref.at[i] if i < half else rest_ref.at[i - half]
        parts = [here_ref.at[i], after_ref.at[i], middle, before_ref.at[i]]
        for x, part in enumerate(parts):
            out_ref[x, i, :, pl.ds(0, QKV)] = part[:, pl.ds(0, QKV)]
        columns = jnp.concatenate([part[:, pl.ds(QKV, CTX)] for part in parts], axis=0)
        turned_columns = columns.astype(F32).T.astype(BF16)
        for x in range(X):
            out_ref[x, i, :, pl.ds(QKV, CTX)] = turned_columns[x * 64 : (x + 1) * 64]


def gather_section(where, w_qkv, w_out, norm_gain):
    rows = w_qkv.shape[1]
    vmem = pl.BlockSpec(memory_space=pltpu.VMEM)
    smem = pl.BlockSpec(memory_space=pltpu.SMEM)
    shards = pl.pallas_call(
        shard_kernel,
        out_shape=jax.ShapeDtypeStruct((ZH, rows, QKV + CTX), BF16),
        in_specs=[smem] + [pl.BlockSpec(memory_space=pl.ANY)] * 3,
        out_specs=vmem,
        scratch_shapes=[
            pltpu.VMEM((rows, QKV), BF16),
            pltpu.VMEM((rows, CTX), BF16),
            pltpu.VMEM(norm_gain.shape, BF16),
            pltpu.SemaphoreType.DMA((3,)),
        ],
        name="shard",
    )(where, w_qkv, w_out.transpose(0, 2, 1), norm_gain)

    one, other = [(x, (x + 1) % X) for x in range(X)], [(x, (x - 1) % X) for x in range(X)]

    def first_along_x(parts):
        return lax.ppermute(parts, "x", one), lax.ppermute(parts, "x", other)

    def rest_along_x(before, after):
        half = before.shape[0] // 2
        return lax.ppermute(before[:half], "x", one), lax.ppermute(after[half:], "x", other)

    def join(here, before, after, half, rest):
        return pl.pallas_call(
            join_kernel,
            out_shape=jax.ShapeDtypeStruct((X, *here.shape), BF16),
            in_specs=[vmem] * 5,
            out_specs=vmem,
            compiler_params=MEDIUM,
            name="join",
        )(here, after, before, half, rest)

    def along_z(parts, by):
        return lax.ppermute(parts, ("z_hi", "tensor"), [(z, (z + by) % Z) for z in range(Z)])

    here = lax.all_to_all(shards, "z_hi", 0, 0)
    half = ZH // 2
    ahead, behind = along_z(here, 1), along_z(here, -1)
    here_x = first_along_x(here)
    near, *here_x = lax.optimization_barrier((jnp.concatenate([ahead, behind]), *here_x))
    near_x = first_along_x(near)
    across = jnp.concatenate([along_z(ahead[:half], 1), along_z(behind[half:], -1)])
    here_rest = rest_along_x(*here_x)
    across, *here_rest = lax.optimization_barrier((across, *here_rest))
    across_x = first_along_x(across)
    near_rest = rest_along_x(*near_x)
    *across_x, near_0, near_1 = lax.optimization_barrier((*across_x, *near_rest))
    across_rest = rest_along_x(*across_x)
    own = [
        join(here, *here_x, *here_rest),
        join(near, *near_x, near_0, near_1),
        join(across, *across_x, *across_rest),
    ]
    return own + [lax.ppermute(part, "core", [(0, 1), (1, 0)]) for part in own]


def turned(values, by):
    result = values
    for count in range(1, X):
        result = jnp.where(by == count, pltpu.roll(values, 64 * count, 1), result)
    return result


def enter_kernel(
    where, down_ref, up_ref, down_docs_ref, up_docs_ref, first_ref, second_ref, allowed_ref
):
    member = where[3]
    x_ref = jnp.where(member < 2, down_ref[member % 2], up_ref[member % 2]).astype(F32)
    docs = [docs_ref[...] for docs_ref in (down_docs_ref, up_docs_ref)]
    docs = jnp.where(member < 2, docs[0], docs[1])
    docs = jnp.where(member % 2 == 0, docs[:1], docs[1:])
    row = lax.broadcasted_iota(jnp.int32, (SEQ, SEQ), 0)
    column = lax.broadcasted_iota(jnp.int32, (SEQ, SEQ), 1)
    own_docs = jnp.sum(jnp.where(row == column, docs, 0), axis=1, keepdims=True)
    allowed = jnp.where((row >= column) & (own_docs == docs), 1.0, 0.0)
    allowed_ref[...] = allowed
    lane = lax.broadcasted_iota(jnp.int32, (SEQ, 128), 1)
    for zh in range(ZH):
        tiles = [x_ref[:, x * 512 + zh * 128 : x * 512 + zh * 128 + 128] for x in range(X)]
        cores = []
        for core in range(2):
            pairs = [
                jnp.where(lane < 64, a, pltpu.roll(b, 64, 1))
                if core == 0
                else jnp.where(lane < 64, pltpu.roll(a, 64, 1), b)
                for a, b in (tiles[:2], tiles[2:])
            ]
            cores.append(turned(jnp.concatenate(pairs, axis=1), (X - where[1]) % X))
        for i in range(2):
            part = jnp.where(where[2] == i, cores[0], cores[1])
            columns = pl.ds((i * ZH + zh) * ROWS, ROWS)
            first_ref[:, columns] = part[:HALF].astype(BF16)
            second_ref[:, columns] = part[HALF:].astype(BF16)


def order_kernel(where, received_ref, down_ref, up_ref):
    plane = where[0] // 4
    rows = received_ref.shape[1]
    parts = [received_ref[(plane if t < 2 else 1 - plane) * 4 + t] for t in range(4)]
    values = jnp.concatenate([part.astype(F32) for part in parts], axis=0)
    lane = lax.broadcasted_iota(jnp.int32, (values.shape[0], 128), 1)
    for zh in range(ZH):
        mine, other = (
            turned(values[:, (i * ZH + zh) * ROWS : (i * ZH + zh + 1) * ROWS], where[1])
            for i in range(2)
        )
        zero, one = jnp.where(where[2] == 0, mine, other), jnp.where(where[2] == 0, other, mine)
        for pair in range(2):
            a, b = (part[:, pair * 128 : (pair + 1) * 128] for part in (zero, one))
            even = jnp.where(lane < 64, a, pltpu.roll(b, 64, 1)).astype(BF16)
            odd = jnp.where(lane < 64, pltpu.roll(a, 64, 1), b).astype(BF16)
            for x, tile in ((2 * pair, even), (2 * pair + 1, odd)):
                columns = pl.ds(x * 512 + zh * 128, 128)
                for t in range(4):
                    out_ref = down_ref if t < 2 else up_ref
                    out_ref[0, t % 2, :, columns] = tile[t * rows : (t + 1) * rows]


def exchange(chunks, where):
    planes, members = lax.axis_size("pipe"), lax.axis_size("tensor")
    rows = SEQ // members
    groups = [
        [plane * members + t for plane in (y, planes - 1 - y) for t in range(members)]
        for y in range(planes // 2)
    ]
    received = lax.all_to_all(chunks, ("pipe", "tensor"), 0, 0, axis_index_groups=groups)
    vmem = pl.BlockSpec(memory_space=pltpu.VMEM)
    shape = jax.ShapeDtypeStruct((1, members // 2, rows, D), BF16)
    return pl.pallas_call(
        order_kernel,
        out_shape=[shape, shape],
        in_specs=[pl.BlockSpec(memory_space=pltpu.SMEM), vmem],
        out_specs=[vmem, vmem],
        compiler_params=SMALL,
        name="order",
    )(where, received)


def on_device(down_in, up_in, w_qkv, w_out, norm_gain, down_docs, up_docs):
    where = jnp.stack([lax.axis_index(name) for name in ("pipe", "x", "core", "tensor")])
    sections = lax.axis_size("pipe")
    weights = gather_section(where, w_qkv, w_out, norm_gain)
    rope = rotary_tables()
    vmem = pl.BlockSpec(memory_space=pltpu.VMEM)
    part = jax.ShapeDtypeStruct((HALF, D), BF16)
    *values, allowed = pl.pallas_call(
        enter_kernel,
        out_shape=[part, part, jax.ShapeDtypeStruct((SEQ, SEQ), F32)],
        in_specs=[pl.BlockSpec(memory_space=pltpu.SMEM)] + [vmem] * 4,
        out_specs=[vmem] * 3,
        compiler_params=SMALL,
        name="enter",
    )(where, down_in, up_in, down_docs, up_docs)
    held = [jnp.zeros((HALF, D), BF16)] * 2
    for step in range(sections):
        last = step + 1 == sections

        def run(half, *more):
            return run_section(
                step, half, last, where, values[half], allowed, held[half], rope, weights, *more
            )

        def next_plane(part):
            return lax.ppermute(part, "pipe", [(step, step + 1)])

        one, *state = run(0)
        if last:
            return exchange(run(1, *state, one)[0], where)
        (two,) = run(1, *state)
        held = [one, two]
        values = [next_plane(one), next_plane(two)]


def solution(mesh):
    fine = Mesh(
        mesh.devices.reshape(X, ZH, 2, *mesh.devices.shape[1:]),
        ("x", "z_hi", "core", "pipe", "tensor"),
    )
    dp = ("x", "z_hi", "core")
    placed = (
        P(dp, None, None),
        P(dp, None, None),
        P(None, dp, "tensor"),
        P(None, "tensor", dp),
        P(None, dp),
        P(dp, None),
        P(dp, None),
    )
    return jax.shard_map(
        on_device,
        mesh=fine,
        in_specs=placed,
        out_specs=(P("pipe", dp, "tensor", None), P("pipe", dp, "tensor", None)),
        check_vma=False,
    )
```

```python
import functools

import jax
import jax.numpy as jnp
import numpy as np
from jax import lax
from jax.experimental import pallas as pl
from jax.experimental.pallas import tpu as pltpu
from jax.sharding import Mesh, PartitionSpec as P

HEAD_DIM = 64
SEQ = 32
D = 2048
EPSILON = 1e-05
THETA = 500000.0

GROUPS = 4
GROUP_HEADS = 4
QKV = 384
CTX = 256
X = 4
ZH = 4
ZL = 4
Z = ZH * ZL
HALF = SEQ // 2
ROWS = 256

F32, BF16 = jnp.float32, jnp.bfloat16

SMALL = pltpu.CompilerParams(vmem_limit_bytes=4 * 1024 * 1024)
MEDIUM = pltpu.CompilerParams(vmem_limit_bytes=20 * 1024 * 1024)


def rotary_tables():
    half = HEAD_DIM // 2
    lane = jnp.arange(4 * half)[None, :]
    frequency = THETA ** (-((lane % half).astype(F32) * 2.0 / HEAD_DIM))
    angles = jnp.arange(SEQ, dtype=F32)[:, None] * frequency
    cos, sin = jnp.cos(angles), jnp.sin(angles)
    return [
        cos,
        sin,
        jnp.where(lane < 2 * half, cos, 1.0),
        jnp.where(lane < half, -sin, 0.0),
        jnp.where((lane >= half) & (lane < 2 * half), sin, 0.0),
    ]


def attention(projected, rope, allowed, earlier):
    rows = projected[0].shape[0]
    lane = lax.broadcasted_iota(jnp.int32, (rows, 128), 1)
    lane2 = lax.broadcasted_iota(jnp.int32, (rows, 256), 1)
    head_of = (lane2 % 128) // 32
    zero = jnp.zeros((), BF16)
    cos, sin, kcos, ksin_a, ksin_b = rope
    queries, keys, values = [], [], []
    for part in projected:
        first, second = part[:, :128], part[:, 128:256]
        query = jnp.concatenate(
            [first * cos - second * sin, second * cos + first * sin], axis=-1
        ).astype(BF16)
        queries.append(
            jnp.concatenate([jnp.where(head_of == h, query, zero) for h in range(GROUP_HEADS)], axis=0)
        )
    for part in projected:
        kv = part[:, 256:]
        kv = kv * kcos + pltpu.roll(kv, 96, 1) * ksin_a + pltpu.roll(kv, 32, 1) * ksin_b
        key_a = jnp.where(lane < 32, kv, 0.0)
        key_a = key_a + pltpu.roll(key_a, 32, 1)
        key_a = key_a + pltpu.roll(key_a, 64, 1)
        key_b = jnp.where((lane >= 32) & (lane < 64), kv, 0.0)
        key_b = key_b + pltpu.roll(key_b, 32, 1)
        key_b = key_b + pltpu.roll(key_b, 64, 1)
        keys.append(jnp.concatenate([key_a, key_b], axis=-1).astype(BF16))
        values.append(kv.astype(BF16))
    all_keys, all_values = keys, values
    if earlier is not None:
        all_keys = [jnp.concatenate(pair, axis=0) for pair in zip(earlier[0], keys)]
        all_values = [jnp.concatenate(pair, axis=0) for pair in zip(earlier[1], values)]
    scores = [
        lax.dot_general(q, k, (((1,), (1,)), ((), ())), preferred_element_type=F32)
        for q, k in zip(queries, all_keys)
    ]
    scores = [jnp.where(allowed, s * HEAD_DIM ** (-0.5), -1e30) for s in scores]
    scores = [jnp.exp(s - jnp.max(s, axis=-1, keepdims=True)) for s in scores]
    weights = [(s * (1.0 / jnp.sum(s, axis=-1, keepdims=True))).astype(BF16) for s in scores]
    contexts = []
    for weight, value in zip(weights, all_values):
        mixed = jnp.dot(weight, value, preferred_element_type=F32)
        heads = [mixed[h * rows : (h + 1) * rows] for h in range(GROUP_HEADS)]
        context = jnp.concatenate(
            [
                jnp.where(lane < 64, pltpu.roll(heads[0], 64, 1), heads[1]),
                jnp.where(lane < 64, pltpu.roll(heads[2], 64, 1), heads[3]),
            ],
            axis=-1,
        )
        contexts.append(context.astype(BF16))
    return contexts, keys, values


def section_kernel(step, half, last, where, x_ref, allowed_ref, held_ref, *refs):
    rope, weights, refs = refs[:5], (refs[5:7], refs[7:9]), refs[9:]
    first = half * HALF
    if half == 0:
        out_ref, keys_ref, values_ref = refs
    elif last:
        keys_ref, values_ref, before_ref, chunks_ref, out_ref = refs
    else:
        keys_ref, values_ref, out_ref = refs
    out_rows = pl.ds(first if last and half else 0, HALF)

    def rows_of(i, zh, t, columns):
        part, start = ((0, 0), (0, 2 * ZH), (1, 0), (0, ZH))[t]
        return jnp.concatenate(
            [weights[i][part][x, start + zh, :, columns] for x in range(X)], axis=0
        )

    @pl.when(where[0] != step)
    def _():
        out_ref[out_rows, :] = held_ref[...].astype(out_ref.dtype)

    @pl.when(where[0] == step)
    def _():
        places = [(i, zh) for i in range(2) for zh in range(ZH)]
        parts = [x_ref[:, pl.ds(j * ROWS, ROWS)] for j in range(2 * ZH)]
        squares = [jnp.sum(jnp.square(part.astype(F32)), axis=-1, keepdims=True) for part in parts]
        scale = lax.rsqrt(functools.reduce(jnp.add, squares) * (1.0 / D) + EPSILON)
        projected = []
        for t in range(GROUPS):
            terms = [
                jnp.dot(part, rows_of(i, zh, t, pl.ds(0, QKV)), preferred_element_type=F32)
                for part, (i, zh) in zip(parts, places)
            ]
            projected.append(functools.reduce(jnp.add, terms) * scale)
        allowed = allowed_ref[pl.ds(first, HALF), pl.ds(0, first + HALF)] > 0.5
        allowed = jnp.concatenate([allowed] * GROUP_HEADS, axis=0)
        earlier = None
        if half:
            earlier = [[ref[t] for t in range(GROUPS)] for ref in (keys_ref, values_ref)]
        contexts, keys, values = attention(
            projected, [part[pl.ds(first, HALF), :] for part in rope], allowed, earlier
        )
        if not half:
            for t in range(GROUPS):
                keys_ref[t] = keys[t]
                values_ref[t] = values[t]
        for j, (i, zh) in enumerate(places):
            terms = [
                jnp.dot(
                    contexts[t], rows_of(i, zh, t, pl.ds(QKV, CTX)), preferred_element_type=F32
                )
                for t in range(GROUPS)
            ]
            total = x_ref[:, pl.ds(j * ROWS, ROWS)].astype(F32) + functools.reduce(jnp.add, terms)
            out_ref[out_rows, pl.ds(j * ROWS, ROWS)] = total.astype(out_ref.dtype)

    if last and half:
        out_ref[pl.ds(0, HALF), :] = before_ref[...].astype(F32)
        for k in range(chunks_ref.shape[0]):
            place = k % GROUPS * (SEQ // GROUPS)
            chunks_ref[k] = out_ref[pl.ds(place, SEQ // GROUPS), :].astype(BF16)


def run_section(step, half, last, where, values, allowed, held, rope, weights, *more):
    vmem = pl.BlockSpec(memory_space=pltpu.VMEM)
    part = jax.ShapeDtypeStruct((HALF, D), BF16)
    split = bool(last and half)
    if half == 0:
        shapes = [
            part,
            jax.ShapeDtypeStruct((GROUPS, HALF, 256), BF16),
            jax.ShapeDtypeStruct((GROUPS, HALF, 128), BF16),
        ]
    else:
        shapes = [jax.ShapeDtypeStruct((8, SEQ // 4, D), BF16) if split else part]
    return pl.pallas_call(
        functools.partial(section_kernel, step, half, last),
        out_shape=shapes,
        in_specs=[pl.BlockSpec(memory_space=pltpu.SMEM)] + [vmem] * (12 + len(more)),
        out_specs=[vmem] * len(shapes),
        scratch_shapes=[pltpu.VMEM((SEQ, D), F32)] if split else [],
        input_output_aliases={} if split else {3: 0},
        compiler_params=MEDIUM,
        name="section",
    )(where, values, allowed, held, *rope, *weights, *more)


def shard_kernel(where, qkv_any, out_any, gain_any, shard_ref, qkv_ref, out_ref, gain_ref, done):
    copies = [
        pltpu.make_async_copy(qkv_any.at[where[0]], qkv_ref, done.at[0]),
        pltpu.make_async_copy(out_any.at[where[0]], out_ref, done.at[1]),
        pltpu.make_async_copy(gain_any, gain_ref, done.at[2]),
    ]
    for copy in copies:
        copy.start()
    for copy in copies:
        copy.wait()
    rows = qkv_ref.shape[0]
    section = lax.broadcasted_iota(jnp.int32, gain_ref.shape, 0)
    gain = jnp.where(section == where[0], gain_ref[...].astype(F32), 0.0)
    gain = jnp.sum(gain, axis=0, keepdims=True)
    row = lax.broadcasted_iota(jnp.int32, (rows, rows), 0)
    column = lax.broadcasted_iota(jnp.int32, (rows, rows), 1)
    gain = jnp.sum(jnp.where(row == column, gain, 0.0), axis=1, keepdims=True)
    qkv = qkv_ref[...].astype(F32) * gain
    one, two = qkv[:, :128], qkv[:, 128:256]
    lane = lax.broadcasted_iota(jnp.int32, (rows, 128), 1)

    def lanes(parts):
        result = parts[3]
        for i in (2, 1, 0):
            result = jnp.where(lane < 32 * (i + 1), parts[i], result)
        return result

    first = lanes([one, pltpu.roll(one, 96, 1), pltpu.roll(two, 64, 1), pltpu.roll(two, 32, 1)])
    second = lanes([pltpu.roll(one, 96, 1), pltpu.roll(one, 64, 1), pltpu.roll(two, 32, 1), two])
    for zh in range(shard_ref.shape[0]):
        shard_ref[zh, :, pl.ds(0, 128)] = first.astype(BF16)
        shard_ref[zh, :, pl.ds(128, 128)] = second.astype(BF16)
        shard_ref[zh, :, pl.ds(256, 128)] = qkv[:, 256:].astype(BF16)
        shard_ref[zh, :, pl.ds(QKV, CTX)] = out_ref[...]


def join_kernel(here_ref, after_ref, before_ref, half_ref, rest_ref, out_ref):
    half = half_ref.shape[0]
    for i in range(out_ref.shape[1]):
        middle = half_ref.at[i] if i < half else rest_ref.at[i - half]
        parts = [here_ref.at[i], after_ref.at[i], middle, before_ref.at[i]]
        for x, part in enumerate(parts):
            out_ref[x, i, :, pl.ds(0, QKV)] = part[:, pl.ds(0, QKV)]
        columns = jnp.concatenate([part[:, pl.ds(QKV, CTX)] for part in parts], axis=0)
        turned_columns = columns.astype(F32).T.astype(BF16)
        for x in range(X):
            out_ref[x, i, :, pl.ds(QKV, CTX)] = turned_columns[x * 64 : (x + 1) * 64]


def gather_section(where, w_qkv, w_out, norm_gain):
    rows = w_qkv.shape[1]
    vmem = pl.BlockSpec(memory_space=pltpu.VMEM)
    smem = pl.BlockSpec(memory_space=pltpu.SMEM)
    shards = pl.pallas_call(
        shard_kernel,
        out_shape=jax.ShapeDtypeStruct((ZH, rows, QKV + CTX), BF16),
        in_specs=[smem] + [pl.BlockSpec(memory_space=pl.ANY)] * 3,
        out_specs=vmem,
        scratch_shapes=[
            pltpu.VMEM((rows, QKV), BF16),
            pltpu.VMEM((rows, CTX), BF16),
            pltpu.VMEM(norm_gain.shape, BF16),
            pltpu.SemaphoreType.DMA((3,)),
        ],
        name="shard",
    )(where, w_qkv, w_out.transpose(0, 2, 1), norm_gain)

    one, other = [(x, (x + 1) % X) for x in range(X)], [(x, (x - 1) % X) for x in range(X)]

    def first_along_x(parts):
        return lax.ppermute(parts, "x", one), lax.ppermute(parts, "x", other)

    def rest_along_x(before, after):
        half = before.shape[0] // 2
        return lax.ppermute(before[:half], "x", one), lax.ppermute(after[half:], "x", other)

    def join(here, before, after, half, rest):
        return pl.pallas_call(
            join_kernel,
            out_shape=jax.ShapeDtypeStruct((X, *here.shape), BF16),
            in_specs=[vmem] * 5,
            out_specs=vmem,
            compiler_params=MEDIUM,
            name="join",
        )(here, after, before, half, rest)

    def along_z(parts, by):
        return lax.ppermute(parts, ("z_hi", "tensor"), [(z, (z + by) % Z) for z in range(Z)])

    here = lax.all_to_all(shards, "z_hi", 0, 0)
    half = ZH // 2
    ahead, behind = along_z(here, 1), along_z(here, -1)
    near = jnp.concatenate([here, ahead, behind])
    near_x = first_along_x(near)
    across = jnp.concatenate([along_z(ahead[:half], 1), along_z(behind[half:], -1)])
    across_x = first_along_x(across)
    rest = rest_along_x(*near_x) + rest_along_x(*across_x)
    rest = lax.optimization_barrier(rest)
    own = [join(near, *near_x, *rest[:2]), join(across, *across_x, *rest[2:])]
    return own + [lax.ppermute(part, "core", [(0, 1), (1, 0)]) for part in own]


def turned(values, by):
    result = values
    for count in range(1, X):
        result = jnp.where(by == count, pltpu.roll(values, 64 * count, 1), result)
    return result


def enter_kernel(
    where, down_ref, up_ref, down_docs_ref, up_docs_ref, first_ref, second_ref, allowed_ref
):
    member = where[3]
    x_ref = jnp.where(member < 2, down_ref[member % 2], up_ref[member % 2]).astype(F32)
    docs = [docs_ref[...] for docs_ref in (down_docs_ref, up_docs_ref)]
    docs = jnp.where(member < 2, docs[0], docs[1])
    docs = jnp.where(member % 2 == 0, docs[:1], docs[1:])
    row = lax.broadcasted_iota(jnp.int32, (SEQ, SEQ), 0)
    column = lax.broadcasted_iota(jnp.int32, (SEQ, SEQ), 1)
    own_docs = jnp.sum(jnp.where(row == column, docs, 0), axis=1, keepdims=True)
    allowed = jnp.where((row >= column) & (own_docs == docs), 1.0, 0.0)
    allowed_ref[...] = allowed
    lane = lax.broadcasted_iota(jnp.int32, (SEQ, 128), 1)
    for zh in range(ZH):
        tiles = [x_ref[:, x * 512 + zh * 128 : x * 512 + zh * 128 + 128] for x in range(X)]
        cores = []
        for core in range(2):
            pairs = [
                jnp.where(lane < 64, a, pltpu.roll(b, 64, 1))
                if core == 0
                else jnp.where(lane < 64, pltpu.roll(a, 64, 1), b)
                for a, b in (tiles[:2], tiles[2:])
            ]
            cores.append(turned(jnp.concatenate(pairs, axis=1), (X - where[1]) % X))
        for i in range(2):
            part = jnp.where(where[2] == i, cores[0], cores[1])
            columns = pl.ds((i * ZH + zh) * ROWS, ROWS)
            first_ref[:, columns] = part[:HALF].astype(BF16)
            second_ref[:, columns] = part[HALF:].astype(BF16)


def order_kernel(where, received_ref, down_ref, up_ref):
    plane = where[0] // 4
    rows = received_ref.shape[1]
    parts = [received_ref[(plane if t < 2 else 1 - plane) * 4 + t] for t in range(4)]
    values = jnp.concatenate([part.astype(F32) for part in parts], axis=0)
    lane = lax.broadcasted_iota(jnp.int32, (values.shape[0], 128), 1)
    for zh in range(ZH):
        mine, other = (
            turned(values[:, (i * ZH + zh) * ROWS : (i * ZH + zh + 1) * ROWS], where[1])
            for i in range(2)
        )
        zero, one = jnp.where(where[2] == 0, mine, other), jnp.where(where[2] == 0, other, mine)
        for pair in range(2):
            a, b = (part[:, pair * 128 : (pair + 1) * 128] for part in (zero, one))
            even = jnp.where(lane < 64, a, pltpu.roll(b, 64, 1)).astype(BF16)
            odd = jnp.where(lane < 64, pltpu.roll(a, 64, 1), b).astype(BF16)
            for x, tile in ((2 * pair, even), (2 * pair + 1, odd)):
                columns = pl.ds(x * 512 + zh * 128, 128)
                for t in range(4):
                    out_ref = down_ref if t < 2 else up_ref
                    out_ref[0, t % 2, :, columns] = tile[t * rows : (t + 1) * rows]


def exchange(chunks, where):
    planes, members = lax.axis_size("pipe"), lax.axis_size("tensor")
    rows = SEQ // members
    groups = [
        [plane * members + t for plane in (y, planes - 1 - y) for t in range(members)]
        for y in range(planes // 2)
    ]
    received = lax.all_to_all(chunks, ("pipe", "tensor"), 0, 0, axis_index_groups=groups)
    vmem = pl.BlockSpec(memory_space=pltpu.VMEM)
    shape = jax.ShapeDtypeStruct((1, members // 2, rows, D), BF16)
    return pl.pallas_call(
        order_kernel,
        out_shape=[shape, shape],
        in_specs=[pl.BlockSpec(memory_space=pltpu.SMEM), vmem],
        out_specs=[vmem, vmem],
        compiler_params=SMALL,
        name="order",
    )(where, received)


def on_device(down_in, up_in, w_qkv, w_out, norm_gain, down_docs, up_docs):
    where = jnp.stack([lax.axis_index(name) for name in ("pipe", "x", "core", "tensor")])
    sections = lax.axis_size("pipe")
    weights = gather_section(where, w_qkv, w_out, norm_gain)
    rope = rotary_tables()
    vmem = pl.BlockSpec(memory_space=pltpu.VMEM)
    part = jax.ShapeDtypeStruct((HALF, D), BF16)
    *values, allowed = pl.pallas_call(
        enter_kernel,
        out_shape=[part, part, jax.ShapeDtypeStruct((SEQ, SEQ), F32)],
        in_specs=[pl.BlockSpec(memory_space=pltpu.SMEM)] + [vmem] * 4,
        out_specs=[vmem] * 3,
        compiler_params=SMALL,
        name="enter",
    )(where, down_in, up_in, down_docs, up_docs)
    held = [jnp.zeros((HALF, D), BF16)] * 2
    for step in range(sections):
        last = step + 1 == sections

        def run(half, *more):
            return run_section(
                step, half, last, where, values[half], allowed, held[half], rope, weights, *more
            )

        def next_plane(part):
            return lax.ppermute(part, "pipe", [(step, step + 1)])

        one, *state = run(0)
        if last:
            return exchange(run(1, *state, one)[0], where)
        (two,) = run(1, *state)
        held = [one, two]
        values = [next_plane(one), next_plane(two)]


def solution(mesh):
    fine = Mesh(
        mesh.devices.reshape(X, ZH, 2, *mesh.devices.shape[1:]),
        ("x", "z_hi", "core", "pipe", "tensor"),
    )
    dp = ("x", "z_hi", "core")
    placed = (
        P(dp, None, None),
        P(dp, None, None),
        P(None, dp, "tensor"),
        P(None, "tensor", dp),
        P(None, dp),
        P(dp, None),
        P(dp, None),
    )
    return jax.shard_map(
        on_device,
        mesh=fine,
        in_specs=placed,
        out_specs=(P("pipe", dp, "tensor", None), P("pipe", dp, "tensor", None)),
        check_vma=False,
    )
```

```python
import functools

import jax
import jax.numpy as jnp
import numpy as np
from jax import lax
from jax.experimental import pallas as pl
from jax.experimental.pallas import tpu as pltpu
from jax.sharding import Mesh, PartitionSpec as P

HEAD_DIM = 64
SEQ = 32
D = 2048
EPSILON = 1e-05
THETA = 500000.0

GROUPS = 4
GROUP_HEADS = 4
QKV = 384
CTX = 256
X = 4
ZH = 4
ZL = 4
Z = ZH * ZL
HALF = SEQ // 2
ROWS = 256

F32, BF16 = jnp.float32, jnp.bfloat16

SMALL = pltpu.CompilerParams(vmem_limit_bytes=4 * 1024 * 1024)
MEDIUM = pltpu.CompilerParams(vmem_limit_bytes=20 * 1024 * 1024)


def device_place():
    return [lax.axis_index(name) for name in ("pipe", "x", "core", "tensor")]


def rotary_tables():
    half = HEAD_DIM // 2
    lane = jnp.arange(4 * half)[None, :]
    frequency = THETA ** (-((lane % half).astype(F32) * 2.0 / HEAD_DIM))
    angles = jnp.arange(SEQ, dtype=F32)[:, None] * frequency
    cos, sin = jnp.cos(angles), jnp.sin(angles)
    return [
        cos,
        sin,
        jnp.where(lane < 2 * half, cos, 1.0),
        jnp.where(lane < half, -sin, 0.0),
        jnp.where((lane >= half) & (lane < 2 * half), sin, 0.0),
    ]


def attention(projected, rope, allowed, earlier):
    rows = projected[0].shape[0]
    lane = lax.broadcasted_iota(jnp.int32, (rows, 128), 1)
    lane2 = lax.broadcasted_iota(jnp.int32, (rows, 256), 1)
    head_of = (lane2 % 128) // 32
    zero = jnp.zeros((), BF16)
    cos, sin, kcos, ksin_a, ksin_b = rope
    queries, keys, values = [], [], []
    for part in projected:
        first, second = part[:, :128], part[:, 128:256]
        query = jnp.concatenate(
            [first * cos - second * sin, second * cos + first * sin], axis=-1
        ).astype(BF16)
        queries.append(
            jnp.concatenate([jnp.where(head_of == h, query, zero) for h in range(GROUP_HEADS)], axis=0)
        )
    for part in projected:
        kv = part[:, 256:]
        kv = kv * kcos + pltpu.roll(kv, 96, 1) * ksin_a + pltpu.roll(kv, 32, 1) * ksin_b
        key_a = jnp.where(lane < 32, kv, 0.0)
        key_a = key_a + pltpu.roll(key_a, 32, 1)
        key_a = key_a + pltpu.roll(key_a, 64, 1)
        key_b = jnp.where((lane >= 32) & (lane < 64), kv, 0.0)
        key_b = key_b + pltpu.roll(key_b, 32, 1)
        key_b = key_b + pltpu.roll(key_b, 64, 1)
        keys.append(jnp.concatenate([key_a, key_b], axis=-1).astype(BF16))
        values.append(kv.astype(BF16))
    all_keys, all_values = keys, values
    if earlier is not None:
        all_keys = [jnp.concatenate(pair, axis=0) for pair in zip(earlier[0], keys)]
        all_values = [jnp.concatenate(pair, axis=0) for pair in zip(earlier[1], values)]
    scores = [
        lax.dot_general(q, k, (((1,), (1,)), ((), ())), preferred_element_type=F32)
        for q, k in zip(queries, all_keys)
    ]
    scores = [jnp.where(allowed, s * HEAD_DIM ** (-0.5), -1e30) for s in scores]
    scores = [jnp.exp(s - jnp.max(s, axis=-1, keepdims=True)) for s in scores]
    weights = [(s * (1.0 / jnp.sum(s, axis=-1, keepdims=True))).astype(BF16) for s in scores]
    contexts = []
    for weight, value in zip(weights, all_values):
        mixed = jnp.dot(weight, value, preferred_element_type=F32)
        heads = [mixed[h * rows : (h + 1) * rows] for h in range(GROUP_HEADS)]
        context = jnp.concatenate(
            [
                jnp.where(lane < 64, pltpu.roll(heads[0], 64, 1), heads[1]),
                jnp.where(lane < 64, pltpu.roll(heads[2], 64, 1), heads[3]),
            ],
            axis=-1,
        )
        contexts.append(context.astype(BF16))
    return contexts, keys, values


def section_kernel(step, half, last, x_ref, allowed_ref, held_ref, *refs):
    where = device_place()
    rope, weights, refs = refs[:5], (refs[5:7], refs[7:9]), refs[9:]
    first = half * HALF
    if half == 0:
        out_ref, keys_ref, values_ref = refs
    elif last:
        keys_ref, values_ref, before_ref, chunks_ref, out_ref = refs
    else:
        keys_ref, values_ref, out_ref = refs
    out_rows = pl.ds(first if last and half else 0, HALF)

    def rows_of(i, zh, t, columns):
        part, start = ((0, 0), (0, 2 * ZH), (1, 0), (0, ZH))[t]
        return jnp.concatenate(
            [weights[i][part][x, start + zh, :, columns] for x in range(X)], axis=0
        )

    @pl.when(where[0] != step)
    def _():
        out_ref[out_rows, :] = held_ref[...].astype(out_ref.dtype)

    @pl.when(where[0] == step)
    def _():
        places = [(i, zh) for i in range(2) for zh in range(ZH)]
        parts = [x_ref[:, pl.ds(j * ROWS, ROWS)] for j in range(2 * ZH)]
        squares = [jnp.sum(jnp.square(part.astype(F32)), axis=-1, keepdims=True) for part in parts]
        scale = lax.rsqrt(functools.reduce(jnp.add, squares) * (1.0 / D) + EPSILON)
        projected = []
        for t in range(GROUPS):
            terms = [
                jnp.dot(part, rows_of(i, zh, t, pl.ds(0, QKV)), preferred_element_type=F32)
                for part, (i, zh) in zip(parts, places)
            ]
            projected.append(functools.reduce(jnp.add, terms) * scale)
        allowed = allowed_ref[pl.ds(first, HALF), pl.ds(0, first + HALF)] > 0.5
        allowed = jnp.concatenate([allowed] * GROUP_HEADS, axis=0)
        earlier = None
        if half:
            earlier = [[ref[t] for t in range(GROUPS)] for ref in (keys_ref, values_ref)]
        contexts, keys, values = attention(
            projected, [part[pl.ds(first, HALF), :] for part in rope], allowed, earlier
        )
        if not half:
            for t in range(GROUPS):
                keys_ref[t] = keys[t]
                values_ref[t] = values[t]
        for j, (i, zh) in enumerate(places):
            terms = [
                jnp.dot(
                    contexts[t], rows_of(i, zh, t, pl.ds(QKV, CTX)), preferred_element_type=F32
                )
                for t in range(GROUPS)
            ]
            total = x_ref[:, pl.ds(j * ROWS, ROWS)].astype(F32) + functools.reduce(jnp.add, terms)
            out_ref[out_rows, pl.ds(j * ROWS, ROWS)] = total.astype(out_ref.dtype)

    if last and half:
        out_ref[pl.ds(0, HALF), :] = before_ref[...].astype(F32)
        for k in range(chunks_ref.shape[0]):
            place = k % GROUPS * (SEQ // GROUPS)
            chunks_ref[k] = out_ref[pl.ds(place, SEQ // GROUPS), :].astype(BF16)


def run_section(step, half, last, values, allowed, held, rope, weights, *more):
    vmem = pl.BlockSpec(memory_space=pltpu.VMEM)
    part = jax.ShapeDtypeStruct((HALF, D), BF16)
    split = bool(last and half)
    if half == 0:
        shapes = [
            part,
            jax.ShapeDtypeStruct((GROUPS, HALF, 256), BF16),
            jax.ShapeDtypeStruct((GROUPS, HALF, 128), BF16),
        ]
    else:
        shapes = [jax.ShapeDtypeStruct((8, SEQ // 4, D), BF16) if split else part]
    return pl.pallas_call(
        functools.partial(section_kernel, step, half, last),
        out_shape=shapes,
        in_specs=[vmem] * (12 + len(more)),
        out_specs=[vmem] * len(shapes),
        scratch_shapes=[pltpu.VMEM((SEQ, D), F32)] if split else [],
        input_output_aliases={} if split else {2: 0},
        compiler_params=MEDIUM,
        name="section",
    )(values, allowed, held, *rope, *weights, *more)


def shard_kernel(qkv_any, out_any, gain_any, shard_ref, qkv_ref, out_ref, gain_ref, done):
    where = device_place()
    copies = [
        pltpu.make_async_copy(qkv_any.at[where[0]], qkv_ref, done.at[0]),
        pltpu.make_async_copy(out_any.at[where[0]], out_ref, done.at[1]),
        pltpu.make_async_copy(gain_any, gain_ref, done.at[2]),
    ]
    for copy in copies:
        copy.start()
    for copy in copies:
        copy.wait()
    rows = qkv_ref.shape[0]
    section = lax.broadcasted_iota(jnp.int32, gain_ref.shape, 0)
    gain = jnp.where(section == where[0], gain_ref[...].astype(F32), 0.0)
    gain = jnp.sum(gain, axis=0, keepdims=True)
    row = lax.broadcasted_iota(jnp.int32, (rows, rows), 0)
    column = lax.broadcasted_iota(jnp.int32, (rows, rows), 1)
    gain = jnp.sum(jnp.where(row == column, gain, 0.0), axis=1, keepdims=True)
    qkv = qkv_ref[...].astype(F32) * gain
    one, two = qkv[:, :128], qkv[:, 128:256]
    lane = lax.broadcasted_iota(jnp.int32, (rows, 128), 1)

    def lanes(parts):
        result = parts[3]
        for i in (2, 1, 0):
            result = jnp.where(lane < 32 * (i + 1), parts[i], result)
        return result

    first = lanes([one, pltpu.roll(one, 96, 1), pltpu.roll(two, 64, 1), pltpu.roll(two, 32, 1)])
    second = lanes([pltpu.roll(one, 96, 1), pltpu.roll(one, 64, 1), pltpu.roll(two, 32, 1), two])
    for zh in range(shard_ref.shape[0]):
        shard_ref[zh, :, pl.ds(0, 128)] = first.astype(BF16)
        shard_ref[zh, :, pl.ds(128, 128)] = second.astype(BF16)
        shard_ref[zh, :, pl.ds(256, 128)] = qkv[:, 256:].astype(BF16)
        shard_ref[zh, :, pl.ds(QKV, CTX)] = out_ref[...]


def join_kernel(here_ref, after_ref, before_ref, half_ref, rest_ref, out_ref):
    half = half_ref.shape[0]
    for i in range(out_ref.shape[1]):
        middle = half_ref.at[i] if i < half else rest_ref.at[i - half]
        parts = [here_ref.at[i], after_ref.at[i], middle, before_ref.at[i]]
        for x, part in enumerate(parts):
            out_ref[x, i, :, pl.ds(0, QKV)] = part[:, pl.ds(0, QKV)]
        columns = jnp.concatenate([part[:, pl.ds(QKV, CTX)] for part in parts], axis=0)
        turned_columns = columns.astype(F32).T.astype(BF16)
        for x in range(X):
            out_ref[x, i, :, pl.ds(QKV, CTX)] = turned_columns[x * 64 : (x + 1) * 64]


def gather_section(w_qkv, w_out, norm_gain):
    rows = w_qkv.shape[1]
    vmem = pl.BlockSpec(memory_space=pltpu.VMEM)
    shards = pl.pallas_call(
        shard_kernel,
        out_shape=jax.ShapeDtypeStruct((ZH, rows, QKV + CTX), BF16),
        in_specs=[pl.BlockSpec(memory_space=pl.ANY)] * 3,
        out_specs=vmem,
        scratch_shapes=[
            pltpu.VMEM((rows, QKV), BF16),
            pltpu.VMEM((rows, CTX), BF16),
            pltpu.VMEM(norm_gain.shape, BF16),
            pltpu.SemaphoreType.DMA((3,)),
        ],
        name="shard",
    )(w_qkv, w_out.transpose(0, 2, 1), norm_gain)

    one, other = [(x, (x + 1) % X) for x in range(X)], [(x, (x - 1) % X) for x in range(X)]

    def first_along_x(parts):
        return lax.ppermute(parts, "x", one), lax.ppermute(parts, "x", other)

    def rest_along_x(before, after):
        half = before.shape[0] // 2
        return lax.ppermute(before[:half], "x", one), lax.ppermute(after[half:], "x", other)

    def join(here, before, after, half, rest):
        return pl.pallas_call(
            join_kernel,
            out_shape=jax.ShapeDtypeStruct((X, *here.shape), BF16),
            in_specs=[vmem] * 5,
            out_specs=vmem,
            compiler_params=MEDIUM,
            name="join",
        )(here, after, before, half, rest)

    def along_z(parts, by):
        return lax.ppermute(parts, ("z_hi", "tensor"), [(z, (z + by) % Z) for z in range(Z)])

    here = lax.all_to_all(shards, "z_hi", 0, 0)
    half = ZH // 2
    ahead, behind = along_z(here, 1), along_z(here, -1)
    near = jnp.concatenate([here, ahead, behind])
    near_x = first_along_x(near)
    across = jnp.concatenate([along_z(ahead[:half], 1), along_z(behind[half:], -1)])
    across_x = first_along_x(across)
    rest = rest_along_x(*near_x) + rest_along_x(*across_x)
    rest = lax.optimization_barrier(rest)
    own = [join(near, *near_x, *rest[:2]), join(across, *across_x, *rest[2:])]
    return own + [lax.ppermute(part, "core", [(0, 1), (1, 0)]) for part in own]


def turned(values, by):
    result = values
    for count in range(1, X):
        result = jnp.where(by == count, pltpu.roll(values, 64 * count, 1), result)
    return result


def enter_kernel(
    down_ref, up_ref, down_docs_ref, up_docs_ref, first_ref, second_ref, allowed_ref
):
    where = device_place()
    member = where[3]
    x_ref = jnp.where(member < 2, down_ref[member % 2], up_ref[member % 2]).astype(F32)
    docs = [docs_ref[...] for docs_ref in (down_docs_ref, up_docs_ref)]
    docs = jnp.where(member < 2, docs[0], docs[1])
    docs = jnp.where(member % 2 == 0, docs[:1], docs[1:])
    row = lax.broadcasted_iota(jnp.int32, (SEQ, SEQ), 0)
    column = lax.broadcasted_iota(jnp.int32, (SEQ, SEQ), 1)
    own_docs = jnp.sum(jnp.where(row == column, docs, 0), axis=1, keepdims=True)
    allowed = jnp.where((row >= column) & (own_docs == docs), 1.0, 0.0)
    allowed_ref[...] = allowed
    lane = lax.broadcasted_iota(jnp.int32, (SEQ, 128), 1)
    for zh in range(ZH):
        tiles = [x_ref[:, x * 512 + zh * 128 : x * 512 + zh * 128 + 128] for x in range(X)]
        cores = []
        for core in range(2):
            pairs = [
                jnp.where(lane < 64, a, pltpu.roll(b, 64, 1))
                if core == 0
                else jnp.where(lane < 64, pltpu.roll(a, 64, 1), b)
                for a, b in (tiles[:2], tiles[2:])
            ]
            cores.append(turned(jnp.concatenate(pairs, axis=1), (X - where[1]) % X))
        for i in range(2):
            part = jnp.where(where[2] == i, cores[0], cores[1])
            columns = pl.ds((i * ZH + zh) * ROWS, ROWS)
            first_ref[:, columns] = part[:HALF].astype(BF16)
            second_ref[:, columns] = part[HALF:].astype(BF16)


def order_kernel(received_ref, down_ref, up_ref):
    where = device_place()
    plane = where[0] // 4
    rows = received_ref.shape[1]
    parts = [received_ref[(plane if t < 2 else 1 - plane) * 4 + t] for t in range(4)]
    values = jnp.concatenate([part.astype(F32) for part in parts], axis=0)
    lane = lax.broadcasted_iota(jnp.int32, (values.shape[0], 128), 1)
    for zh in range(ZH):
        mine, other = (
            turned(values[:, (i * ZH + zh) * ROWS : (i * ZH + zh + 1) * ROWS], where[1])
            for i in range(2)
        )
        zero, one = jnp.where(where[2] == 0, mine, other), jnp.where(where[2] == 0, other, mine)
        for pair in range(2):
            a, b = (part[:, pair * 128 : (pair + 1) * 128] for part in (zero, one))
            even = jnp.where(lane < 64, a, pltpu.roll(b, 64, 1)).astype(BF16)
            odd = jnp.where(lane < 64, pltpu.roll(a, 64, 1), b).astype(BF16)
            for x, tile in ((2 * pair, even), (2 * pair + 1, odd)):
                columns = pl.ds(x * 512 + zh * 128, 128)
                for t in range(4):
                    out_ref = down_ref if t < 2 else up_ref
                    out_ref[0, t % 2, :, columns] = tile[t * rows : (t + 1) * rows]


def exchange(chunks):
    planes, members = lax.axis_size("pipe"), lax.axis_size("tensor")
    rows = SEQ // members
    groups = [
        [plane * members + t for plane in (y, planes - 1 - y) for t in range(members)]
        for y in range(planes // 2)
    ]
    received = lax.all_to_all(chunks, ("pipe", "tensor"), 0, 0, axis_index_groups=groups)
    vmem = pl.BlockSpec(memory_space=pltpu.VMEM)
    shape = jax.ShapeDtypeStruct((1, members // 2, rows, D), BF16)
    return pl.pallas_call(
        order_kernel,
        out_shape=[shape, shape],
        in_specs=[vmem],
        out_specs=[vmem, vmem],
        compiler_params=SMALL,
        name="order",
    )(received)


def on_device(down_in, up_in, w_qkv, w_out, norm_gain, down_docs, up_docs):
    sections = lax.axis_size("pipe")
    weights = gather_section(w_qkv, w_out, norm_gain)
    rope = rotary_tables()
    vmem = pl.BlockSpec(memory_space=pltpu.VMEM)
    part = jax.ShapeDtypeStruct((HALF, D), BF16)
    *values, allowed = pl.pallas_call(
        enter_kernel,
        out_shape=[part, part, jax.ShapeDtypeStruct((SEQ, SEQ), F32)],
        in_specs=[vmem] * 4,
        out_specs=[vmem] * 3,
        compiler_params=SMALL,
        name="enter",
    )(down_in, up_in, down_docs, up_docs)
    held = [jnp.zeros((HALF, D), BF16)] * 2
    for step in range(sections):
        last = step + 1 == sections

        def run(half, *more):
            return run_section(
                step, half, last, values[half], allowed, held[half], rope, weights, *more
            )

        def next_plane(part):
            return lax.ppermute(part, "pipe", [(step, step + 1)])

        one, *state = run(0)
        if last:
            return exchange(run(1, *state, one)[0])
        (two,) = run(1, *state)
        held = [one, two]
        values = [next_plane(one), next_plane(two)]


def solution(mesh):
    fine = Mesh(
        mesh.devices.reshape(X, ZH, 2, *mesh.devices.shape[1:]),
        ("x", "z_hi", "core", "pipe", "tensor"),
    )
    dp = ("x", "z_hi", "core")
    placed = (
        P(dp, None, None),
        P(dp, None, None),
        P(None, dp, "tensor"),
        P(None, "tensor", dp),
        P(None, dp),
        P(dp, None),
        P(dp, None),
    )
    return jax.shard_map(
        on_device,
        mesh=fine,
        in_specs=placed,
        out_specs=(P("pipe", dp, "tensor", None), P("pipe", dp, "tensor", None)),
        check_vma=False,
    )
```

```python
import functools

import jax
import jax.numpy as jnp
import numpy as np
from jax import lax
from jax.experimental import pallas as pl
from jax.experimental.pallas import tpu as pltpu
from jax.sharding import Mesh, PartitionSpec as P

HEAD_DIM = 64
SEQ = 32
D = 2048
EPSILON = 1e-05
THETA = 500000.0

GROUPS = 4
GROUP_HEADS = 4
QKV = 384
CTX = 256
X = 4
ZH = 4
ZL = 4
Z = ZH * ZL
HALF = SEQ // 2
ROWS = 256

F32, BF16 = jnp.float32, jnp.bfloat16

SMALL = pltpu.CompilerParams(vmem_limit_bytes=4 * 1024 * 1024)
MEDIUM = pltpu.CompilerParams(vmem_limit_bytes=20 * 1024 * 1024)


def device_place():
    return [lax.axis_index(name) for name in ("pipe", "x", "core", "tensor")]


def rotary_tables():
    half = HEAD_DIM // 2
    lane = jnp.arange(4 * half)[None, :]
    frequency = THETA ** (-((lane % half).astype(F32) * 2.0 / HEAD_DIM))
    angles = jnp.arange(SEQ, dtype=F32)[:, None] * frequency
    cos, sin = jnp.cos(angles), jnp.sin(angles)
    return [
        cos,
        sin,
        jnp.where(lane < 2 * half, cos, 1.0),
        jnp.where(lane < half, -sin, 0.0),
        jnp.where((lane >= half) & (lane < 2 * half), sin, 0.0),
    ]


def attention(projected, rope, allowed, earlier):
    rows = projected[0].shape[0]
    lane = lax.broadcasted_iota(jnp.int32, (rows, 128), 1)
    lane2 = lax.broadcasted_iota(jnp.int32, (rows, 256), 1)
    head_of = (lane2 % 128) // 32
    zero = jnp.zeros((), BF16)
    cos, sin, kcos, ksin_a, ksin_b = rope
    queries, keys, values = [], [], []
    for part in projected:
        first, second = part[:, :128], part[:, 128:256]
        query = jnp.concatenate(
            [first * cos - second * sin, second * cos + first * sin], axis=-1
        ).astype(BF16)
        queries.append(
            jnp.concatenate([jnp.where(head_of == h, query, zero) for h in range(GROUP_HEADS)], axis=0)
        )
    for part in projected:
        kv = part[:, 256:]
        kv = kv * kcos + pltpu.roll(kv, 96, 1) * ksin_a + pltpu.roll(kv, 32, 1) * ksin_b
        key_a = jnp.where(lane < 32, kv, 0.0)
        key_a = key_a + pltpu.roll(key_a, 32, 1)
        key_a = key_a + pltpu.roll(key_a, 64, 1)
        key_b = jnp.where((lane >= 32) & (lane < 64), kv, 0.0)
        key_b = key_b + pltpu.roll(key_b, 32, 1)
        key_b = key_b + pltpu.roll(key_b, 64, 1)
        keys.append(jnp.concatenate([key_a, key_b], axis=-1).astype(BF16))
        values.append(kv.astype(BF16))
    all_keys, all_values = keys, values
    if earlier is not None:
        all_keys = [jnp.concatenate(pair, axis=0) for pair in zip(earlier[0], keys)]
        all_values = [jnp.concatenate(pair, axis=0) for pair in zip(earlier[1], values)]
    scores = [
        lax.dot_general(q, k, (((1,), (1,)), ((), ())), preferred_element_type=F32)
        for q, k in zip(queries, all_keys)
    ]
    scores = [jnp.where(allowed, s * HEAD_DIM ** (-0.5), -1e30) for s in scores]
    scores = [jnp.exp(s - jnp.max(s, axis=-1, keepdims=True)) for s in scores]
    weights = [(s * (1.0 / jnp.sum(s, axis=-1, keepdims=True))).astype(BF16) for s in scores]
    contexts = []
    for weight, value in zip(weights, all_values):
        mixed = jnp.dot(weight, value, preferred_element_type=F32)
        heads = [mixed[h * rows : (h + 1) * rows] for h in range(GROUP_HEADS)]
        context = jnp.concatenate(
            [
                jnp.where(lane < 64, pltpu.roll(heads[0], 64, 1), heads[1]),
                jnp.where(lane < 64, pltpu.roll(heads[2], 64, 1), heads[3]),
            ],
            axis=-1,
        )
        contexts.append(context.astype(BF16))
    return contexts, keys, values


def section_kernel(step, half, last, x_ref, allowed_ref, held_ref, *refs):
    where = device_place()
    rope, weights, refs = refs[:5], (refs[5:7], refs[7:9]), refs[9:]
    first = half * HALF
    if half == 0:
        out_ref, keys_ref, values_ref = refs
    elif last:
        keys_ref, values_ref, before_ref, chunks_ref, out_ref = refs
    else:
        keys_ref, values_ref, out_ref = refs
    out_rows = pl.ds(first if last and half else 0, HALF)

    def rows_of(i, zh, t, columns):
        part, start = ((0, 0), (0, 2 * ZH), (1, 0), (0, ZH))[t]
        return jnp.concatenate(
            [weights[i][part][x, start + zh, :, columns] for x in range(X)], axis=0
        )

    @pl.when(where[0] != step)
    def _():
        out_ref[out_rows, :] = held_ref[...].astype(out_ref.dtype)

    @pl.when(where[0] == step)
    def _():
        places = [(i, zh) for i in range(2) for zh in range(ZH)]
        parts = [x_ref[:, pl.ds(j * ROWS, ROWS)] for j in range(2 * ZH)]
        squares = [jnp.sum(jnp.square(part.astype(F32)), axis=-1, keepdims=True) for part in parts]
        scale = lax.rsqrt(functools.reduce(jnp.add, squares) * (1.0 / D) + EPSILON)
        projected = []
        for t in range(GROUPS):
            terms = [
                jnp.dot(part, rows_of(i, zh, t, pl.ds(0, QKV)), preferred_element_type=F32)
                for part, (i, zh) in zip(parts, places)
            ]
            projected.append(functools.reduce(jnp.add, terms) * scale)
        allowed = allowed_ref[pl.ds(first, HALF), pl.ds(0, first + HALF)] > 0.5
        allowed = jnp.concatenate([allowed] * GROUP_HEADS, axis=0)
        earlier = None
        if half:
            earlier = [[ref[t] for t in range(GROUPS)] for ref in (keys_ref, values_ref)]
        contexts, keys, values = attention(
            projected, [part[pl.ds(first, HALF), :] for part in rope], allowed, earlier
        )
        if not half:
            for t in range(GROUPS):
                keys_ref[t] = keys[t]
                values_ref[t] = values[t]
        for j, (i, zh) in enumerate(places):
            terms = [
                jnp.dot(
                    contexts[t], rows_of(i, zh, t, pl.ds(QKV, CTX)), preferred_element_type=F32
                )
                for t in range(GROUPS)
            ]
            total = x_ref[:, pl.ds(j * ROWS, ROWS)].astype(F32) + functools.reduce(jnp.add, terms)
            out_ref[out_rows, pl.ds(j * ROWS, ROWS)] = total.astype(out_ref.dtype)

    if last and half:
        out_ref[pl.ds(0, HALF), :] = before_ref[...].astype(F32)
        for k in range(chunks_ref.shape[0]):
            place = k % GROUPS * (SEQ // GROUPS)
            chunks_ref[k] = out_ref[pl.ds(place, SEQ // GROUPS), :].astype(BF16)


def run_section(step, half, last, values, allowed, held, rope, weights, *more):
    vmem = pl.BlockSpec(memory_space=pltpu.VMEM)
    part = jax.ShapeDtypeStruct((HALF, D), BF16)
    split = bool(last and half)
    if half == 0:
        shapes = [
            part,
            jax.ShapeDtypeStruct((GROUPS, HALF, 256), BF16),
            jax.ShapeDtypeStruct((GROUPS, HALF, 128), BF16),
        ]
    else:
        shapes = [jax.ShapeDtypeStruct((8, SEQ // 4, D), BF16) if split else part]
    return pl.pallas_call(
        functools.partial(section_kernel, step, half, last),
        out_shape=shapes,
        in_specs=[vmem] * (12 + len(more)),
        out_specs=[vmem] * len(shapes),
        scratch_shapes=[pltpu.VMEM((SEQ, D), F32)] if split else [],
        input_output_aliases={} if split else {2: 0},
        compiler_params=MEDIUM,
        name="section",
    )(values, allowed, held, *rope, *weights, *more)


def shard_kernel(qkv_any, out_any, gain_any, shard_ref, qkv_ref, out_ref, gain_ref, done):
    where = device_place()
    copies = [
        pltpu.make_async_copy(qkv_any.at[where[0]], qkv_ref, done.at[0]),
        pltpu.make_async_copy(out_any.at[where[0]], out_ref, done.at[1]),
        pltpu.make_async_copy(gain_any, gain_ref, done.at[2]),
    ]
    for copy in copies:
        copy.start()
    for copy in copies:
        copy.wait()
    rows = qkv_ref.shape[0]
    section = lax.broadcasted_iota(jnp.int32, gain_ref.shape, 0)
    gain = jnp.where(section == where[0], gain_ref[...].astype(F32), 0.0)
    gain = jnp.sum(gain, axis=0, keepdims=True)
    row = lax.broadcasted_iota(jnp.int32, (rows, rows), 0)
    column = lax.broadcasted_iota(jnp.int32, (rows, rows), 1)
    gain = jnp.sum(jnp.where(row == column, gain, 0.0), axis=1, keepdims=True)
    qkv = qkv_ref[...].astype(F32) * gain
    one, two = qkv[:, :128], qkv[:, 128:256]
    lane = lax.broadcasted_iota(jnp.int32, (rows, 128), 1)

    def lanes(parts):
        result = parts[3]
        for i in (2, 1, 0):
            result = jnp.where(lane < 32 * (i + 1), parts[i], result)
        return result

    first = lanes([one, pltpu.roll(one, 96, 1), pltpu.roll(two, 64, 1), pltpu.roll(two, 32, 1)])
    second = lanes([pltpu.roll(one, 96, 1), pltpu.roll(one, 64, 1), pltpu.roll(two, 32, 1), two])
    for zh in range(shard_ref.shape[0]):
        shard_ref[zh, :, pl.ds(0, 128)] = first.astype(BF16)
        shard_ref[zh, :, pl.ds(128, 128)] = second.astype(BF16)
        shard_ref[zh, :, pl.ds(256, 128)] = qkv[:, 256:].astype(BF16)
        shard_ref[zh, :, pl.ds(QKV, CTX)] = out_ref[...]


def join_parts(parts_of, out_ref):
    for i in range(out_ref.shape[1]):
        parts = parts_of(i)
        for x, part in enumerate(parts):
            out_ref[x, i, :, pl.ds(0, QKV)] = part[:, pl.ds(0, QKV)]
        columns = jnp.concatenate([part[:, pl.ds(QKV, CTX)] for part in parts], axis=0)
        turned_columns = columns.astype(F32).T.astype(BF16)
        for x in range(X):
            out_ref[x, i, :, pl.ds(QKV, CTX)] = turned_columns[x * 64 : (x + 1) * 64]


def join_kernel(here_ref, after_ref, before_ref, half_ref, rest_ref, out_ref):
    half = half_ref.shape[0]

    def parts_of(i):
        middle = half_ref.at[i] if i < half else rest_ref.at[i - half]
        return [here_ref.at[i], after_ref.at[i], middle, before_ref.at[i]]

    join_parts(parts_of, out_ref)


def join_across_kernel(low_ref, high_ref, low_middle_ref, high_middle_ref, out_ref):
    half = low_middle_ref.shape[0]

    def parts_of(i):
        part, middle = (low_ref, low_middle_ref) if i < half else (high_ref, high_middle_ref)
        i = i % half
        return [part.at[i], part.at[half + i], middle.at[i], part.at[2 * half + i]]

    join_parts(parts_of, out_ref)


def gather_section(w_qkv, w_out, norm_gain):
    rows = w_qkv.shape[1]
    vmem = pl.BlockSpec(memory_space=pltpu.VMEM)
    shards = pl.pallas_call(
        shard_kernel,
        out_shape=jax.ShapeDtypeStruct((ZH, rows, QKV + CTX), BF16),
        in_specs=[pl.BlockSpec(memory_space=pl.ANY)] * 3,
        out_specs=vmem,
        scratch_shapes=[
            pltpu.VMEM((rows, QKV), BF16),
            pltpu.VMEM((rows, CTX), BF16),
            pltpu.VMEM(norm_gain.shape, BF16),
            pltpu.SemaphoreType.DMA((3,)),
        ],
        name="shard",
    )(w_qkv, w_out.transpose(0, 2, 1), norm_gain)

    one, other = [(x, (x + 1) % X) for x in range(X)], [(x, (x - 1) % X) for x in range(X)]

    def first_along_x(parts):
        return lax.ppermute(parts, "x", one), lax.ppermute(parts, "x", other)

    def rest_along_x(before, after):
        half = before.shape[0] // 2
        return lax.ppermute(before[:half], "x", one), lax.ppermute(after[half:], "x", other)

    def join(here, before, after, half, rest):
        return pl.pallas_call(
            join_kernel,
            out_shape=jax.ShapeDtypeStruct((X, *here.shape), BF16),
            in_specs=[vmem] * 5,
            out_specs=vmem,
            compiler_params=MEDIUM,
            name="join",
        )(here, after, before, half, rest)

    def along_z(parts, by):
        return lax.ppermute(parts, ("z_hi", "tensor"), [(z, (z + by) % Z) for z in range(Z)])

    here = lax.all_to_all(shards, "z_hi", 0, 0)
    half = ZH // 2
    ahead, behind = along_z(here, 1), along_z(here, -1)
    near = jnp.concatenate([here, ahead, behind])
    before, after = first_along_x(near)
    near_rest = rest_along_x(before, after)

    def pieces(first):
        return jnp.concatenate([part[first : first + half] for part in (near, after, before)])

    across = [
        along_z(pieces(ZH), 1),
        along_z(pieces(2 * ZH + half), -1),
        along_z(near_rest[0][ZH : ZH + half], 1),
        along_z(near_rest[1][ZH : ZH + half], -1),
    ]
    near_0, near_1, *across = lax.optimization_barrier((*near_rest, *across))
    across = pl.pallas_call(
        join_across_kernel,
        out_shape=jax.ShapeDtypeStruct((X, *here.shape), BF16),
        in_specs=[vmem] * 4,
        out_specs=vmem,
        compiler_params=MEDIUM,
        name="join_across",
    )(*across)
    own = [join(near, before, after, near_0, near_1), across]
    return own + [lax.ppermute(part, "core", [(0, 1), (1, 0)]) for part in own]


def turned(values, by):
    result = values
    for count in range(1, X):
        result = jnp.where(by == count, pltpu.roll(values, 64 * count, 1), result)
    return result


def enter_kernel(
    down_ref, up_ref, down_docs_ref, up_docs_ref, first_ref, second_ref, allowed_ref
):
    where = device_place()
    member = where[3]
    x_ref = jnp.where(member < 2, down_ref[member % 2], up_ref[member % 2]).astype(F32)
    docs = [docs_ref[...] for docs_ref in (down_docs_ref, up_docs_ref)]
    docs = jnp.where(member < 2, docs[0], docs[1])
    docs = jnp.where(member % 2 == 0, docs[:1], docs[1:])
    row = lax.broadcasted_iota(jnp.int32, (SEQ, SEQ), 0)
    column = lax.broadcasted_iota(jnp.int32, (SEQ, SEQ), 1)
    own_docs = jnp.sum(jnp.where(row == column, docs, 0), axis=1, keepdims=True)
    allowed = jnp.where((row >= column) & (own_docs == docs), 1.0, 0.0)
    allowed_ref[...] = allowed
    lane = lax.broadcasted_iota(jnp.int32, (SEQ, 128), 1)
    for zh in range(ZH):
        tiles = [x_ref[:, x * 512 + zh * 128 : x * 512 + zh * 128 + 128] for x in range(X)]
        cores = []
        for core in range(2):
            pairs = [
                jnp.where(lane < 64, a, pltpu.roll(b, 64, 1))
                if core == 0
                else jnp.where(lane < 64, pltpu.roll(a, 64, 1), b)
                for a, b in (tiles[:2], tiles[2:])
            ]
            cores.append(turned(jnp.concatenate(pairs, axis=1), (X - where[1]) % X))
        for i in range(2):
            part = jnp.where(where[2] == i, cores[0], cores[1])
            columns = pl.ds((i * ZH + zh) * ROWS, ROWS)
            first_ref[:, columns] = part[:HALF].astype(BF16)
            second_ref[:, columns] = part[HALF:].astype(BF16)


def order_kernel(received_ref, down_ref, up_ref):
    where = device_place()
    plane = where[0] // 4
    rows = received_ref.shape[1]
    parts = [received_ref[(plane if t < 2 else 1 - plane) * 4 + t] for t in range(4)]
    values = jnp.concatenate([part.astype(F32) for part in parts], axis=0)
    lane = lax.broadcasted_iota(jnp.int32, (values.shape[0], 128), 1)
    for zh in range(ZH):
        mine, other = (
            turned(values[:, (i * ZH + zh) * ROWS : (i * ZH + zh + 1) * ROWS], where[1])
            for i in range(2)
        )
        zero, one = jnp.where(where[2] == 0, mine, other), jnp.where(where[2] == 0, other, mine)
        for pair in range(2):
            a, b = (part[:, pair * 128 : (pair + 1) * 128] for part in (zero, one))
            even = jnp.where(lane < 64, a, pltpu.roll(b, 64, 1)).astype(BF16)
            odd = jnp.where(lane < 64, pltpu.roll(a, 64, 1), b).astype(BF16)
            for x, tile in ((2 * pair, even), (2 * pair + 1, odd)):
                columns = pl.ds(x * 512 + zh * 128, 128)
                for t in range(4):
                    out_ref = down_ref if t < 2 else up_ref
                    out_ref[0, t % 2, :, columns] = tile[t * rows : (t + 1) * rows]


def exchange(chunks):
    planes, members = lax.axis_size("pipe"), lax.axis_size("tensor")
    rows = SEQ // members
    groups = [
        [plane * members + t for plane in (y, planes - 1 - y) for t in range(members)]
        for y in range(planes // 2)
    ]
    received = lax.all_to_all(chunks, ("pipe", "tensor"), 0, 0, axis_index_groups=groups)
    vmem = pl.BlockSpec(memory_space=pltpu.VMEM)
    shape = jax.ShapeDtypeStruct((1, members // 2, rows, D), BF16)
    return pl.pallas_call(
        order_kernel,
        out_shape=[shape, shape],
        in_specs=[vmem],
        out_specs=[vmem, vmem],
        compiler_params=SMALL,
        name="order",
    )(received)


def on_device(down_in, up_in, w_qkv, w_out, norm_gain, down_docs, up_docs):
    sections = lax.axis_size("pipe")
    weights = gather_section(w_qkv, w_out, norm_gain)
    rope = rotary_tables()
    vmem = pl.BlockSpec(memory_space=pltpu.VMEM)
    part = jax.ShapeDtypeStruct((HALF, D), BF16)
    *values, allowed = pl.pallas_call(
        enter_kernel,
        out_shape=[part, part, jax.ShapeDtypeStruct((SEQ, SEQ), F32)],
        in_specs=[vmem] * 4,
        out_specs=[vmem] * 3,
        compiler_params=SMALL,
        name="enter",
    )(down_in, up_in, down_docs, up_docs)
    held = [jnp.zeros((HALF, D), BF16)] * 2
    for step in range(sections):
        last = step + 1 == sections

        def run(half, *more):
            return run_section(
                step, half, last, values[half], allowed, held[half], rope, weights, *more
            )

        def next_plane(part):
            return lax.ppermute(part, "pipe", [(step, step + 1)])

        one, *state = run(0)
        if last:
            return exchange(run(1, *state, one)[0])
        (two,) = run(1, *state)
        held = [one, two]
        values = [next_plane(one), next_plane(two)]


def solution(mesh):
    fine = Mesh(
        mesh.devices.reshape(X, ZH, 2, *mesh.devices.shape[1:]),
        ("x", "z_hi", "core", "pipe", "tensor"),
    )
    dp = ("x", "z_hi", "core")
    placed = (
        P(dp, None, None),
        P(dp, None, None),
        P(None, dp, "tensor"),
        P(None, "tensor", dp),
        P(None, dp),
        P(dp, None),
        P(dp, None),
    )
    return jax.shard_map(
        on_device,
        mesh=fine,
        in_specs=placed,
        out_specs=(P("pipe", dp, "tensor", None), P("pipe", dp, "tensor", None)),
        check_vma=False,
    )
```
